32 devices in a mesh: section: 2 (over x), dp: 16 (over z, y, core).
Axes of the slice: x: 2, y: 2, z: 4, core: 2. Of those that a mesh axis runs over, the one named last changes fastest.
Arguments:
- inputs: bfloat16 [2, 32, 256, 768], P('section', 'dp'), may hold values from -6 to 6
- cotangent: bfloat16 [2, 32, 256, 768], P('section', 'dp'), may hold values from -6 to 6
- enc_segments: int32 [32, 256], P('dp'), may hold values from 0 to 3, as said below
- dec_segments: int32 [32, 256], P('dp'), may hold values from 0 to 3, as said below
- rel_bias: float32 [32, 12], replicated, may hold values from -4 to 4
- attn_norm: bfloat16 [2, 768], P('section'), may hold values from 0.099609375 to 1.8984375
- ffn_norm: bfloat16 [2, 768], P('section'), may hold values from 0.099609375 to 1.8984375
- w_qkv: bfloat16 [2, 768, 2304], P('section'), may hold values from -0.078125 to 0.078125
- w_attn_out: bfloat16 [2, 768, 768], P('section'), may hold values from -3 to 3
- w_gate_up: bfloat16 [2, 768, 4096], P('section'), may hold values from -0.21875 to 0.21875
- w_down: bfloat16 [2, 2048, 768], P('section'), may hold values from -0.1875 to 0.1875
- cross_norm: bfloat16 [768], replicated, may hold values from 0.099609375 to 1.8984375
- cross_query: bfloat16 [768, 768], replicated, may hold values from -0.078125 to 0.078125
- cross_kv: bfloat16 [768, 1536], replicated, may hold values from -0.078125 to 0.078125
- cross_out: bfloat16 [768, 768], replicated, may hold values from -3 to 3
- final_norm: bfloat16 [768], replicated, may hold values from 0.099609375 to 1.8984375
Outputs:
- layer_out: bfloat16 [2, 32, 256, 768], P('section', 'dp')
- grad_inputs: float32 [2, 32, 256, 768], P('section', 'dp')
- grad_qkv: float32 [2, 768, 2304], P('section', 'dp')
- grad_attn_out: float32 [2, 768, 768], P('section', 'dp')
- grad_gate_up: float32 [2, 768, 4096], P('section', 'dp')
- grad_down: float32 [2, 2048, 768], P('section', 'dp')
- grad_attn_norm: float32 [2, 768], P('section', 'dp')
- grad_ffn_norm: float32 [2, 768], P('section', 'dp')
- grad_cross_query: float32 [768, 768], P('dp')
- grad_cross_kv: float32 [768, 1536], P('dp')
- grad_cross_out: float32 [768, 768], P('dp')
- grad_cross_norm: float32 [768], P('dp')
- grad_final_norm: float32 [768], P('dp')
- grad_rel_bias: float32 [32, 12], replicated
The draws below stay inside these ranges and needn't reach their ends.
Inputs may be any that keep to these rules, and one draw needn't show every extreme that they name: `enc_segments`: each row holds documents 0 to 3 in order, each of one token or more; every row of the targets has the same 4 documents as the encoder row of the same index. `dec_segments`: as enc_segments: documents 0 to 3 in order, each of one token or more.
All inputs are finite; a program needn't handle non-finite values.
Results may differ from the reference program's by a relative error of at most 0.024.
Values may be sent and summed in bfloat16 or wider, within the bound.
A program may use at most 448 MiB of HBM per device.

```python
import jax
import jax.numpy as jnp
import numpy as np
from jax import lax

D = 768
H = 12
HD = 64
FF = 2048
NBUCKET = 32
MAXDIST = 128
LEN = 256
DOCS = 4
B = 32


def doc_ids(key, row_count, length, documents):
    scores = jax.random.randint(key, (row_count, length - 1), 0, 1 << 20) * length + jnp.arange(length - 1)[None, :]
    unused, picked = lax.top_k(scores, documents - 1)
    starts = picked + 1
    positions = jnp.arange(length)
    return jnp.sum((starts[:, :, None] <= positions[None, None, :]).astype(jnp.int32), axis=1).astype(jnp.int32)


def draw_enc_segments(key, part):
    key = jax.random.fold_in(key, 11)
    return doc_ids(key, B, LEN, DOCS)


def draw_dec_segments(key, part):
    key = jax.random.fold_in(key, 23)
    return doc_ids(key, B, LEN, DOCS)


def levels(key, dims, pieces, low, high):
    factor_of, own = 1.0, jax.random.fold_in(key, 6)
    for dim, shards_of in pieces:
        steps = jnp.exp(jax.random.uniform(jax.random.fold_in(own, dim), (shards_of,), jnp.float32, low / len(pieces), high / len(pieces)))
        factor_of = factor_of * jnp.repeat(steps, dims[dim] // shards_of).reshape([-1 if axis == dim else 1 for axis in range(len(dims))])
    return factor_of


def bell_draw(rng, shape, scale, reach, shards=(), kind=jnp.bfloat16):
    values = scale * jax.random.normal(rng, shape, jnp.float32)
    if shards:
        values = values * levels(rng, shape, shards, -0.22, 0.18)
    return jnp.clip(values, -reach, reach).astype(kind)


def setup_inputs(seed: int = 0) -> dict:
    key_list = jax.random.split(jax.random.key(seed), 17)
    return {
        "inputs": bell_draw(key_list[0], (2, B, LEN, D), 1.0, 6.0, ((0, 2), (1, 16))),
        "cotangent": bell_draw(key_list[1], (2, B, LEN, D), 1.0, 6.0, ((0, 2), (1, 16))),
        "enc_segments": draw_enc_segments(jax.random.fold_in(key_list[16], 71), 0),
        "dec_segments": draw_dec_segments(jax.random.fold_in(key_list[16], 71), 0),
        "rel_bias": bell_draw(key_list[4], (NBUCKET, H), 1.0, 4.0, (), jnp.float32),
        "attn_norm": jnp.clip(1.0 + 0.18 * jax.random.normal(key_list[5], (2, D), jnp.float32), 0.099609375, 1.8984375).astype(jnp.bfloat16),
        "ffn_norm": jnp.clip(1.0 + 0.18 * jax.random.normal(key_list[6], (2, D), jnp.float32), 0.099609375, 1.8984375).astype(jnp.bfloat16),
        "w_qkv": bell_draw(key_list[7], (2, D, 3 * D), (8 * D) ** -0.5, 0.078125, ((0, 2),)),
        "w_attn_out": bell_draw(key_list[8], (2, D, D), 4 ** -0.5, 3.0, ((0, 2),)),
        "w_gate_up": bell_draw(key_list[9], (2, D, 2 * FF), D ** -0.5, 0.21875, ((0, 2),)),
        "w_down": bell_draw(key_list[10], (2, FF, D), (FF // 2) ** -0.5, 0.1875, ((0, 2),)),
        "cross_norm": jnp.clip(1.0 + 0.18 * jax.random.normal(key_list[11], (D,), jnp.float32), 0.099609375, 1.8984375).astype(jnp.bfloat16),
        "cross_query": bell_draw(key_list[12], (D, D), (8 * D) ** -0.5, 0.078125),
        "cross_kv": bell_draw(key_list[13], (D, 2 * D), (8 * D) ** -0.5, 0.078125),
        "cross_out": bell_draw(key_list[14], (D, D), 4 ** -0.5, 3.0),
        "final_norm": jnp.clip(1.0 + 0.18 * jax.random.normal(key_list[15], (D,), jnp.float32), 0.099609375, 1.8984375).astype(jnp.bfloat16),
    }


@jax.custom_vjp
def low(v):
    return lax.optimization_barrier(v.astype(jnp.bfloat16)).astype(jnp.float32)

@jax.custom_vjp
def low_back(v):
    return v

def low_keep(v):
    return (low(v), None)

def low_pass(kept, grad):
    return (grad,)

def back_keep(v):
    return (v, None)

def back_low(kept, grad):
    return (low(grad),)
low.defvjp(low_keep, low_pass)
low_back.defvjp(back_keep, back_low)
EPSILON = 1e-06
MASKED = -1000000000.0
PRECISE = lax.Precision.HIGHEST

def bucket_grid(length, causal, buckets, reach_max):
    offsets = np.arange(length)[None, :] - np.arange(length)[:, None]
    if causal:
        half_count = buckets
        side_offset = offsets * 0
        distance = np.maximum(-offsets, 0)
    else:
        half_count = buckets // 2
        side_offset = (offsets > 0).astype(np.int32) * half_count
        distance = np.abs(offsets)
    exact_count = half_count // 2
    clipped = np.maximum(distance, exact_count)
    spread = exact_count + np.floor(np.log(clipped / exact_count) / np.log(reach_max / exact_count) * (half_count - exact_count) + 1e-09).astype(np.int32)
    spread = np.minimum(spread, half_count - 1)
    return (side_offset + np.where(distance < exact_count, distance, spread)).astype(np.int32)

def rms_norm(values, gain_vec):
    return values * lax.rsqrt(lax.optimization_barrier(jnp.mean(values * values, -1, keepdims=True)) + EPSILON) * gain_vec

def attention(queries, key_rows, value_rows, rel_terms, allowed):
    scores = jnp.einsum('qhd,khd->hqk', queries, key_rows, precision=PRECISE)
    if rel_terms is not None:
        scores = scores + rel_terms
    scores = low_back(jnp.where(allowed[None], scores, MASKED))
    softmaxed = low(jax.nn.softmax(scores, axis=-1))
    mixture = jnp.einsum('hqk,khd->qhd', softmaxed, value_rows, precision=PRECISE)
    return low_back(low(mixture.reshape(mixture.shape[0], -1)))

def self_block(normed, w_in, w_outer, rel_terms, allowed):
    length = normed.shape[0]
    packed = low_back(low(jnp.dot(normed, w_in, precision=PRECISE))).reshape(length, 3, H, HD)
    mixture = attention(packed[:, 0], packed[:, 1], packed[:, 2], rel_terms, allowed)
    return low_back(jnp.dot(mixture, w_outer, precision=PRECISE))

def cross_block(normed, memory, w_query, w_pair, w_outer, allowed):
    length = normed.shape[0]
    queries = low_back(low(jnp.dot(normed, w_query, precision=PRECISE))).reshape(length, H, HD)
    key_value = low_back(low(jnp.dot(memory, w_pair, precision=PRECISE))).reshape(memory.shape[0], 2, H, HD)
    mixture = attention(queries, key_value[:, 0], key_value[:, 1], None, allowed)
    return low_back(jnp.dot(mixture, w_outer, precision=PRECISE))

def feed_forward(normed, w_pair, w_lower):
    joined = low_back(jnp.dot(normed, w_pair, precision=PRECISE))
    hidden = low(jax.nn.gelu(joined[:, :FF], approximate=True) * joined[:, FF:])
    return low_back(jnp.dot(hidden, w_lower, precision=PRECISE))

def layer_pair(enc_input, dec_input, enc_segment, dec_segment, params, grid_enc, grid_dec):
    rel_bias, attn_norm, ffn_norm, w_qkv, w_attn_out, w_gate_up, w_down, cross_norm, cross_query, cross_kv, cross_out, final_norm = params
    length = enc_input.shape[0]
    enc_terms = jnp.transpose(jnp.take(rel_bias, grid_enc, axis=0), (2, 0, 1))
    dec_terms = jnp.transpose(jnp.take(rel_bias, grid_dec, axis=0), (2, 0, 1))
    lower_tri = jnp.arange(length)[:, None] >= jnp.arange(length)[None, :]
    enc_allowed = enc_segment[:, None] == enc_segment[None, :]
    dec_allowed = (dec_segment[:, None] == dec_segment[None, :]) & lower_tri
    cross_allowed = dec_segment[:, None] == enc_segment[None, :]
    after_attn = enc_input + self_block(low(rms_norm(enc_input, attn_norm[0])), w_qkv[0], w_attn_out[0], enc_terms, enc_allowed)
    second = after_attn + feed_forward(low(rms_norm(after_attn, ffn_norm[0])), w_gate_up[0], w_down[0])
    memory = low(rms_norm(second, final_norm))
    memory_in = low_back(memory)
    dec_attn = dec_input + self_block(low(rms_norm(dec_input, attn_norm[1])), w_qkv[1], w_attn_out[1], dec_terms, dec_allowed)
    middle = dec_attn + cross_block(low(rms_norm(dec_attn, cross_norm)), memory_in, cross_query, cross_kv, cross_out, cross_allowed)
    result = middle + feed_forward(low(rms_norm(middle, ffn_norm[1])), w_gate_up[1], w_down[1])
    return (memory, result)

def reference(inputs, cotangent, enc_segments, dec_segments, rel_bias, attn_norm, ffn_norm, w_qkv, w_attn_out, w_gate_up, w_down, cross_norm, cross_query, cross_kv, cross_out, final_norm):
    params = tuple((weight_in.astype(jnp.float32) for weight_in in (rel_bias, attn_norm, ffn_norm, w_qkv, w_attn_out, w_gate_up, w_down, cross_norm, cross_query, cross_kv, cross_out, final_norm)))
    length = inputs.shape[2]
    grid_enc = jnp.asarray(bucket_grid(length, False, NBUCKET, MAXDIST))
    grid_dec = jnp.asarray(bucket_grid(length, True, NBUCKET, MAXDIST))

    def one_row(totals, row_data):
        enc_input, dec_input, enc_grad_out, dec_grad_out, enc_segment, dec_segment = row_data

        def forward(enc_value, dec_value, weights):
            return layer_pair(enc_value, dec_value, enc_segment, dec_segment, weights, grid_enc, grid_dec)
        outputs, pullback = jax.vjp(forward, enc_input.astype(jnp.float32), dec_input.astype(jnp.float32), params)
        grad_enc, grad_dec, grad_params = pullback((enc_grad_out.astype(jnp.float32), dec_grad_out.astype(jnp.float32)))
        totals = jax.tree.map(lambda running, addend: running + addend, totals, grad_params)
        return (totals, (outputs[0].astype(jnp.bfloat16), outputs[1].astype(jnp.bfloat16), grad_enc, grad_dec))
    initial = jax.tree.map(jnp.zeros_like, params)
    totals, (memories, results, grad_enc, grad_dec) = lax.scan(one_row, initial, (inputs[0], inputs[1], cotangent[0], cotangent[1], enc_segments, dec_segments))
    layer_out = jnp.stack([memories, results])
    grad_inputs = jnp.stack([grad_enc, grad_dec])
    grad_rel_bias, grad_attn_norm, grad_ffn_norm, grad_qkv, grad_attn_out, grad_gate_up, grad_down, grad_cross_norm, grad_cross_query, grad_cross_kv, grad_cross_out, grad_final_norm = totals
    return (layer_out, grad_inputs, grad_qkv, grad_attn_out, grad_gate_up, grad_down, grad_attn_norm, grad_ffn_norm, grad_cross_query, grad_cross_kv, grad_cross_out, grad_cross_norm, grad_final_norm, grad_rel_bias)
```

```python
import functools

import jax
import jax.numpy as jnp
import numpy as np
from jax import lax
from jax.experimental import pallas as pl
from jax.experimental.pallas import tpu as pltpu
from jax.sharding import PartitionSpec as P

H = 12
HD = 64
NBUCKET = 32
MAXDIST = 128
MICRO = 2


EPSILON = 1e-06
MASKED = -1000000000.0
PRECISE = lax.Precision.HIGHEST
HALF_TYPE = jnp.bfloat16
FULL_TYPE = jnp.float32


MESH = pl.DeviceIdType.MESH


class Item:
    def __init__(self, rows, cols):
        self.rows, self.cols = rows, cols


def reduce_scratch(items):
    shapes = []
    for item in items:
        r, n = item.rows, item.cols
        shapes += [
            pltpu.VMEM((4, 2, 2, r, n), HALF_TYPE),
            pltpu.VMEM((4, 2, r, n), HALF_TYPE),
            pltpu.VMEM((4, r, n), HALF_TYPE),
            pltpu.VMEM((3, r, n), HALF_TYPE),
        ]
    count = len(items)
    return shapes + [pltpu.SemaphoreType.DMA((count, 10)), pltpu.SemaphoreType.DMA((count,))]


def reduce_kernel(items, *refs):
    count = len(items)
    ins, outs, scratch = refs[:count], refs[count : 2 * count], refs[2 * count :]
    sem, local_sem = scratch[4 * count], scratch[4 * count + 1]
    me, section = lax.axis_index("dp"), lax.axis_index("section")
    z, y, c = me // 4, (me // 2) % 2, me % 2

    def device(zz, yy, cc):
        return (section, zz * 4 + yy * 2 + cc)

    sibling, beside = device(z, y, 1 - c), device(z, 1 - y, c)
    peers = [(z + d) % 4 for d in (1, 2, 3)]
    barrier = pltpu.get_barrier_semaphore()
    for target in [sibling, beside] + [device(peer, y, c) for peer in peers]:
        pl.semaphore_signal(barrier, inc=1, device_id=target, device_id_type=MESH)
    pl.semaphore_wait(barrier, 5)

    def buffers(i):
        return scratch[4 * i : 4 * i + 4]

    def to_sibling(i):
        own, first, _, _ = buffers(i)
        return pltpu.make_async_remote_copy(
            own.at[:, :, 1 - c], first, sem.at[i, 0], sem.at[i, 1], device_id=sibling, device_id_type=MESH
        )

    def to_beside(i):
        own, _, second, _ = buffers(i)
        return pltpu.make_async_remote_copy(
            own.at[:, 1 - y, c], second, sem.at[i, 2], sem.at[i, 3], device_id=beside, device_id_type=MESH
        )

    def to_peer(i, d):
        own, _, _, third = buffers(i)
        return pltpu.make_async_remote_copy(
            own.at[peers[d], y, c],
            third.at[d],
            sem.at[i, 4 + d],
            sem.at[i, 7 + d],
            device_id=device(peers[d], y, c),
            device_id_type=MESH,
        )

    def add_first(i):
        own, first, _, _ = buffers(i)
        to_sibling(i).wait_recv()

        def body(j, carry):
            own[j // 2, j % 2, c] = own[j // 2, j % 2, c] + first[j // 2, j % 2]
            return carry

        lax.fori_loop(0, 8, body, 0)

    def add_second(i):
        own, _, second, _ = buffers(i)
        to_beside(i).wait_recv()

        def body(j, carry):
            own[j, y, c] = own[j, y, c] + second[j]
            return carry

        lax.fori_loop(0, 4, body, 0)

    def add_third(i):
        own, _, _, third = buffers(i)
        for d in range(3):
            to_peer(i, d).wait_recv()
        outs[i][...] = (own[z, y, c].astype(FULL_TYPE) + third[0].astype(FULL_TYPE)) + (
            third[1].astype(FULL_TYPE) + third[2].astype(FULL_TYPE)
        )

    local = [pltpu.make_async_copy(ins[i], buffers(i)[0], local_sem.at[i]) for i in range(count)]
    for copy in local:
        copy.start()
    for i in range(count):
        local[i].wait()
        to_sibling(i).start()
    for i in range(count):
        add_first(i)
        to_beside(i).start()
    for i in range(count):
        add_second(i)
        for d in range(3):
            to_peer(i, d).start()
    for i in range(count):
        add_third(i)
    for i in range(count):
        to_sibling(i).wait_send()
        to_beside(i).wait_send()
        for d in range(3):
            to_peer(i, d).wait_send()


def reduce_all(grads, width, ways):
    if ways != 16:
        return [
            lax.psum_scatter(g.astype(HALF_TYPE), "dp", scatter_dimension=0, tiled=True).astype(FULL_TYPE)
            for g in grads
        ]
    items, pieces = [], []
    for g in grads:
        rows = g.shape[0] // ways
        step = 512 if g.shape[1] % 768 else (768 if rows <= 48 else 256)
        for at in range(0, g.shape[1], step):
            items.append(Item(rows, step))
            pieces.append(g[:, at : at + step].astype(HALF_TYPE).reshape(4, 2, 2, rows, step))
    out = pl.pallas_call(
        functools.partial(reduce_kernel, items),
        out_shape=[jax.ShapeDtypeStruct((it.rows, it.cols), FULL_TYPE) for it in items],
        in_specs=[pl.BlockSpec(memory_space=pl.ANY)] * len(items),
        out_specs=[pl.BlockSpec(memory_space=pltpu.VMEM)] * len(items),
        scratch_shapes=reduce_scratch(items),
        compiler_params=pltpu.CompilerParams(
            collective_id=1, has_side_effects=True, vmem_limit_bytes=62 * 2**20
        ),
    )(*pieces)
    results, at = [], 0
    for g in grads:
        n = 0
        parts = []
        while n < g.shape[1]:
            parts.append(out[at])
            n += items[at].cols
            at += 1
        results.append(parts[0] if len(parts) == 1 else jnp.concatenate(parts, 1))
    return results


def shifted(value, axis, by):
    devices = lax.axis_size(axis)
    pairs = [(i, i + by) for i in range(devices) if 0 <= i + by < devices]
    return lax.ppermute(value, axis, pairs)


def bucket_grid(length, causal, buckets, reach_max):
    offsets = np.arange(length)[None, :] - np.arange(length)[:, None]
    if causal:
        half_count = buckets
        side_offset = offsets * 0
        distance = np.maximum(-offsets, 0)
    else:
        half_count = buckets // 2
        side_offset = (offsets > 0).astype(np.int32) * half_count
        distance = np.abs(offsets)
    exact_count = half_count // 2
    clipped = np.maximum(distance, exact_count)
    spread = exact_count + np.floor(
        np.log(clipped / exact_count) / np.log(reach_max / exact_count) * (half_count - exact_count)
        + 1e-09
    ).astype(np.int32)
    spread = np.minimum(spread, half_count - 1)
    return (side_offset + np.where(distance < exact_count, distance, spread)).astype(np.int32)


def matmul(left_side, right_side):
    return jnp.dot(left_side, right_side, preferred_element_type=FULL_TYPE)


def inner_rows(left_side, right_side):
    return lax.dot_general(
        left_side, right_side, (((0,), (0,)), ((), ())), preferred_element_type=FULL_TYPE
    )


def outer_cols(left_side, right_side):
    return lax.dot_general(
        left_side, right_side, (((1,), (1,)), ((), ())), preferred_element_type=FULL_TYPE
    )


def flatten_for(grads, ways):
    return jnp.concatenate([grad_part.reshape(ways, -1) for grad_part in grads], 1)


def unflatten_from(flat, grads, ways):
    pieces = []
    offset = 0
    for grad_part in grads:
        count = grad_part.size // ways
        shape = (grad_part.shape[0] // ways,) + tuple(grad_part.shape[1:])
        pieces.append(flat[0, offset : offset + count].reshape(shape))
        offset = offset + count
    return tuple(pieces)


def norm_forward(values, gain_vec):
    inverse = lax.rsqrt(jnp.mean(values * values, -1, keepdims=True) + EPSILON)
    unit_rows = values * inverse
    return (unit_rows * gain_vec, unit_rows, inverse)


def norm_backward(grad_normed, unit_rows, inverse, gain_vec):
    grad_unit = grad_normed * gain_vec
    grad_values = inverse * (
        grad_unit - unit_rows * jnp.mean(grad_unit * unit_rows, -1, keepdims=True)
    )
    grad_gain = jnp.sum((grad_normed * unit_rows).reshape(-1, unit_rows.shape[-1]), axis=0)
    return (grad_values, grad_gain)


def relative_terms(rel_bias, length, causal):
    bucket_ids = jnp.asarray(bucket_grid(length, causal, NBUCKET, MAXDIST))
    one_hot = bucket_ids[:, :, None] == jnp.arange(rel_bias.shape[0])[None, None, :]
    rel_terms = jnp.einsum("qkb,bh->hqk", one_hot.astype(FULL_TYPE), rel_bias, precision=PRECISE)
    return (rel_terms, one_hot.astype(HALF_TYPE))


def bias_gradient(grad_scores, one_hot):
    return jnp.einsum("rhqk,qkb->bh", grad_scores, one_hot, preferred_element_type=FULL_TYPE)


def scores_of(queries, key_rows, rel_terms, allowed):
    scores = jnp.einsum("rqhd,rkhd->rhqk", queries, key_rows, preferred_element_type=FULL_TYPE)
    if rel_terms is not None:
        scores = scores + rel_terms[None]
    return jnp.where(allowed[:, None], scores, MASKED)


def attend_forward(queries, key_rows, value_rows, rel_terms, allowed):
    scores = scores_of(queries, key_rows, rel_terms, allowed)
    row_max = jnp.max(scores, -1, keepdims=True)
    raised = jnp.exp(scores - row_max)
    row_total = jnp.sum(raised, -1, keepdims=True)
    softmaxed = (raised / row_total).astype(HALF_TYPE)
    mixture = jnp.einsum("rhqk,rkhd->rqhd", softmaxed, value_rows, preferred_element_type=FULL_TYPE)
    return (mixture, row_max + jnp.log(row_total))


def attend_backward(queries, key_rows, value_rows, rel_terms, allowed, log_total, grad_mixture):
    scores = scores_of(queries, key_rows, rel_terms, allowed)
    softmaxed = jnp.exp(scores - log_total)
    grad_value = jnp.einsum(
        "rhqk,rqhd->rkhd",
        softmaxed.astype(HALF_TYPE),
        grad_mixture,
        preferred_element_type=FULL_TYPE,
    )
    grad_probs = jnp.einsum(
        "rqhd,rkhd->rhqk", grad_mixture, value_rows, preferred_element_type=FULL_TYPE
    )
    grad_scores = (
        softmaxed * (grad_probs - jnp.sum(softmaxed * grad_probs, -1, keepdims=True))
    ).astype(HALF_TYPE)
    grad_query = jnp.einsum(
        "rhqk,rkhd->rqhd", grad_scores, key_rows, preferred_element_type=FULL_TYPE
    )
    grad_key = jnp.einsum("rhqk,rqhd->rkhd", grad_scores, queries, preferred_element_type=FULL_TYPE)
    return (grad_query, grad_key, grad_value, grad_scores)


def self_forward(values, gain_vec, w_in, w_outer, rel_terms, allowed):
    row_count, length, model_width = values.shape
    normed, unit_rows, inverse = norm_forward(values, gain_vec)
    normed_low = normed.astype(HALF_TYPE).reshape(-1, model_width)
    packed = matmul(normed_low, w_in).astype(HALF_TYPE).reshape(row_count, length, 3, H, HD)
    mixture, log_total = attend_forward(
        packed[:, :, 0], packed[:, :, 1], packed[:, :, 2], rel_terms, allowed
    )
    mixture_low = mixture.astype(HALF_TYPE).reshape(-1, model_width)
    branch = matmul(mixture_low, w_outer).reshape(values.shape)
    return (values + branch, (unit_rows, inverse, normed_low, packed, log_total, mixture_low))


def self_backward(grad_after, gain_vec, w_in, w_outer, rel_terms, allowed, kept_state):
    unit_rows, inverse, normed_low, packed, log_total, mixture_low = kept_state
    grad_low = grad_after.reshape(-1, grad_after.shape[-1]).astype(HALF_TYPE)
    grad_w_outer = inner_rows(mixture_low, grad_low)
    grad_mixture = outer_cols(grad_low, w_outer).astype(HALF_TYPE).reshape(packed[:, :, 0].shape)
    grad_query, grad_key, grad_value, grad_scores = attend_backward(
        packed[:, :, 0],
        packed[:, :, 1],
        packed[:, :, 2],
        rel_terms,
        allowed,
        log_total,
        grad_mixture,
    )
    grad_packed = (
        jnp.stack([grad_query, grad_key, grad_value], 2)
        .astype(HALF_TYPE)
        .reshape(normed_low.shape[0], -1)
    )
    grad_w_in = inner_rows(normed_low, grad_packed)
    grad_normed = outer_cols(grad_packed, w_in).reshape(grad_after.shape)
    grad_values, grad_gain = norm_backward(grad_normed, unit_rows, inverse, gain_vec)
    return (grad_after + grad_values, grad_w_in, grad_w_outer, grad_gain, grad_scores)


def cross_forward(values, gain_vec, w_query, w_pair, w_outer, memory, allowed):
    row_count, length, model_width = values.shape
    normed, unit_rows, inverse = norm_forward(values, gain_vec)
    normed_low = normed.astype(HALF_TYPE).reshape(-1, model_width)
    queries = matmul(normed_low, w_query).astype(HALF_TYPE).reshape(row_count, length, H, HD)
    memory_flat = memory.reshape(-1, model_width)
    key_value = (
        matmul(memory_flat, w_pair).astype(HALF_TYPE).reshape(row_count, memory.shape[1], 2, H, HD)
    )
    mixture, log_total = attend_forward(
        queries, key_value[:, :, 0], key_value[:, :, 1], None, allowed
    )
    mixture_low = mixture.astype(HALF_TYPE).reshape(-1, model_width)
    branch = matmul(mixture_low, w_outer).reshape(values.shape)
    return (
        values + branch,
        (unit_rows, inverse, normed_low, queries, key_value, log_total, mixture_low),
    )


def cross_backward(grad_after, gain_vec, w_query, w_pair, w_outer, memory, allowed, kept_state):
    unit_rows, inverse, normed_low, queries, key_value, log_total, mixture_low = kept_state
    model_width = grad_after.shape[-1]
    grad_low = grad_after.reshape(-1, model_width).astype(HALF_TYPE)
    grad_w_outer = inner_rows(mixture_low, grad_low)
    grad_mixture = outer_cols(grad_low, w_outer).astype(HALF_TYPE).reshape(queries.shape)
    grad_query, grad_key, grad_value, unused = attend_backward(
        queries, key_value[:, :, 0], key_value[:, :, 1], None, allowed, log_total, grad_mixture
    )
    grad_query_low = grad_query.astype(HALF_TYPE).reshape(normed_low.shape[0], -1)
    grad_pairs = jnp.stack([grad_key, grad_value], 2).astype(HALF_TYPE).reshape(-1, 2 * model_width)
    memory_flat = memory.reshape(-1, model_width)
    grad_w_query = inner_rows(normed_low, grad_query_low)
    grad_w_pair = inner_rows(memory_flat, grad_pairs)
    grad_memory = outer_cols(grad_pairs, w_pair).reshape(memory.shape)
    grad_normed = outer_cols(grad_query_low, w_query).reshape(grad_after.shape)
    grad_values, grad_gain = norm_backward(grad_normed, unit_rows, inverse, gain_vec)
    return (
        grad_after + grad_values,
        grad_w_query,
        grad_w_pair,
        grad_w_outer,
        grad_gain,
        grad_memory,
    )


def gated(gate_part, up_part):
    return jax.nn.gelu(gate_part, approximate=True) * up_part


def ffn_forward(values, gain_vec, w_pair, w_lower):
    model_width = values.shape[-1]
    hidden_units = w_lower.shape[0]
    normed, unit_rows, inverse = norm_forward(values, gain_vec)
    normed_low = normed.astype(HALF_TYPE).reshape(-1, model_width)
    joined = matmul(normed_low, w_pair)
    hidden_low = gated(joined[:, :hidden_units], joined[:, hidden_units:]).astype(HALF_TYPE)
    branch = matmul(hidden_low, w_lower).reshape(values.shape)
    return (values + branch, (unit_rows, inverse, normed_low, joined, hidden_low))


def ffn_backward(grad_after, gain_vec, w_pair, w_lower, kept_state):
    unit_rows, inverse, normed_low, joined, hidden_low = kept_state
    hidden_units = w_lower.shape[0]
    grad_low = grad_after.reshape(-1, grad_after.shape[-1]).astype(HALF_TYPE)
    grad_w_lower = inner_rows(hidden_low, grad_low)
    grad_hidden = outer_cols(grad_low, w_lower)
    unused, pullback = jax.vjp(gated, joined[:, :hidden_units], joined[:, hidden_units:])
    grad_gate, grad_up = pullback(grad_hidden)
    grad_joined = jnp.concatenate([grad_gate, grad_up], -1).astype(HALF_TYPE)
    grad_w_pair = inner_rows(normed_low, grad_joined)
    grad_normed = outer_cols(grad_joined, w_pair).reshape(grad_after.shape)
    grad_values, grad_gain = norm_backward(grad_normed, unit_rows, inverse, gain_vec)
    return (grad_after + grad_values, grad_w_pair, grad_w_lower, grad_gain)


def on_section(active, section_work, *operands):
    return lax.cond(
        active,
        section_work,
        lambda *passed: jax.tree.map(jnp.zeros_like, section_work(*passed)),
        *operands
    )


def add_trees(first_tree, second_tree):
    return tuple(
        jax.tree.map(
            lambda first_part, second_part: first_part + second_part, first_tree, second_tree
        )
    )


def shards(
    inputs,
    cotangent,
    enc_segments,
    dec_segments,
    rel_bias,
    attn_norm,
    ffn_norm,
    w_qkv,
    w_attn_out,
    w_gate_up,
    w_down,
    cross_norm,
    cross_query,
    cross_kv,
    cross_out,
    final_norm,
):
    section_id = lax.axis_index("section")
    ways = lax.axis_size("dp")
    encoder_side = section_id == 0
    decoder_side = section_id == 1
    length = inputs.shape[2]
    model_width = inputs.shape[3]
    rows_each = inputs.shape[1] // MICRO
    self_gain = attn_norm[0].astype(FULL_TYPE)
    ffn_gain = ffn_norm[0].astype(FULL_TYPE)
    cross_gain = cross_norm.astype(FULL_TYPE)
    final_gain = final_norm.astype(FULL_TYPE)
    qkv_local = w_qkv[0]
    out_local = w_attn_out[0]
    pair_local = w_gate_up[0]
    lower_local = w_down[0]
    lower_tri = jnp.arange(length)[:, None] >= jnp.arange(length)[None, :]
    width_zeros = jnp.zeros((model_width,), FULL_TYPE)

    def encoder_forward(values, segments):
        allowed = segments[:, :, None] == segments[:, None, :]
        rel_terms, one_hot = relative_terms(rel_bias, length, False)
        after_attn, kept_attn = self_forward(
            values, self_gain, qkv_local, out_local, rel_terms, allowed
        )
        second, kept_ffn = ffn_forward(after_attn, ffn_gain, pair_local, lower_local)
        normed, unit_rows, inverse = norm_forward(second, final_gain)
        return (normed.astype(HALF_TYPE), (kept_attn, kept_ffn, unit_rows, inverse))

    def encoder_top(kept_state, grad_memory):
        kept_attn, kept_ffn, unit_rows, inverse = kept_state
        grad_second, grad_final = norm_backward(grad_memory, unit_rows, inverse, final_gain)
        grad_middle, grad_pair, grad_lower, grad_ffn_gain = ffn_backward(
            grad_second, ffn_gain, pair_local, lower_local, kept_ffn
        )
        return (grad_middle, grad_pair, grad_lower, grad_ffn_gain, grad_final)

    def encoder_attn(segments, kept_state, grad_middle):
        allowed = segments[:, :, None] == segments[:, None, :]
        rel_terms, one_hot = relative_terms(rel_bias, length, False)
        grad_input, grad_in, grad_outer, grad_self_gain, grad_scores = self_backward(
            grad_middle, self_gain, qkv_local, out_local, rel_terms, allowed, kept_state[0]
        )
        return (
            grad_input,
            grad_in,
            grad_outer,
            grad_self_gain,
            bias_gradient(grad_scores, one_hot),
        )

    def encoder_backward(segments, kept_state, grad_memory):
        grad_middle, grad_pair, grad_lower, grad_ffn_gain, grad_final = encoder_top(
            kept_state, grad_memory
        )
        grad_input, grad_in, grad_outer, grad_self_gain, grad_rel = encoder_attn(
            segments, kept_state, grad_middle
        )
        grads = (
            grad_in,
            grad_outer,
            grad_pair,
            grad_lower,
            grad_self_gain,
            grad_ffn_gain,
            jnp.zeros(cross_query.shape, FULL_TYPE),
            jnp.zeros(cross_kv.shape, FULL_TYPE),
            jnp.zeros(cross_out.shape, FULL_TYPE),
            width_zeros,
            grad_final,
            grad_rel,
        )
        return (grad_input, grads)

    def decoder_step(values, grad_result, segments, memory_segments, memory):
        allowed = (segments[:, :, None] == segments[:, None, :]) & lower_tri[None]
        cross_allowed = segments[:, :, None] == memory_segments[:, None, :]
        rel_terms, one_hot = relative_terms(rel_bias, length, True)
        dec_attn, kept_attn = self_forward(
            values, self_gain, qkv_local, out_local, rel_terms, allowed
        )
        middle, kept_cross = cross_forward(
            dec_attn, cross_gain, cross_query, cross_kv, cross_out, memory, cross_allowed
        )
        result, kept_ffn = ffn_forward(middle, ffn_gain, pair_local, lower_local)
        grad_middle, grad_pair, grad_lower, grad_ffn_gain = ffn_backward(
            grad_result, ffn_gain, pair_local, lower_local, kept_ffn
        )
        (
            grad_upper,
            grad_cross_query,
            grad_cross_kv,
            grad_cross_out,
            grad_cross_gain,
            grad_memory,
        ) = cross_backward(
            grad_middle,
            cross_gain,
            cross_query,
            cross_kv,
            cross_out,
            memory,
            cross_allowed,
            kept_cross,
        )
        grad_input, grad_in, grad_outer, grad_self_gain, grad_scores = self_backward(
            grad_upper, self_gain, qkv_local, out_local, rel_terms, allowed, kept_attn
        )
        grads = (
            grad_in,
            grad_outer,
            grad_pair,
            grad_lower,
            grad_self_gain,
            grad_ffn_gain,
            grad_cross_query,
            grad_cross_kv,
            grad_cross_out,
            grad_cross_gain,
            width_zeros,
            bias_gradient(grad_scores, one_hot),
        )
        return (result.astype(HALF_TYPE), grad_input, grads, grad_memory.astype(HALF_TYPE))

    collected = None
    out_pieces = []
    grad_pieces = []
    for number in range(MICRO):
        row_slice = slice(number * rows_each, (number + 1) * rows_each)
        values = inputs[0, row_slice].astype(FULL_TYPE)
        grad_result = cotangent[0, row_slice].astype(FULL_TYPE)
        enc_segment = enc_segments[row_slice]
        dec_segment = dec_segments[row_slice]
        memory, kept_state = on_section(encoder_side, encoder_forward, values, enc_segment)
        received = shifted(memory, "section", 1)
        result, grad_dec_input, grads_dec, grad_memory = on_section(
            decoder_side, decoder_step, values, grad_result, dec_segment, enc_segment, received
        )
        returned = shifted(grad_memory, "section", -1)
        grad_top = grad_result + returned.astype(FULL_TYPE)
        out_pieces.append(memory + result)
        grad_enc_input, grads_enc = on_section(
            encoder_side, encoder_backward, enc_segment, kept_state, grad_top
        )
        micro_grads = add_trees(grads_dec, grads_enc)
        if collected is None:
            collected = micro_grads
        else:
            collected = add_trees(collected, micro_grads)
        grad_pieces.append(grad_dec_input + grad_enc_input)
    big = [collected[i] for i in (0, 1, 2, 3, 6, 7, 8)]
    small = [collected[i] for i in (4, 5, 9, 10)]
    big = reduce_all(big, model_width, ways)
    small = lax.psum_scatter(jnp.stack(small, 1), "dp", scatter_dimension=0, tiled=True)
    collected = (
        big[0],
        big[1],
        big[2],
        big[3],
        small[:, 0],
        small[:, 1],
        big[4],
        big[5],
        big[6],
        small[:, 2],
        small[:, 3],
        collected[11],
    )
    (
        shard_qkv,
        shard_out,
        shard_pair,
        shard_lower,
        shard_attn,
        shard_ffn,
        shard_query,
        shard_kv,
        shard_cross_out,
        shard_cross_gain,
        shard_final,
        shard_rel,
    ) = collected
    shared_query, shared_kv, shared_cross_out, shared_cross_gain, shared_final = (
        lax.psum(shard_query.astype(jnp.bfloat16), "section").astype(jnp.float32),
        lax.psum(shard_kv.astype(jnp.bfloat16), "section").astype(jnp.float32),
        lax.psum(shard_cross_out.astype(jnp.bfloat16), "section").astype(jnp.float32),
        lax.psum(shard_cross_gain.astype(jnp.bfloat16), "section").astype(jnp.float32),
        lax.psum(shard_final.astype(jnp.bfloat16), "section").astype(jnp.float32),
    )
    rel_total = lax.psum(shard_rel, ("section", "dp"))
    layer_out = jnp.concatenate(out_pieces, 0)[None]
    grad_inputs = jnp.concatenate(grad_pieces, 0)[None]
    return (
        layer_out,
        grad_inputs,
        shard_qkv[None],
        shard_out[None],
        shard_pair[None],
        shard_lower[None],
        shard_attn[None],
        shard_ffn[None],
        shared_query,
        shared_kv,
        shared_cross_out,
        shared_cross_gain,
        shared_final,
        rel_total,
    )


def solution(mesh):
    return jax.shard_map(
        shards,
        mesh=mesh,
        in_specs=(
            P("section", "dp", None, None),
            P("section", "dp", None, None),
            P("dp", None),
            P("dp", None),
            P(),
            P("section", None),
            P("section", None),
            P("section", None, None),
            P("section", None, None),
            P("section", None, None),
            P("section", None, None),
            P(),
            P(),
            P(),
            P(),
            P(),
        ),
        out_specs=(
            P("section", "dp", None, None),
            P("section", "dp", None, None),
            P("section", "dp", None),
            P("section", "dp", None),
            P("section", "dp", None),
            P("section", "dp", None),
            P("section", "dp"),
            P("section", "dp"),
            P("dp", None),
            P("dp", None),
            P("dp", None),
            P("dp"),
            P("dp"),
            P(),
        ),
        check_vma=False,
    )
```

```python
import functools
import math
import types

import jax
import jax.numpy as jnp
import numpy as np
from jax import lax
from jax.experimental import pallas as pl
from jax.experimental.pallas import tpu as pltpu
from jax.sharding import PartitionSpec as P

H = 12
HD = 64
NBUCKET = 32
MAXDIST = 128
EPSILON = 1e-06
MASKED = -1000000000.0
MESH = pl.DeviceIdType.MESH
PRECISE = lax.Precision.HIGHEST
HALF = jnp.bfloat16
FULL = jnp.float32
PAIRS = H // 2
CHUNK = 256
BLOCK = 64
GATE_UP, DOWN, CROSS, SELF = range(4)
GELU_SCALE = math.sqrt(2.0 / math.pi)
GELU_CUBE = 0.044715


def bucket_of(offsets, causal, buckets, reach_max):
    if causal:
        half_count = buckets
        side_offset = offsets * 0
        distance = np.maximum(-offsets, 0)
    else:
        half_count = buckets // 2
        side_offset = (offsets > 0).astype(np.int32) * half_count
        distance = np.abs(offsets)
    exact_count = half_count // 2
    clipped = np.maximum(distance, exact_count)
    spread = exact_count + np.floor(
        np.log(clipped / exact_count) / np.log(reach_max / exact_count) * (half_count - exact_count)
        + 1e-09
    ).astype(np.int32)
    spread = np.minimum(spread, half_count - 1)
    return (side_offset + np.where(distance < exact_count, distance, spread)).astype(np.int32)


def bucket_tables(length):
    lane = np.arange(length)
    spread = np.concatenate([-lane, length - lane])
    summed = np.concatenate([-(lane + 1), length - 1 - lane])
    tables = []
    for offsets in (spread, summed):
        clipped = np.clip(offsets, -(length - 1), length - 1)
        tables.append(
            np.stack(
                [
                    (bucket_of(clipped, causal, NBUCKET, MAXDIST)[None] == np.arange(NBUCKET)[:, None])
                    for causal in (False, True)
                ]
            ).astype(np.float32)
        )
    return tables


def dot(left, right):
    return jnp.dot(left, right, preferred_element_type=FULL)


def dot_inner(left, right):
    return lax.dot_general(left, right, (((0,), (0,)), ((), ())), preferred_element_type=FULL)


def dot_outer(left, right):
    return lax.dot_general(left, right, (((1,), (1,)), ((), ())), preferred_element_type=FULL)


def repeat(count, step):
    def body(index, carry):
        step(index)
        return carry

    lax.fori_loop(0, count, body, 0)


def at128(index, scale):
    return pl.multiple_of(index * scale, 128)


class Group:
    def __init__(self, name, count, rows, cols):
        self.name, self.count, self.rows, self.cols = name, count, rows, cols


def layer_kernel(names, groups, reduce, rows, length, width, hidden, *refs):
    v = types.SimpleNamespace(**dict(zip(names, refs)))
    tokens = rows * length
    chunks = hidden // CHUNK
    ways_rows = width // 16
    me, section = lax.axis_index("dp"), lax.axis_index("section")
    encoder, decoder = section == 0, section == 1
    z, y, c = me // 4, (me // 2) % 2, me % 2
    other = (1 - section, me)

    x_send, x_recv = v.x_send, v.x_recv
    low, low_t = v.low, v.low_t
    unit_ffn, unit_mid, cot = v.unit_ffn, v.unit_mid, v.cot
    grad_mix = cot
    res, grad = v.res, v.grad
    w_att, w_out, w_pair, w_lower = v.w_att, v.w_out, v.w_pair, v.w_lower
    qkv_self, qkv_cross = v.qkv_self, v.qkv_cross
    mix_self, mix_cross = v.mix_self, v.mix_cross
    probs, big = v.probs, v.big
    inverse, table, sums = v.inverse, v.table, v.sums
    joint, wide, narrow = v.joint, v.wide, v.narrow
    bias = [wide.at[e * length : (e + 1) * length, :length] for e in range(2)]
    mask = [wide.at[row * length : (row + 1) * length, length : 2 * length] for row in range(rows)]
    misc = v.misc
    load, sem_x, sem_misc, sem_out = v.load, v.sem_x, v.sem_misc, v.sem_out

    def device(zz, yy, cc):
        return (section, zz * 4 + yy * 2 + cc)

    partners = [other]
    if reduce:
        sibling, beside = device(z, y, 1 - c), device(z, 1 - y, c)
        peer_z = [(z + d) % 4 for d in (1, 2, 3)]
        partners += [sibling, beside] + [device(p, y, c) for p in peer_z]
    barrier = pltpu.get_barrier_semaphore()
    for target in partners:
        pl.semaphore_signal(barrier, inc=1, device_id=target, device_id_type=MESH)

    def copy_in(source, target, slot):
        return pltpu.make_async_copy(source, target, load.at[slot])

    def load_x():
        return copy_in(v.inputs, x_send, 0)

    def load_cot():
        return copy_in(v.cotangent, cot, 1)

    def load_att():
        return copy_in(v.w_qkv.at[0], w_att, 2)

    def load_out():
        return copy_in(v.w_attn_out.at[0], w_out, 3)

    def load_cross():
        return [
            copy_in(v.cross_query, w_att.at[:, pl.ds(0, width)], 2),
            copy_in(v.cross_kv, w_att.at[:, pl.ds(width, 2 * width)], 4),
        ]

    def load_cross_out():
        return copy_in(v.cross_out, w_out, 3)

    def load_chunk(index):
        slot = index % 2
        at = at128(index, CHUNK)
        return [
            copy_in(
                v.w_gate_up.at[0, :, pl.ds(at, CHUNK)], w_pair.at[slot, :, pl.ds(0, CHUNK)], 5 + slot
            ),
            copy_in(
                v.w_gate_up.at[0, :, pl.ds(pl.multiple_of(hidden + at, 128), CHUNK)],
                w_pair.at[slot, :, pl.ds(CHUNK, CHUNK)],
                7 + slot,
            ),
            copy_in(v.w_down.at[0, pl.ds(at, CHUNK), :], w_lower.at[slot], 9 + slot),
        ]

    load_x().start()
    load_att().start()
    load_out().start()
    load_cot().start()
    for copy in load_chunk(0):
        copy.start()

    by_name = {group.name: group for group in groups}
    stacks = {
        group.name: (big if group.name == SELF else getattr(v, f"own{group.name}")) for group in groups
    }

    def block_place(shard):
        if not reduce:
            return shard
        return (shard % 2) * 8 + ((shard // 2) % 2) * 4 + shard // 4

    def put(name, item, columns, tile):
        own, r = stacks[name], by_name[name].rows
        low_tile = tile.astype(HALF)
        for shard in range(16):
            own[item, block_place(shard) * r : (block_place(shard) + 1) * r, columns] = low_tile[
                shard * r : (shard + 1) * r
            ]

    def send_first(name, i):
        r = by_name[name].rows
        return pltpu.make_async_remote_copy(
            stacks[name].at[i, pl.ds(pl.multiple_of((1 - c) * 8 * r, 16), 8 * r)],
            getattr(v, f"first{name}").at[i],
            getattr(v, f"sem{name}").at[i, 0],
            getattr(v, f"sem{name}").at[i, 1],
            device_id=sibling,
            device_id_type=MESH,
        )

    def send_second(name, i):
        r = by_name[name].rows
        return pltpu.make_async_remote_copy(
            stacks[name].at[i, pl.ds(pl.multiple_of(c * 8 * r + (1 - y) * 4 * r, 16), 4 * r)],
            getattr(v, f"second{name}").at[i],
            getattr(v, f"sem{name}").at[i, 2],
            getattr(v, f"sem{name}").at[i, 3],
            device_id=beside,
            device_id_type=MESH,
        )

    def send_third(name, i, d):
        r = by_name[name].rows
        return pltpu.make_async_remote_copy(
            stacks[name].at[i, pl.ds(pl.multiple_of(c * 8 * r + y * 4 * r + peer_z[d] * r, 16), r)],
            getattr(v, f"third{name}").at[i, d],
            getattr(v, f"sem{name}").at[i, 4 + d],
            getattr(v, f"sem{name}").at[i, 7 + d],
            device_id=device(peer_z[d], y, c),
            device_id_type=MESH,
        )

    def kept_rows(name):
        r = by_name[name].rows
        return pl.ds(pl.multiple_of(c * 8 * r + y * 4 * r + z * r, 16), r)

    def write_out(name, i):
        if reduce:
            source = stacks[name].at[i, kept_rows(name)]
        else:
            source = stacks[name].at[i]
        return pltpu.make_async_copy(source, getattr(v, f"out{name}").at[i], getattr(v, f"sem{name}").at[i, 10])

    def cross_over(i):
        return pltpu.make_async_remote_copy(
            stacks[CROSS].at[i, kept_rows(CROSS)],
            v.out2.at[i],
            v.sem2.at[i, 11],
            v.sem2.at[i, 12],
            device_id=other,
            device_id_type=MESH,
        )

    def begin(name, i):
        if reduce:
            send_first(name, i).start()
        else:
            write_out(name, i).start()

    def add_first(name, i):
        if not reduce:
            return
        own, first, r = stacks[name], getattr(v, f"first{name}"), by_name[name].rows
        send_first(name, i).wait_recv()

        def step(m):
            kept = pl.ds(pl.multiple_of(c * 8 * r + m * r, 16), r)
            own[i, kept] = own[i, kept] + first[i, pl.ds(pl.multiple_of(m * r, 16), r)]

        repeat(8, step)
        send_second(name, i).start()

    def add_second(name, i):
        if not reduce:
            return
        own, second, r = stacks[name], getattr(v, f"second{name}"), by_name[name].rows
        send_second(name, i).wait_recv()

        def step(m):
            kept = pl.ds(pl.multiple_of(c * 8 * r + y * 4 * r + m * r, 16), r)
            own[i, kept] = own[i, kept] + second[i, pl.ds(pl.multiple_of(m * r, 16), r)]

        repeat(4, step)
        for d in range(3):
            send_third(name, i, d).start()

    def add_third(name, i):
        if reduce:
            own, third = stacks[name], getattr(v, f"third{name}")
            for d in range(3):
                send_third(name, i, d).wait_recv()
            kept = kept_rows(name)
            total = (own[i, kept].astype(FULL) + third[i, 0].astype(FULL)) + (
                third[i, 1].astype(FULL) + third[i, 2].astype(FULL)
            )
            own[i, kept] = total.astype(HALF)
            write_out(name, i).start()
            if name == CROSS:
                cross_over(i).start()

    def finish(name, i):
        write_out(name, i).wait()
        if reduce:
            send_first(name, i).wait_send()
            send_second(name, i).wait_send()
            for d in range(3):
                send_third(name, i, d).wait_send()
            if name == CROSS:
                cross_over(i).wait_send()

    def block_of(ref, b):
        return ref.at[b // 9, pl.ds(at128((b % 9) // 3, 256), 256), pl.ds(at128(b % 3, 256), 256)]

    def self_probs(head, row):
        return probs.at[head * rows + row]

    def cross_probs(head, row):
        return block_of(big, head * rows + row)

    def row_slice(row):
        return slice(row * length, (row + 1) * length)

    lanes = lax.broadcasted_iota(jnp.int32, (1, 128), 1)
    half_lanes = [(lanes < HD).astype(HALF), (lanes >= HD).astype(HALF)]

    def make_mask(key_segments, query_segments, causal):
        for row in range(rows):
            keys = jnp.broadcast_to(key_segments[row : row + 1].astype(FULL), (8, length)).T[:, :1]
            queries = query_segments[row : row + 1].astype(FULL)
            same = keys == queries
            if causal is not None:
                key_at = lax.broadcasted_iota(jnp.int32, (length, length), 0)
                query_at = lax.broadcasted_iota(jnp.int32, (length, length), 1)
                same = same & ((key_at <= query_at) | causal)
            mask[row][...] = jnp.where(same, 0.0, MASKED).astype(FULL)

    def attend(qkv, probs_of, mix, with_bias):
        def pair(hp):
            if with_bias:
                key_at = lax.broadcasted_iota(jnp.int32, (length, length), 0)
                lane = lax.broadcasted_iota(jnp.int32, (length, length), 1)
                for e in range(2):
                    line = table[pl.ds(hp * 2 + e, 1), :]
                    skewed = jnp.where(
                        lane + key_at < length,
                        jnp.broadcast_to(line[:, :length], (length, length)),
                        jnp.broadcast_to(line[:, length:], (length, length)),
                    )
                    bias[e][...] = pltpu.roll(skewed, 0, 1, stride=1, stride_axis=0)
            for row in range(rows):
                at = row_slice(row)
                queries = qkv[at, pl.ds(at128(hp, 128), 128)]
                keys = qkv[at, pl.ds(pl.multiple_of(width + hp * 128, 128), 128)]
                values_t = qkv[at, pl.ds(pl.multiple_of(2 * width + hp * 128, 128), 128)].T
                for e in range(2):
                    scores = dot_outer(keys * half_lanes[e], queries)
                    soft_parts = []
                    for part in range(length // 128):
                        n = slice(part * 128, (part + 1) * 128)
                        shifted = scores[:, n] + mask[row][:, n]
                        if with_bias:
                            shifted = shifted + bias[e][:, n]
                        raised = jnp.exp(shifted - jnp.max(shifted, 0, keepdims=True))
                        total = jnp.sum(raised, 0, keepdims=True)
                        soft_parts.append((raised * (1.0 / total)).astype(HALF))
                    softmaxed = jnp.concatenate(soft_parts, 1)
                    probs_of(hp * 2 + e, row)[...] = softmaxed
                    mixed = dot(values_t[e * HD : (e + 1) * HD], softmaxed)
                    mix[pl.ds(pl.multiple_of(hp * 128 + e * HD, 16), HD), at] = mixed.astype(HALF)

        repeat(PAIRS, pair)

    def attend_back(qkv, probs_of, with_bias):
        upper = lax.broadcasted_iota(jnp.int32, (128, length), 0) < HD
        left = lax.broadcasted_iota(jnp.int32, (length, 128), 1) < HD
        if with_bias:
            row_at = lax.broadcasted_iota(jnp.int32, (length, length), 0)
            lane_at = lax.broadcasted_iota(jnp.int32, (length, length), 1)
            flip = (row_at + lane_at == length - 1).astype(FULL).astype(HALF)

        def pair(hp):
            turned = [None, None]
            for row in range(rows):
                at = row_slice(row)
                q_lanes = pl.ds(at128(hp, 128), 128)
                k_lanes = pl.ds(pl.multiple_of(width + hp * 128, 128), 128)
                v_lanes = pl.ds(pl.multiple_of(2 * width + hp * 128, 128), 128)
                queries, keys, values = qkv[at, q_lanes], qkv[at, k_lanes], qkv[at, v_lanes]
                outer = grad_mix[at, q_lanes]
                keys_t = keys.T
                parts = []
                for e in range(2):
                    soft_low = probs_of(hp * 2 + e, row)[...]
                    grad_soft = dot_outer(values * half_lanes[e], outer)
                    score_parts = []
                    for part in range(length // 128):
                        n = slice(part * 128, (part + 1) * 128)
                        soft = soft_low[:, n].astype(FULL)
                        weighted = soft * grad_soft[:, n]
                        shared = jnp.sum(weighted, 0, keepdims=True)
                        score_parts.append((weighted - soft * shared).astype(HALF))
                    scores = jnp.concatenate(score_parts, 1)
                    parts.append((dot(keys_t, scores), dot(scores, queries), dot(soft_low, outer)))
                    if with_bias:
                        more = dot(flip, scores)
                        turned[e] = more if turned[e] is None else turned[e] + more
                qkv[at, q_lanes] = jnp.where(upper, parts[0][0], parts[1][0]).T.astype(HALF)
                qkv[at, k_lanes] = jnp.where(left, parts[0][1], parts[1][1]).astype(HALF)
                qkv[at, v_lanes] = jnp.where(left, parts[0][2], parts[1][2]).astype(HALF)
            if with_bias:
                for e in range(2):
                    aligned = pltpu.roll(turned[e], 0, 1, stride=1, stride_axis=0)
                    before = jnp.sum(jnp.where(lane_at < row_at, aligned, 0.0), 0, keepdims=True)
                    after = jnp.sum(jnp.where(lane_at < row_at, 0.0, aligned), 0, keepdims=True)
                    sums[pl.ds(hp * 2 + e, 1), :length] = before
                    sums[pl.ds(hp * 2 + e, 1), length:] = after

        repeat(PAIRS, pair)

    blocks = tokens // BLOCK

    def row_block(b):
        return pl.ds(pl.multiple_of(b * BLOCK, BLOCK), BLOCK)

    def normalise(load_rows, column, gain, unit_ref, target):
        def step(b):
            at = row_block(b)
            value = load_rows(at)
            scale = lax.rsqrt(jnp.mean(value * value, -1, keepdims=True) + EPSILON)
            inverse[at, column : column + 1] = scale
            unit = value * scale
            if unit_ref is not None:
                unit_ref[at, :] = unit.astype(HALF)
            target[at, :] = (unit * gain).astype(HALF)

        repeat(blocks, step)

    def norm_back(load_grad, load_unit, column, gain, misc_row, load_base, copy_low):
        def step(b, gain_sum):
            at = row_block(b)
            normed, unit = load_grad(at), load_unit(at)
            weighted = normed * unit
            grad_unit = normed * gain
            scale = inverse[at, column : column + 1]
            inner = jnp.mean(weighted * gain, -1, keepdims=True)
            result = scale * (grad_unit - unit * inner)
            if load_base is not None:
                result = result + load_base(at)
            grad[at, :] = result
            if copy_low:
                low[at, :] = result.astype(HALF)
            return gain_sum + jnp.sum(weighted.reshape(BLOCK // 8, 8, width), 0)

        gain_sum = lax.fori_loop(0, blocks, step, jnp.zeros((8, width), FULL))
        misc[0, misc_row : misc_row + 1, :width] = jnp.sum(gain_sum, 0, keepdims=True)

    def transpose_into(target, source):
        if source.shape[0] == tokens:

            def step(b):
                at = pl.ds(at128(b, 128), 128)
                target[:, at] = source[at, :].T
        else:

            def step(b):
                at = pl.ds(at128(b, 128), 128)
                target[at, :] = source[:, at].T

        repeat(tokens // 128, step)

    def column_tiles(count, step):
        repeat(count, lambda j: step(pl.ds(at128(j, 256), 256)))

    def add_projection(weights, base):
        def step(columns):
            res[:, columns] = base[:, columns].astype(FULL) + dot(low[...], weights[:, columns])

        column_tiles(width // 256, step)

    def feed_forward(forward, backward, total, grad_result):
        if backward:
            total[...] = jnp.zeros_like(total)

        def step(k):
            slot = k % 2

            @pl.when(k + 1 < chunks)
            def _():
                for copy in load_chunk(k + 1):
                    copy.start()

            for copy in load_chunk(k):
                copy.wait()
            kept = [[block_of(big, k * 4 + 2 * part + side) for side in range(2)] for part in range(2)]
            half = tokens // 2
            if forward:
                for side in range(2):
                    n = slice(side * CHUNK, (side + 1) * CHUNK)
                    if backward:
                        wide[:, n] = dot(low[...], w_pair[slot, :, n])
                    else:
                        product = dot(low[...], w_pair[slot, :, n])
                        wide[:, n] = product
                        for part in range(2):
                            kept[part][side][...] = product[part * half : (part + 1) * half].astype(HALF)
            if backward:
                narrow[...] = dot_outer(grad_result[...], w_lower[slot])
            for part in range(2):

                def bend(b):
                    inside = pl.ds(pl.multiple_of(b * BLOCK, BLOCK), BLOCK)
                    at = pl.ds(pl.multiple_of(part * half + b * BLOCK, BLOCK), BLOCK)
                    if forward:
                        gate, up = wide[at, :CHUNK], wide[at, CHUNK:]
                    else:
                        gate = kept[part][0][inside, :].astype(FULL)
                        up = kept[part][1][inside, :].astype(FULL)
                    squared = gate * gate
                    curve = jnp.tanh(gate * (GELU_SCALE + GELU_SCALE * GELU_CUBE * squared))
                    rising = 0.5 + 0.5 * curve
                    bent = gate * rising
                    v.units[at, :] = (bent * up).astype(HALF)
                    if backward:
                        grad_hidden = narrow[at, :]
                        slope = rising + 0.5 * gate * (1.0 - curve * curve) * (
                            GELU_SCALE + 3.0 * GELU_SCALE * GELU_CUBE * squared
                        )
                        joint[at, :CHUNK] = (grad_hidden * up * slope).astype(HALF)
                        joint[at, CHUNK:] = (grad_hidden * bent).astype(HALF)

                repeat(half // BLOCK, bend)
            if forward:
                for j in range(width // 256):
                    n = slice(j * 256, (j + 1) * 256)
                    res[:, n] = res[:, n] + dot(v.units[...], w_lower[slot, :, n])
            if backward:
                r = by_name[DOWN].rows
                for part in range(3):
                    lower = dot_inner(v.units[...], grad_result[:, part * 256 : (part + 1) * 256])
                    lower = lower.astype(HALF)
                    if reduce:
                        for shard in range(CHUNK // r):
                            place = (shard % 2) * 8 + (k % 2) * 4 + k // 2
                            v.own1[part, pl.ds(pl.multiple_of(place * r, 16), r)] = lower[
                                shard * r : (shard + 1) * r
                            ]
                    else:
                        v.own1[part, pl.ds(at128(k, CHUNK), CHUNK)] = lower
                for part in range(2):
                    columns = slice(part * CHUNK, (part + 1) * CHUNK)
                    put(GATE_UP, k, columns, dot(low_t[...], joint[:, columns]))
                begin(GATE_UP, k)

                @pl.when(k > 0)
                def _():
                    add_first(GATE_UP, k - 1)

                for j in range(width // 256):
                    n = slice(j * 256, (j + 1) * 256)
                    total[:, n] = total[:, n] + dot_outer(joint[...], w_pair[slot, n, :])

        repeat(chunks, step)
        if backward:
            for part in range(3):
                begin(DOWN, part)
            add_first(GATE_UP, chunks - 1)
            for part in range(3):
                add_first(DOWN, part)

    def weight_gradient(name, item, left_t, right, at):
        def step(j):
            tile = dot(left_t[...], right[:, pl.ds(pl.multiple_of(at + j * 256, 128), 256)])
            put(name, item, pl.ds(at128(j, 256), 256), tile)

        repeat(width // 256, step)
        begin(name, item)

    def back_through_out(mix, name):
        def step(j):
            n = pl.ds(at128(j, 256), 256)
            grad_mix[:, n] = dot_outer(low[...], w_out[n, :]).astype(HALF)

        repeat(width // 256, step)
        weight_gradient(name, 0, mix, low, 0)

    def as_full(ref):
        return lambda at: ref[at, :].astype(FULL)

    load_x().wait()
    normalise(as_full(x_send), 0, v.attn_norm[...].astype(FULL), None, low)
    load_att().wait()

    def project(columns):
        qkv_self[:, columns] = dot(low[...], w_att[:, columns]).astype(HALF)

    column_tiles(3 * width // 256, project)

    @pl.when(decoder)
    def _():
        for copy in load_cross():
            copy.start()

    segments = jnp.where(encoder, v.enc_segments[...], v.dec_segments[...])
    make_mask(segments, segments, encoder)
    table[0:H, :] = lax.dot_general(
        v.rel_bias[...],
        v.spread[section],
        (((0,), (0,)), ((), ())),
        precision=PRECISE,
        preferred_element_type=FULL,
    )
    attend(qkv_self, self_probs, mix_self, True)
    transpose_into(low, mix_self)
    load_out().wait()
    add_projection(w_out, x_send)

    @pl.when(decoder)
    def _():
        load_cross_out().start()

    def memory_copy(row):
        return pltpu.make_async_remote_copy(
            x_send.at[pl.ds(row * length, length)],
            x_recv.at[pl.ds(row * length, length)],
            sem_x.at[0, row],
            sem_x.at[1, row],
            device_id=other,
            device_id_type=MESH,
        )

    def memory_back(row):
        return pltpu.make_async_remote_copy(
            x_send.at[pl.ds(row * length, length)],
            x_recv.at[pl.ds(row * length, length)],
            sem_x.at[2, row],
            sem_x.at[3, row],
            device_id=other,
            device_id_type=MESH,
        )

    def write_layer():
        return pltpu.make_async_copy(x_send, v.layer_out, sem_out.at[0])

    pl.semaphore_wait(barrier, len(partners))
    ffn_gain = v.ffn_norm[...].astype(FULL)

    def enter_feed_forward():
        normalise(as_full(res), 1, ffn_gain, unit_ffn, low)
        transpose_into(low_t, low)

    @pl.when(encoder)
    def _():
        enter_feed_forward()
        feed_forward(True, False, None, None)
        for copy in load_chunk(0):
            copy.start()
        final_gain = v.final_norm[...].astype(FULL)
        normalise(as_full(res), 2, final_gain, unit_mid, x_send)
        for row in range(rows):
            memory_copy(row).start()
        write_layer().start()
        load_cot().wait()
        for row in range(rows):
            memory_back(row).wait_recv()

        def memory_grads(at):
            return cot[at, :].astype(FULL) + x_recv[at, :].astype(FULL)

        norm_back(memory_grads, as_full(unit_mid), 2, final_gain, 2, None, True)
        feed_forward(False, True, res, low)
        norm_back(as_full(res), as_full(unit_ffn), 1, ffn_gain, 1, as_full(grad), True)
        for row in range(rows):
            memory_copy(row).wait_send()

    @pl.when(decoder)
    def _():
        cross_gain = v.cross_norm[...].astype(FULL)
        normalise(as_full(res), 2, cross_gain, unit_mid, low)
        for copy in load_cross():
            copy.wait()

        def project_query(columns):
            qkv_cross[:, columns] = dot(low[...], w_att[:, columns]).astype(HALF)

        column_tiles(width // 256, project_query)
        make_mask(v.enc_segments[...], v.dec_segments[...], None)
        for row in range(rows):
            memory_copy(row).wait_recv()

        def project_memory(j):
            columns = pl.ds(pl.multiple_of(width + j * 256, 128), 256)
            qkv_cross[:, columns] = dot(x_recv[...], w_att[:, columns]).astype(HALF)

        repeat(2 * width // 256, project_memory)
        attend(qkv_cross, cross_probs, mix_cross, False)
        transpose_into(low, mix_cross)
        load_cross_out().wait()
        add_projection(w_out, res)
        enter_feed_forward()
        load_cot().wait()
        feed_forward(True, True, grad, cot)
        x_send[...] = res[...].astype(HALF)
        write_layer().start()
        norm_back(as_full(grad), as_full(unit_ffn), 1, ffn_gain, 1, as_full(cot), True)
        back_through_out(mix_cross, CROSS)
        load_out().start()
        attend_back(qkv_cross, cross_probs, False)
        write_layer().wait()

        def memory_grad(j):
            n = pl.ds(at128(j, 256), 256)
            x_send[:, n] = dot_outer(
                qkv_cross[:, pl.ds(width, 2 * width)], w_att[n, pl.ds(width, 2 * width)]
            ).astype(HALF)

        repeat(width // 256, memory_grad)
        for row in range(rows):
            memory_back(row).start()

        def query_grad(j):
            n = pl.ds(at128(j, 256), 256)
            res[:, n] = dot_outer(qkv_cross[:, pl.ds(0, width)], w_att[n, pl.ds(0, width)])

        repeat(width // 256, query_grad)
        load_att().start()

        def gained(b):
            at = pl.ds(at128(b, 128), 128)
            low_t[:, at] = (unit_mid[at, :].astype(FULL) * cross_gain).astype(HALF).T

        repeat(tokens // 128, gained)
        weight_gradient(CROSS, 1, low_t, qkv_cross, 0)
        transpose_into(low_t, x_recv)
        weight_gradient(CROSS, 2, low_t, qkv_cross, width)
        weight_gradient(CROSS, 3, low_t, qkv_cross, 2 * width)
        for item in range(4):
            add_first(CROSS, item)
        norm_back(as_full(res), as_full(unit_mid), 2, cross_gain, 2, as_full(grad), True)
        for row in range(rows):
            memory_back(row).wait_send()
        load_att().wait()
        load_out().wait()

    @pl.when(encoder)
    def _():
        write_layer().wait()

    load_x().start()
    back_through_out(mix_self, SELF)
    attend_back(qkv_self, self_probs, True)
    load_x().wait()
    attn_gain = v.attn_norm[...].astype(FULL)

    def unit_self(at):
        return x_send[at, :].astype(FULL) * inverse[at, 0:1]

    def gained_self(b):
        at = pl.ds(at128(b, 128), 128)
        low_t[:, at] = (unit_self(at) * attn_gain).astype(HALF).T

    repeat(tokens // 128, gained_self)
    add_first(SELF, 0)
    for item in range(1, 4):
        weight_gradient(SELF, item, low_t, qkv_self, (item - 1) * width)
    for item in range(1, 4):
        add_first(SELF, item)

    def input_grad(j):
        n = pl.ds(at128(j, 256), 256)
        res[:, n] = dot_outer(qkv_self[...], w_att[n, :])

    repeat(width // 256, input_grad)
    norm_back(as_full(res), unit_self, 0, attn_gain, 0, as_full(grad), False)
    write_grad = pltpu.make_async_copy(grad, v.grad_inputs, sem_out.at[1])
    write_grad.start()
    misc[0, 0:H, width : width + NBUCKET] = lax.dot_general(
        sums[0:H, :],
        v.summed[section],
        (((1,), (1,)), ((), ())),
        precision=PRECISE,
        preferred_element_type=FULL,
    )

    def misc_copy(source, target, slot, to):
        return pltpu.make_async_remote_copy(
            misc.at[source],
            misc.at[target],
            sem_misc.at[slot, 0],
            sem_misc.at[slot, 1],
            device_id=to,
            device_id_type=MESH,
        )

    def misc_out(source, place, slot):
        return pltpu.make_async_copy(misc.at[source], v.out_misc.at[place], sem_out.at[slot])

    if reduce:
        first = misc_copy(0, 1, 0, sibling)
        first.start()
        first.wait_recv()
        misc[2] = misc[0] + misc[1]
        second = misc_copy(2, 3, 1, beside)
        second.start()

    def drain(name):
        count = by_name[name].count

        def step(i):
            add_second(name, i)

            @pl.when(i >= 2)
            def _():
                add_third(name, i - 2)

        repeat(count, step)
        for i in range(max(count - 2, 0), count):
            add_third(name, i)

    order = [GATE_UP, DOWN]
    for name in order:
        drain(name)

    @pl.when(decoder)
    def _():
        drain(CROSS)

    if reduce:
        second.wait_recv()
        misc[4 + z] = misc[2] + misc[3]
        thirds = [misc_copy(4 + z, 4 + z, 2 + d, device(peer_z[d], y, c)) for d in range(3)]
        for copy in thirds:
            copy.start()
    drain(SELF)
    if reduce:
        for d in range(3):
            came = misc_copy(4 + z, 4 + (z + 3 - d) % 4, 2 + d, device(peer_z[d], y, c))
            came.wait_recv()
        misc[8] = (misc[4] + misc[5]) + (misc[6] + misc[7])
        across = misc_copy(8, 9, 5, other)
        across.start()
        across.wait_recv()
        outs = [misc_out(8, section, 2), misc_out(9, 1 - section, 3)]
    else:
        outs = [misc_out(0, 0, 2)]
    for copy in outs:
        copy.start()
    for name in (GATE_UP, DOWN, SELF):
        repeat(by_name[name].count, functools.partial(finish, name))

    @pl.when(decoder)
    def _():
        repeat(by_name[CROSS].count, functools.partial(finish, CROSS))

    if reduce:

        @pl.when(encoder)
        def _():
            repeat(by_name[CROSS].count, lambda i: cross_over(i).wait_recv())

        for copy in [first, second, across] + thirds:
            copy.wait_send()
    for copy in outs:
        copy.wait()
    write_grad.wait()


def run_layers(args, ways):
    (
        inputs,
        cotangent,
        enc_segments,
        dec_segments,
        rel_bias,
        attn_norm,
        ffn_norm,
        w_qkv,
        w_attn_out,
        w_gate_up,
        w_down,
        cross_norm,
        cross_query,
        cross_kv,
        cross_out,
        final_norm,
    ) = args
    _, rows, length, width = inputs.shape
    hidden = w_down.shape[1]
    tokens = rows * length
    reduce = ways == 16
    spread, summed = bucket_tables(length)
    operands = dict(
        inputs=inputs.reshape(tokens, width),
        cotangent=cotangent.reshape(tokens, width),
        w_qkv=w_qkv,
        w_attn_out=w_attn_out,
        w_gate_up=w_gate_up,
        w_down=w_down,
        cross_query=cross_query,
        cross_kv=cross_kv,
        cross_out=cross_out,
    )
    small = dict(
        enc_segments=enc_segments,
        dec_segments=dec_segments,
        rel_bias=rel_bias,
        attn_norm=attn_norm,
        ffn_norm=ffn_norm,
        cross_norm=cross_norm.reshape(1, width),
        final_norm=final_norm.reshape(1, width),
        spread=jnp.asarray(spread),
        summed=jnp.asarray(summed),
    )
    block = width // 16
    groups = [
        Group(GATE_UP, hidden // CHUNK, block, 2 * CHUNK),
        Group(DOWN, 3, hidden // 16, 256),
        Group(CROSS, 4, block, width),
        Group(SELF, 4, block, width),
    ]
    outs = dict(
        layer_out=((tokens, width), HALF),
        grad_inputs=((tokens, width), FULL),
    )
    for g in groups:
        outs[f"out{g.name}"] = ((g.count, g.rows if reduce else 16 * g.rows, g.cols), HALF)
    outs[MISC] = ((2 if reduce else 1, 16, width + 128), FULL)
    scratch = dict(
        x_send=pltpu.VMEM((tokens, width), HALF),
        x_recv=pltpu.VMEM((tokens, width), HALF),
        low=pltpu.VMEM((tokens, width), HALF),
        low_t=pltpu.VMEM((width, tokens), HALF),
        unit_ffn=pltpu.VMEM((tokens, width), HALF),
        unit_mid=pltpu.VMEM((tokens, width), HALF),
        cot=pltpu.VMEM((tokens, width), HALF),
        res=pltpu.VMEM((tokens, width), FULL),
        grad=pltpu.VMEM((tokens, width), FULL),
        joint=pltpu.VMEM((tokens, 2 * CHUNK), HALF),
        w_att=pltpu.VMEM((width, 3 * width), HALF),
        w_out=pltpu.VMEM((width, width), HALF),
        w_pair=pltpu.VMEM((2, width, 2 * CHUNK), HALF),
        w_lower=pltpu.VMEM((2, CHUNK, width), HALF),
        qkv_self=pltpu.VMEM((tokens, 3 * width), HALF),
        qkv_cross=pltpu.VMEM((tokens, 3 * width), HALF),
        mix_self=pltpu.VMEM((width, tokens), HALF),
        mix_cross=pltpu.VMEM((width, tokens), HALF),
        probs=pltpu.VMEM((H * rows, length, length), HALF),
        big=pltpu.VMEM((4, width, width), HALF),
        inverse=pltpu.VMEM((tokens, 8), FULL),
        wide=pltpu.VMEM((tokens, 2 * CHUNK), FULL),
        narrow=pltpu.VMEM((tokens, CHUNK), FULL),
        units=pltpu.VMEM((tokens, CHUNK), HALF),
        table=pltpu.VMEM((16, 2 * length), FULL),
        sums=pltpu.VMEM((16, 2 * length), FULL),
        misc=pltpu.VMEM((10 if reduce else 1, 16, width + 128), FULL),
        load=pltpu.SemaphoreType.DMA((11,)),
        sem_x=pltpu.SemaphoreType.DMA((4, rows)),
        sem_misc=pltpu.SemaphoreType.DMA((6, 2)),
        sem_out=pltpu.SemaphoreType.DMA((4,)),
    )
    for g in groups:
        if g.name != SELF:
            scratch[f"own{g.name}"] = pltpu.VMEM((g.count, 16 * g.rows, g.cols), HALF)
        if reduce:
            scratch[f"first{g.name}"] = pltpu.VMEM((g.count, 8 * g.rows, g.cols), HALF)
            scratch[f"second{g.name}"] = pltpu.VMEM((g.count, 4 * g.rows, g.cols), HALF)
            scratch[f"third{g.name}"] = pltpu.VMEM((g.count, 3, g.rows, g.cols), HALF)
        scratch[f"sem{g.name}"] = pltpu.SemaphoreType.DMA((g.count, 13))
    names = list(operands) + list(small) + list(outs) + list(scratch)
    results = pl.pallas_call(
        functools.partial(layer_kernel, names, groups, reduce, rows, length, width, hidden),
        out_shape=[jax.ShapeDtypeStruct(*out) for out in outs.values()],
        in_specs=[pl.BlockSpec(memory_space=pl.ANY)] * len(operands)
        + [pl.BlockSpec(memory_space=pltpu.VMEM)] * len(small),
        out_specs=[pl.BlockSpec(memory_space=pl.ANY)] * len(outs),
        scratch_shapes=list(scratch.values()),
        compiler_params=pltpu.CompilerParams(
            collective_id=1, has_side_effects=True, vmem_limit_bytes=VMEM_LIMIT
        ),
    )(*operands.values(), *small.values())
    return dict(zip(outs, results)), reduce


LAYER, INPUT, MISC = "layer_out", "grad_inputs", "out_misc"
VMEM_LIMIT = 64 * 2**20 - 64 * 2**10


def shards(*args):
    inputs, rel_bias = args[0], args[4]
    ways = lax.axis_size("dp")
    _, rows, length, width = inputs.shape
    hidden = args[10].shape[1]
    out, reduce = run_layers(args, ways)

    def wide(name):
        value = out[f"out{name}"]
        if reduce:
            return value.astype(FULL)
        total = lax.psum_scatter(value, "dp", scatter_dimension=1, tiled=True)
        if name == CROSS:
            total = lax.psum(jnp.where(lax.axis_index("section") == 1, total, 0), "section")
        return total.astype(FULL)

    def side_by_side(value):
        return jnp.swapaxes(value, 0, 1).reshape(value.shape[1], -1)

    gate_up = wide(GATE_UP)
    chunks, block, _ = gate_up.shape
    gate_up = gate_up.reshape(chunks, block, 2, CHUNK).transpose(1, 2, 0, 3).reshape(block, 2 * hidden)
    down, cross, late = wide(DOWN), wide(CROSS), wide(SELF)
    misc = out[MISC]
    section = lax.axis_index("section")
    if not reduce:
        mine = lax.psum(misc[0], "dp")
        misc = lax.all_gather(mine, "section", axis=0)
    own = lax.dynamic_index_in_dim(misc, section, 0, keepdims=False)
    start = lax.axis_index("dp") * block

    def piece(vector):
        return lax.dynamic_slice_in_dim(vector, start, block, 0)

    rel = (misc[0] + misc[1])[:H, width : width + NBUCKET].T
    return (
        out[LAYER].reshape(inputs.shape),
        out[INPUT].reshape(inputs.shape),
        side_by_side(late[1:])[None],
        late[0][None],
        gate_up[None],
        side_by_side(down)[None],
        piece(own[0, :width])[None],
        piece(own[1, :width])[None],
        cross[1],
        side_by_side(cross[2:]),
        cross[0],
        piece(misc[1, 2, :width]),
        piece(misc[0, 2, :width]),
        rel,
    )


def solution(mesh):
    layer = P("section", "dp", None, None)
    matrix = P("section", None, None)
    return jax.shard_map(
        shards,
        mesh=mesh,
        in_specs=(layer, layer, P("dp", None), P("dp", None), P())
        + (P("section", None),) * 2
        + (matrix,) * 4
        + (P(),) * 5,
        out_specs=(layer, layer)
        + (P("section", "dp", None),) * 4
        + (P("section", "dp"),) * 2
        + (P("dp", None),) * 3
        + (P("dp"),) * 2
        + (P(),),
        check_vma=False,
    )
```

```python
import functools
import math
import types

import jax
import jax.numpy as jnp
import numpy as np
from jax import lax
from jax.experimental import pallas as pl
from jax.experimental.pallas import tpu as pltpu
from jax.sharding import PartitionSpec as P

H = 12
HD = 64
NBUCKET = 32
MAXDIST = 128
EPSILON = 1e-06
MASKED = -1000000000.0
MESH = pl.DeviceIdType.MESH
PRECISE = lax.Precision.HIGHEST
HALF = jnp.bfloat16
FULL = jnp.float32
PAIRS = H // 2
CHUNK = 256
BLOCK = 64
UNROLL = 2
GATE_UP, DOWN, CROSS, SELF = range(4)
GELU_SCALE = math.sqrt(2.0 / math.pi)
GELU_CUBE = 0.044715


def bucket_of(offsets, causal, buckets, reach_max):
    if causal:
        half_count = buckets
        side_offset = offsets * 0
        distance = np.maximum(-offsets, 0)
    else:
        half_count = buckets // 2
        side_offset = (offsets > 0).astype(np.int32) * half_count
        distance = np.abs(offsets)
    exact_count = half_count // 2
    clipped = np.maximum(distance, exact_count)
    spread = exact_count + np.floor(
        np.log(clipped / exact_count) / np.log(reach_max / exact_count) * (half_count - exact_count)
        + 1e-09
    ).astype(np.int32)
    spread = np.minimum(spread, half_count - 1)
    return (side_offset + np.where(distance < exact_count, distance, spread)).astype(np.int32)


def bucket_tables(length):
    lane = np.arange(length)
    spread = np.concatenate([-lane, length - lane])
    summed = np.concatenate([-(lane + 1), length - 1 - lane])
    tables = []
    for offsets in (spread, summed):
        clipped = np.clip(offsets, -(length - 1), length - 1)
        tables.append(
            np.stack(
                [
                    (bucket_of(clipped, causal, NBUCKET, MAXDIST)[None] == np.arange(NBUCKET)[:, None])
                    for causal in (False, True)
                ]
            ).astype(np.float32)
        )
    return tables


def dot(left, right):
    return jnp.dot(left, right, preferred_element_type=FULL)


def dot_outer(left, right):
    return lax.dot_general(left, right, (((1,), (1,)), ((), ())), preferred_element_type=FULL)


def repeat(count, step):
    def body(index, carry):
        step(index)
        return carry

    lax.fori_loop(0, count, body, 0)


def at128(index, scale):
    return pl.multiple_of(index * scale, 128)


class Group:
    def __init__(self, name, count, rows, cols):
        self.name, self.count, self.rows, self.cols = name, count, rows, cols


def layer_kernel(names, groups, reduce, rows, length, width, hidden, *refs):
    v = types.SimpleNamespace(**dict(zip(names, refs)))
    tokens = rows * length
    chunks = hidden // CHUNK
    ways_rows = width // 16
    me, section = lax.axis_index("dp"), lax.axis_index("section")
    encoder, decoder = section == 0, section == 1
    z, y, c = me // 4, (me // 2) % 2, me % 2
    other = (1 - section, me)

    x_send, x_recv = v.x_send, v.x_recv
    low, low_t, grad_mix = v.low, v.low_t, v.grad_mix
    joint, units = grad_mix.at[:, : 2 * CHUNK], grad_mix.at[:, 2 * CHUNK : 3 * CHUNK]
    unit_ffn, unit_mid, cot = v.unit_ffn, v.unit_mid, v.cot
    res, grad = v.res, v.grad
    w_att, w_out, w_pair, w_lower = v.w_att, v.w_out, v.w_pair, v.w_lower
    qkv_self, qkv_cross = v.qkv_self, v.qkv_cross
    mix_self, mix_cross = v.mix_self, v.mix_cross
    probs, big = v.probs, v.big
    inverse, table, sums, mask = v.inverse, v.table, v.sums, v.mask
    misc = v.misc
    load, sem_x, sem_misc, sem_out = v.load, v.sem_x, v.sem_misc, v.sem_out

    def device(zz, yy, cc):
        return (section, zz * 4 + yy * 2 + cc)

    partners = [other]
    if reduce:
        sibling, beside = device(z, y, 1 - c), device(z, 1 - y, c)
        peer_z = [(z + d) % 4 for d in (1, 2, 3)]
        partners += [sibling, beside] + [device(p, y, c) for p in peer_z]
    barrier = pltpu.get_barrier_semaphore()
    for target in partners:
        pl.semaphore_signal(barrier, inc=1, device_id=target, device_id_type=MESH)

    def copy_in(source, target, slot):
        return pltpu.make_async_copy(source, target, load.at[slot])

    def load_x():
        return copy_in(v.inputs, x_send, 0)

    def load_cot():
        return copy_in(v.cotangent, cot, 1)

    def load_att():
        return copy_in(v.w_qkv.at[0], w_att, 2)

    def load_out():
        return copy_in(v.w_attn_out.at[0], w_out, 3)

    def load_cross():
        return [
            copy_in(v.cross_query, w_att.at[:, pl.ds(0, width)], 2),
            copy_in(v.cross_kv, w_att.at[:, pl.ds(width, 2 * width)], 4),
        ]

    def load_cross_out():
        return copy_in(v.cross_out, w_out, 3)

    def load_chunk(index):
        slot = index % 2
        at = at128(index, CHUNK)
        return [
            copy_in(
                v.w_gate_up.at[0, :, pl.ds(at, CHUNK)], w_pair.at[slot, :, pl.ds(0, CHUNK)], 5 + slot
            ),
            copy_in(
                v.w_gate_up.at[0, :, pl.ds(pl.multiple_of(hidden + at, 128), CHUNK)],
                w_pair.at[slot, :, pl.ds(CHUNK, CHUNK)],
                7 + slot,
            ),
            copy_in(v.w_down.at[0, pl.ds(at, CHUNK), :], w_lower.at[slot], 9 + slot),
        ]

    load_x().start()
    load_att().start()
    load_out().start()
    load_cot().start()
    misc[0] = jnp.zeros_like(misc[0])
    sums[...] = jnp.zeros_like(sums)
    for copy in load_chunk(0):
        copy.start()

    by_name = {group.name: group for group in groups}
    stacks = {
        group.name: (big if group.name == SELF else getattr(v, f"own{group.name}")) for group in groups
    }

    def block_place(shard):
        if not reduce:
            return shard
        return (shard % 2) * 8 + ((shard // 2) % 2) * 4 + shard // 4

    def put(name, item, columns, tile):
        own, r = stacks[name], by_name[name].rows
        low_tile = tile.astype(HALF)
        for shard in range(16):
            own[item, block_place(shard) * r : (block_place(shard) + 1) * r, columns] = low_tile[
                shard * r : (shard + 1) * r
            ]

    def send_first(name, i):
        r = by_name[name].rows
        return pltpu.make_async_remote_copy(
            stacks[name].at[i, pl.ds(pl.multiple_of((1 - c) * 8 * r, 16), 8 * r)],
            getattr(v, f"first{name}").at[i],
            getattr(v, f"sem{name}").at[i, 0],
            getattr(v, f"sem{name}").at[i, 1],
            device_id=sibling,
            device_id_type=MESH,
        )

    def send_second(name, i):
        r = by_name[name].rows
        return pltpu.make_async_remote_copy(
            stacks[name].at[i, pl.ds(pl.multiple_of(c * 8 * r + (1 - y) * 4 * r, 16), 4 * r)],
            getattr(v, f"second{name}").at[i],
            getattr(v, f"sem{name}").at[i, 2],
            getattr(v, f"sem{name}").at[i, 3],
            device_id=beside,
            device_id_type=MESH,
        )

    def send_third(name, i, d):
        r = by_name[name].rows
        return pltpu.make_async_remote_copy(
            stacks[name].at[i, pl.ds(pl.multiple_of(c * 8 * r + y * 4 * r + peer_z[d] * r, 16), r)],
            getattr(v, f"third{name}").at[i, d],
            getattr(v, f"sem{name}").at[i, 4 + d],
            getattr(v, f"sem{name}").at[i, 7 + d],
            device_id=device(peer_z[d], y, c),
            device_id_type=MESH,
        )

    def kept_rows(name):
        r = by_name[name].rows
        return pl.ds(pl.multiple_of(c * 8 * r + y * 4 * r + z * r, 16), r)

    def write_out(name, i):
        if reduce:
            source = stacks[name].at[i, kept_rows(name)]
        else:
            source = stacks[name].at[i]
        return pltpu.make_async_copy(source, getattr(v, f"out{name}").at[i], getattr(v, f"sem{name}").at[i, 10])

    def cross_over(i):
        return pltpu.make_async_remote_copy(
            stacks[CROSS].at[i, kept_rows(CROSS)],
            v.out2.at[i],
            v.sem2.at[i, 11],
            v.sem2.at[i, 12],
            device_id=other,
            device_id_type=MESH,
        )

    def begin(name, i):
        if reduce:
            send_first(name, i).start()
        else:
            write_out(name, i).start()

    def add_first(name, i):
        if not reduce:
            return
        own, first, r = stacks[name], getattr(v, f"first{name}"), by_name[name].rows
        send_first(name, i).wait_recv()

        def step(m):
            kept = pl.ds(pl.multiple_of(c * 8 * r + m * r, 16), r)
            own[i, kept] = own[i, kept] + first[i, pl.ds(pl.multiple_of(m * r, 16), r)]

        repeat(8, step)
        send_second(name, i).start()

    def add_second(name, i):
        if not reduce:
            return
        own, second, r = stacks[name], getattr(v, f"second{name}"), by_name[name].rows
        send_second(name, i).wait_recv()

        def step(m):
            kept = pl.ds(pl.multiple_of(c * 8 * r + y * 4 * r + m * r, 16), r)
            own[i, kept] = own[i, kept] + second[i, pl.ds(pl.multiple_of(m * r, 16), r)]

        repeat(4, step)
        for d in range(3):
            send_third(name, i, d).start()

    def add_third(name, i):
        if reduce:
            own, third = stacks[name], getattr(v, f"third{name}")
            for d in range(3):
                send_third(name, i, d).wait_recv()
            kept = kept_rows(name)
            total = (own[i, kept].astype(FULL) + third[i, 0].astype(FULL)) + (
                third[i, 1].astype(FULL) + third[i, 2].astype(FULL)
            )
            own[i, kept] = total.astype(HALF)
            write_out(name, i).start()
            if name == CROSS:
                cross_over(i).start()

    def finish(name, i):
        write_out(name, i).wait()
        if reduce:
            send_first(name, i).wait_send()
            send_second(name, i).wait_send()
            for d in range(3):
                send_third(name, i, d).wait_send()
            if name == CROSS:
                cross_over(i).wait_send()

    def block_of(ref, b):
        return ref.at[b // 9, pl.ds(at128((b % 9) // 3, 256), 256), pl.ds(at128(b % 3, 256), 256)]

    def decoder_unit(k):
        return block_of(big, H + 2 * chunks + k)

    def encoder_unit(k):
        lanes = pl.ds(pl.multiple_of(width + k // 2 * CHUNK, 128), CHUNK)
        return qkv_cross.at[pl.ds(at128(k % 2, length), length), lanes]

    def self_probs(head, row):
        return probs.at[head * rows + row]

    def cross_probs(head, row):
        return block_of(big, head)

    def row_slice(row):
        return pl.ds(pl.multiple_of(row * length, length), length)

    def part_slice(row, b, size):
        return pl.ds(pl.multiple_of(row * length + b * size, size), size)

    lanes = lax.broadcasted_iota(jnp.int32, (1, 128), 1)
    half_lanes = [(lanes < HD).astype(HALF), (lanes >= HD).astype(HALF)]

    def make_mask(key_segments, query_segments, row, causal):
        keys = key_segments[pl.ds(row, 1), :].astype(FULL)
        keys = jnp.broadcast_to(keys, (8, length)).T[:, :1]
        queries = query_segments[pl.ds(row, 1), :].astype(FULL)
        same = keys == queries
        if causal is not None:
            key_at = lax.broadcasted_iota(jnp.int32, (length, length), 0)
            query_at = lax.broadcasted_iota(jnp.int32, (length, length), 1)
            same = same & ((key_at <= query_at) | causal)
        mask[...] = jnp.where(same, 0.0, MASKED).astype(HALF)

    def lanes_of(offset, hp):
        return pl.ds(pl.multiple_of(offset + hp * 128, 128), 128)

    def attend(qkv, probs_of, mix, row, with_bias):
        at = row_slice(row)

        def pair(hp):
            queries = qkv[at, lanes_of(0, hp)]
            keys = qkv[at, lanes_of(width, hp)]
            values_t = qkv[at, lanes_of(2 * width, hp)].T
            both = jnp.concatenate([keys * half_lanes[0], keys * half_lanes[1]], 0)
            scores = dot_outer(both, queries)
            for e in range(2):
                if with_bias:
                    line = table[pl.ds(hp * 2 + e, 1), :]
                    skewed = line[:, length:] + v.near[...].astype(FULL) * (line[:, :length] - line[:, length:])
                    bias = pltpu.roll(skewed, 0, 1, stride=1, stride_axis=0)
                soft_parts = []
                for part in range(length // 128):
                    n = slice(part * 128, (part + 1) * 128)
                    shifted = scores[e * length : (e + 1) * length, n] + mask[:, n].astype(FULL)
                    if with_bias:
                        shifted = shifted + bias[:, n]
                    raised = jnp.exp(shifted - jnp.max(shifted, 0, keepdims=True))
                    total = jnp.sum(raised, 0, keepdims=True)
                    soft_parts.append((raised * (1.0 / total)).astype(HALF))
                softmaxed = jnp.concatenate(soft_parts, 1)
                probs_of(hp * 2 + e, row)[...] = softmaxed
                mixed = dot(values_t[e * HD : (e + 1) * HD], softmaxed)
                mix[pl.ds(pl.multiple_of(hp * 128 + e * HD, 16), HD), at] = mixed.astype(HALF)

        repeat_pairs(pair)

    def repeat_pairs(pair):
        def step(g):
            for u in range(UNROLL):
                pair(g * UNROLL + u)

        repeat(PAIRS // UNROLL, step)

    def attend_back(qkv, probs_of, row, with_bias, tick):
        at = row_slice(row)
        left = lax.broadcasted_iota(jnp.int32, (length, 128), 1) < HD
        def pair(hp):
            q_lanes, k_lanes, v_lanes = lanes_of(0, hp), lanes_of(width, hp), lanes_of(2 * width, hp)
            queries, keys, values = qkv[at, q_lanes], qkv[at, k_lanes], qkv[at, v_lanes]
            outer = grad_mix[:, q_lanes]
            keys_t = keys.T
            both = jnp.concatenate([values * half_lanes[0], values * half_lanes[1]], 0)
            grad_soft = dot_outer(both, outer)
            softs, scores = [], []
            for e in range(2):
                soft_low = probs_of(hp * 2 + e, row)[...]
                score_parts = []
                for part in range(length // 128):
                    n = slice(part * 128, (part + 1) * 128)
                    soft = soft_low[:, n].astype(FULL)
                    weighted = soft * grad_soft[e * length : (e + 1) * length, n]
                    shared = jnp.sum(weighted, 0, keepdims=True)
                    score_parts.append((weighted - soft * shared).astype(HALF))
                scores.append(jnp.concatenate(score_parts, 1))
                softs.append(soft_low)
            grad_keys = dot(jnp.concatenate(scores, 0), queries)
            grad_values = dot(jnp.concatenate(softs, 0), outer)
            left_side = jnp.concatenate([keys_t, v.flip[...]], 0) if with_bias else keys_t
            parts = []
            for e in range(2):
                product = dot(left_side, scores[e])
                parts.append(product[e * HD : (e + 1) * HD])
                if with_bias:
                    aligned = pltpu.roll(product[128:], 0, 1, stride=1, stride_axis=0)
                    before = jnp.sum(aligned * v.past[...].astype(FULL), 0, keepdims=True)
                    after = jnp.sum(aligned, 0, keepdims=True) - before
                    line = pl.ds(hp * 2 + e, 1)
                    sums[line, :] = sums[line, :] + jnp.concatenate([before, after], 1)
            qkv[at, q_lanes] = jnp.concatenate(parts, 0).T.astype(HALF)
            qkv[at, k_lanes] = jnp.where(left, grad_keys[:length], grad_keys[length:]).astype(HALF)
            qkv[at, v_lanes] = jnp.where(left, grad_values[:length], grad_values[length:]).astype(HALF)
            if tick is not None:
                tick(hp)

        repeat_pairs(pair)

    def normalise(load_rows, row, column, gain, unit_ref, target):
        for b in range(length // BLOCK):
            at = part_slice(row, b, BLOCK)
            value = load_rows(at)
            scale = lax.rsqrt(jnp.mean(value * value, -1, keepdims=True) + EPSILON)
            inverse[at, column : column + 1] = scale
            unit = value * scale
            if unit_ref is not None:
                unit_ref[at, :] = unit.astype(HALF)
            target[at, :] = (unit * gain).astype(HALF)

    def norm_back(load_grad, load_unit, row, column, gain, misc_row, load_base, low_ref):
        def step(b, gain_sum):
            at = part_slice(row, b, BLOCK)
            normed, unit = load_grad(at), load_unit(at)
            weighted = normed * unit
            grad_unit = normed * gain
            scale = inverse[at, column : column + 1]
            inner = jnp.mean(weighted * gain, -1, keepdims=True)
            result = scale * (grad_unit - unit * inner)
            if load_base is not None:
                result = result + load_base(at)
            grad[at, :] = result
            if low_ref is not None:
                low_ref[at, :] = result.astype(HALF)
            return gain_sum + jnp.sum(weighted.reshape(BLOCK // 8, 8, width), 0)

        gain_sum = lax.fori_loop(0, length // BLOCK, step, jnp.zeros((8, width), FULL))
        line = slice(misc_row, misc_row + 1)
        misc[0, line, :width] = misc[0, line, :width] + jnp.sum(gain_sum, 0, keepdims=True)

    def transpose_rows(target, source, row):
        for b in range(length // 128):
            at = part_slice(row, b, 128)
            target[:, at] = source[at, :].T

    def transpose_back(target, source, row):
        for b in range(length // 128):
            at = part_slice(row, b, 128)
            target[at, :] = source[:, at].T

    def add_projection(weights, base, row):
        at = row_slice(row)
        for j in range(width // 256):
            n = slice(j * 256, (j + 1) * 256)
            res[at, n] = base[at, n].astype(FULL) + dot(low[at, :], weights[:, n])

    def feed_forward(row, forward, backward, total, base, unit_block, more):
        at = row_slice(row)
        if backward:
            total[at, :] = jnp.zeros((length, width), FULL)

        def step(k):
            slot = k % 2

            @pl.when((k + 1 < chunks) | more)
            def _():
                for copy in load_chunk((k + 1) % chunks):
                    copy.start()

            for copy in load_chunk(k):
                copy.wait()
            kept = [block_of(big, row * 2 * chunks + k * 2 + side) for side in range(2)]
            if forward:
                joined = dot(low[at, :], w_pair[slot])
                gate, up = joined[:, :CHUNK], joined[:, CHUNK:]
                if not backward:
                    kept[0][...] = gate.astype(HALF)
                    kept[1][...] = up.astype(HALF)
            else:
                gate, up = kept[0][...].astype(FULL), kept[1][...].astype(FULL)
            squared = gate * gate
            curve = jnp.tanh(gate * (GELU_SCALE + GELU_SCALE * GELU_CUBE * squared))
            rising = 0.5 + 0.5 * curve
            bent = gate * rising
            unit = (bent * up).astype(HALF)
            if forward:
                res[at, :] = res[at, :] + dot(unit, w_lower[slot])
            if not backward:
                return
            grad_hidden = dot_outer(cot[at, :], w_lower[slot])
            slope = rising + 0.5 * gate * (1.0 - curve * curve) * (
                GELU_SCALE + 3.0 * GELU_SCALE * GELU_CUBE * squared
            )
            pair = jnp.concatenate(
                [(grad_hidden * up * slope).astype(HALF), (grad_hidden * bent).astype(HALF)], 1
            )
            total[at, :] = total[at, :] + dot_outer(pair, w_pair[slot])
            joint[...] = pair
            units[...] = unit.T
            first = [block_of(big, base + k * 2 + side) for side in range(2)]

            @pl.when(row == 0)
            def _():
                first[0][...] = joint[:, :CHUNK]
                first[1][...] = joint[:, CHUNK:]
                unit_block(k)[...] = units[...]

            @pl.when(row == rows - 1)
            def _():
                for part in range(2):
                    columns = slice(part * CHUNK, (part + 1) * CHUNK)
                    right = jnp.concatenate([first[part][...], joint[:, columns]], 0)
                    put(GATE_UP, k, columns, dot(low_t[...], right))
                begin(GATE_UP, k)
                r = by_name[DOWN].rows
                both = jnp.concatenate([unit_block(k)[...], units[...]], 1)
                for part in range(3):
                    lower = dot(both, cot[:, part * 256 : (part + 1) * 256]).astype(HALF)
                    if reduce:
                        for shard in range(CHUNK // r):
                            place = (shard % 2) * 8 + (k % 2) * 4 + k // 2
                            v.own1[part, pl.ds(pl.multiple_of(place * r, 16), r)] = lower[
                                shard * r : (shard + 1) * r
                            ]
                    else:
                        v.own1[part, pl.ds(at128(k, CHUNK), CHUNK)] = lower

                @pl.when(k > 0)
                def _():
                    add_first(GATE_UP, k - 1)

        repeat(chunks, step)
        if backward:

            @pl.when(row == rows - 1)
            def _():
                for part in range(3):
                    begin(DOWN, part)
                add_first(GATE_UP, chunks - 1)
                for part in range(3):
                    add_first(DOWN, part)

    def weight_gradient(name, item, left_t, right, at):
        def step(j):
            tile = dot(left_t[...], right[:, pl.ds(pl.multiple_of(at + j * 256, 128), 256)])
            put(name, item, pl.ds(at128(j, 256), 256), tile)

        repeat(width // 256, step)
        begin(name, item)

    def back_through_out(row):
        for j in range(width // 256):
            n = slice(j * 256, (j + 1) * 256)
            grad_mix[:, n] = dot_outer(low[row_slice(row), :], w_out[n, :]).astype(HALF)

    def as_full(ref):
        return lambda at: ref[at, :].astype(FULL)

    def memory_copy(row):
        return pltpu.make_async_remote_copy(
            x_send.at[row_slice(row)],
            x_recv.at[row_slice(row)],
            sem_x.at[0, row],
            sem_x.at[1, row],
            device_id=other,
            device_id_type=MESH,
        )

    def memory_back(row):
        return pltpu.make_async_remote_copy(
            x_send.at[row_slice(row)],
            x_recv.at[row_slice(row)],
            sem_x.at[2, row],
            sem_x.at[3, row],
            device_id=other,
            device_id_type=MESH,
        )

    def write_layer(row):
        return pltpu.make_async_copy(
            x_send.at[row_slice(row)], v.layer_out.at[row_slice(row)], sem_out.at[4 + row]
        )

    ffn_gain = v.ffn_norm[...].astype(FULL)
    attn_gain = v.attn_norm[...].astype(FULL)
    cross_gain = v.cross_norm[...].astype(FULL)
    final_gain = v.final_norm[...].astype(FULL)

    def enter_feed_forward(row):
        normalise(as_full(res), row, 1, ffn_gain, unit_ffn, low)
        transpose_rows(low_t, low, row)

    row_at = lax.broadcasted_iota(jnp.int32, (length, length), 0)
    lane_at = lax.broadcasted_iota(jnp.int32, (length, length), 1)
    v.near[...] = (lane_at + row_at < length).astype(FULL).astype(HALF)
    v.past[...] = (lane_at < row_at).astype(FULL).astype(HALF)
    v.flip[...] = (row_at + lane_at == length - 1).astype(FULL).astype(HALF)

    table[0:H, :] = lax.dot_general(
        v.rel_bias[...],
        v.spread[section].astype(FULL),
        (((0,), (0,)), ((), ())),
        precision=PRECISE,
        preferred_element_type=FULL,
    )
    segments = jnp.where(encoder, v.enc_segments[...], v.dec_segments[...])
    v.segments[0:rows, :] = segments
    load_x().wait()
    load_att().wait()
    load_out().wait()
    load_cot().wait()
    pl.semaphore_wait(barrier, len(partners))

    def forward_row(row):
        at = row_slice(row)
        normalise(as_full(x_send), row, 0, attn_gain, None, low)

        def project(j):
            columns = pl.ds(at128(j, 256), 256)
            qkv_self[at, columns] = dot(low[at, :], w_att[:, columns]).astype(HALF)

        repeat(3 * width // 256, project)
        make_mask(v.segments, v.segments, row, encoder)
        attend(qkv_self, self_probs, mix_self, row, True)
        transpose_back(low, mix_self, row)
        add_projection(w_out, x_send, row)

        @pl.when(encoder)
        def _():
            enter_feed_forward(row)
            feed_forward(row, True, False, None, 0, None, True)
            normalise(as_full(res), row, 2, final_gain, unit_mid, x_send)
            memory_copy(row).start()
            write_layer(row).start()

    repeat(rows, forward_row)

    def decoder_row(row):
        at = row_slice(row)
        normalise(as_full(res), row, 2, cross_gain, unit_mid, low)
        for j in range(width // 256):
            n = slice(j * 256, (j + 1) * 256)
            qkv_cross[at, n] = dot(low[at, :], w_att[:, n]).astype(HALF)
        make_mask(v.enc_segments, v.dec_segments, row, None)
        memory_copy(row).wait_recv()

        def project_memory(j):
            columns = pl.ds(pl.multiple_of(width + j * 256, 128), 256)
            qkv_cross[at, columns] = dot(x_recv[at, :], w_att[:, columns]).astype(HALF)

        repeat(2 * width // 256, project_memory)
        attend(qkv_cross, cross_probs, mix_cross, row, False)
        transpose_back(low, mix_cross, row)
        add_projection(w_out, res, row)
        enter_feed_forward(row)
        feed_forward(row, True, True, grad, H, decoder_unit, row + 1 < rows)
        x_send[at, :] = res[at, :].astype(HALF)
        write_layer(row).start()
        norm_back(as_full(grad), as_full(unit_ffn), row, 1, ffn_gain, 1, as_full(cot), low)
        back_through_out(row)
        attend_back(qkv_cross, cross_probs, row, False, None)
        write_layer(row).wait()
        for j in range(width // 256):
            n = slice(j * 256, (j + 1) * 256)
            x_send[at, n] = dot_outer(
                qkv_cross[at, width : 3 * width], w_att[n, width : 3 * width]
            ).astype(HALF)
        memory_back(row).start()
        for j in range(width // 256):
            n = slice(j * 256, (j + 1) * 256)
            res[at, n] = dot_outer(qkv_cross[at, :width], w_att[n, :width])

    def load_x_again():
        return copy_in(v.inputs, qkv_cross.at[:, pl.ds(0, width)], 0)

    @pl.when(encoder)
    def _():
        load_x_again().start()

    @pl.when(decoder)
    def _():
        for copy in load_cross():
            copy.start()
        load_cross_out().start()
        for copy in load_cross():
            copy.wait()
        load_cross_out().wait()
        repeat(rows, decoder_row)
        load_att().start()
        load_out().start()
        weight_gradient(CROSS, 0, mix_cross, low, 0)

        def gained(b):
            at = pl.ds(at128(b, 128), 128)
            low_t[:, at] = (unit_mid[at, :].astype(FULL) * cross_gain).astype(HALF).T

        repeat(tokens // 128, gained)
        weight_gradient(CROSS, 1, low_t, qkv_cross, 0)
        for row in range(rows):
            transpose_rows(low_t, x_recv, row)
        weight_gradient(CROSS, 2, low_t, qkv_cross, width)
        weight_gradient(CROSS, 3, low_t, qkv_cross, 2 * width)
        load_x_again().start()
        for row in range(rows):
            norm_back(as_full(res), as_full(unit_mid), row, 2, cross_gain, 2, as_full(grad), low)
        for item in range(4):
            add_first(CROSS, item)
        load_att().wait()
        load_out().wait()

    load_x_again().wait()

    def unit_self(at):
        return qkv_cross[at, :width].astype(FULL) * inverse[at, 0:1]

    def backward_row(row):
        at = row_slice(row)

        @pl.when(encoder)
        def _():
            memory_back(row).wait_recv()

            def memory_grads(at):
                return cot[at, :].astype(FULL) + x_recv[at, :].astype(FULL)

            norm_back(memory_grads, as_full(unit_mid), row, 2, final_gain, 2, None, cot)
            feed_forward(row, False, True, res, 0, encoder_unit, row + 1 < rows)
            norm_back(as_full(res), as_full(unit_ffn), row, 1, ffn_gain, 1, as_full(grad), low)

        def tick(hp):
            @pl.when(jnp.where(encoder, row == rows - 1, row == 0))
            def _():
                add_second(GATE_UP, hp)

            @pl.when(decoder & (row == rows - 1) & (hp < 2))
            def _():
                add_second(GATE_UP, PAIRS + hp)

        back_through_out(row)
        attend_back(qkv_self, self_probs, row, True, tick)
        for j in range(width // 256):
            n = slice(j * 256, (j + 1) * 256)
            res[at, n] = dot_outer(qkv_self[at, :], w_att[n, :])
        norm_back(as_full(res), unit_self, row, 0, attn_gain, 0, as_full(grad), None)

    repeat(rows, backward_row)
    write_grad = pltpu.make_async_copy(grad, v.grad_inputs, sem_out.at[1])
    write_grad.start()
    weight_gradient(SELF, 0, mix_self, low, 0)

    def gained_self(b):
        at = pl.ds(at128(b, 128), 128)
        low_t[:, at] = (unit_self(at) * attn_gain).astype(HALF).T

    repeat(tokens // 128, gained_self)
    for item in range(1, 4):
        weight_gradient(SELF, item, low_t, qkv_self, (item - 1) * width)
    for item in range(4):
        add_first(SELF, item)
    misc[0, 0:H, width : width + NBUCKET] = lax.dot_general(
        sums[0:H, :],
        v.summed[section].astype(FULL),
        (((1,), (1,)), ((), ())),
        precision=PRECISE,
        preferred_element_type=FULL,
    )

    def misc_copy(source, target, slot, to):
        return pltpu.make_async_remote_copy(
            misc.at[source],
            misc.at[target],
            sem_misc.at[slot, 0],
            sem_misc.at[slot, 1],
            device_id=to,
            device_id_type=MESH,
        )

    def misc_out(source, place, slot):
        return pltpu.make_async_copy(misc.at[source], v.out_misc.at[place], sem_out.at[slot])

    if reduce:
        first = misc_copy(0, 1, 0, sibling)
        first.start()
        first.wait_recv()
        misc[2] = misc[0] + misc[1]
        second = misc_copy(2, 3, 1, beside)
        second.start()

    def drain(name, done=0):
        count = by_name[name].count

        def step(i):
            @pl.when(i >= done)
            def _():
                add_second(name, i)

            @pl.when(i >= 2)
            def _():
                add_third(name, i - 2)

        repeat(count, step)
        for i in range(max(count - 2, 0), count):
            add_third(name, i)

    drain(GATE_UP, jnp.where(encoder, PAIRS, by_name[GATE_UP].count))
    drain(DOWN)

    @pl.when(decoder)
    def _():
        drain(CROSS)

    if reduce:
        second.wait_recv()
        misc[4 + z] = misc[2] + misc[3]
        thirds = [misc_copy(4 + z, 4 + z, 2 + d, device(peer_z[d], y, c)) for d in range(3)]
        for copy in thirds:
            copy.start()
    drain(SELF)
    if reduce:
        for d in range(3):
            came = misc_copy(4 + z, 4 + (z + 3 - d) % 4, 2 + d, device(peer_z[d], y, c))
            came.wait_recv()
        misc[8] = (misc[4] + misc[5]) + (misc[6] + misc[7])
        across = misc_copy(8, 9, 5, other)
        across.start()
        across.wait_recv()
        outs = [misc_out(8, section, 2), misc_out(9, 1 - section, 3)]
    else:
        outs = [misc_out(0, 0, 2)]
    for copy in outs:
        copy.start()
    for name in (GATE_UP, DOWN, SELF):
        repeat(by_name[name].count, functools.partial(finish, name))

    @pl.when(decoder)
    def _():
        repeat(by_name[CROSS].count, functools.partial(finish, CROSS))

    if reduce:

        @pl.when(encoder)
        def _():
            repeat(by_name[CROSS].count, lambda i: cross_over(i).wait_recv())

        for copy in [first, second, across] + thirds:
            copy.wait_send()
    for copy in outs:
        copy.wait()
    write_grad.wait()

    @pl.when(encoder)
    def _():
        for row in range(rows):
            memory_copy(row).wait_send()
            write_layer(row).wait()

    @pl.when(decoder)
    def _():
        for row in range(rows):
            memory_back(row).wait_send()


def run_layers(args, ways):
    (
        inputs,
        cotangent,
        enc_segments,
        dec_segments,
        rel_bias,
        attn_norm,
        ffn_norm,
        w_qkv,
        w_attn_out,
        w_gate_up,
        w_down,
        cross_norm,
        cross_query,
        cross_kv,
        cross_out,
        final_norm,
    ) = args
    _, rows, length, width = inputs.shape
    hidden = w_down.shape[1]
    tokens = rows * length
    reduce = ways == 16
    spread, summed = bucket_tables(length)
    operands = dict(
        inputs=inputs.reshape(tokens, width),
        cotangent=cotangent.reshape(tokens, width),
        w_qkv=w_qkv,
        w_attn_out=w_attn_out,
        w_gate_up=w_gate_up,
        w_down=w_down,
        cross_query=cross_query,
        cross_kv=cross_kv,
        cross_out=cross_out,
    )
    small = dict(
        enc_segments=enc_segments,
        dec_segments=dec_segments,
        rel_bias=rel_bias,
        attn_norm=attn_norm,
        ffn_norm=ffn_norm,
        cross_norm=cross_norm.reshape(1, width),
        final_norm=final_norm.reshape(1, width),
        spread=jnp.asarray(spread, HALF),
        summed=jnp.asarray(summed, HALF),
    )
    block = width // 16
    groups = [
        Group(GATE_UP, hidden // CHUNK, block, 2 * CHUNK),
        Group(DOWN, 3, hidden // 16, 256),
        Group(CROSS, 4, block, width),
        Group(SELF, 4, block, width),
    ]
    outs = dict(
        layer_out=((tokens, width), HALF),
        grad_inputs=((tokens, width), FULL),
    )
    for g in groups:
        outs[f"out{g.name}"] = ((g.count, g.rows if reduce else 16 * g.rows, g.cols), HALF)
    outs[MISC] = ((2 if reduce else 1, 16, width + 128), FULL)
    scratch = dict(
        x_send=pltpu.VMEM((tokens, width), HALF),
        x_recv=pltpu.VMEM((tokens, width), HALF),
        low=pltpu.VMEM((tokens, width), HALF),
        low_t=pltpu.VMEM((width, tokens), HALF),
        unit_ffn=pltpu.VMEM((tokens, width), HALF),
        unit_mid=pltpu.VMEM((tokens, width), HALF),
        cot=pltpu.VMEM((tokens, width), HALF),
        res=pltpu.VMEM((tokens, width), FULL),
        grad=pltpu.VMEM((tokens, width), FULL),
        w_att=pltpu.VMEM((width, 3 * width), HALF),
        w_out=pltpu.VMEM((width, width), HALF),
        w_pair=pltpu.VMEM((2, width, 2 * CHUNK), HALF),
        w_lower=pltpu.VMEM((2, CHUNK, width), HALF),
        qkv_self=pltpu.VMEM((tokens, 3 * width), HALF),
        qkv_cross=pltpu.VMEM((tokens, 3 * width), HALF),
        mix_self=pltpu.VMEM((width, tokens), HALF),
        mix_cross=pltpu.VMEM((width, tokens), HALF),
        probs=pltpu.VMEM((H * rows, length, length), HALF),
        big=pltpu.VMEM((4, width, width), HALF),
        inverse=pltpu.VMEM((tokens, 8), FULL),
        mask=pltpu.VMEM((length, length), HALF),
        near=pltpu.VMEM((length, length), HALF),
        past=pltpu.VMEM((length, length), HALF),
        flip=pltpu.VMEM((length, length), HALF),
        grad_mix=pltpu.VMEM((length, width), HALF),
        segments=pltpu.VMEM((8, length), jnp.int32),
        table=pltpu.VMEM((16, 2 * length), FULL),
        sums=pltpu.VMEM((16, 2 * length), FULL),
        misc=pltpu.VMEM((10 if reduce else 1, 16, width + 128), FULL),
        load=pltpu.SemaphoreType.DMA((11,)),
        sem_x=pltpu.SemaphoreType.DMA((4, rows)),
        sem_misc=pltpu.SemaphoreType.DMA((6, 2)),
        sem_out=pltpu.SemaphoreType.DMA((4 + rows,)),
    )
    for g in groups:
        if g.name != SELF:
            scratch[f"own{g.name}"] = pltpu.VMEM((g.count, 16 * g.rows, g.cols), HALF)
        if reduce:
            scratch[f"first{g.name}"] = pltpu.VMEM((g.count, 8 * g.rows, g.cols), HALF)
            scratch[f"second{g.name}"] = pltpu.VMEM((g.count, 4 * g.rows, g.cols), HALF)
            scratch[f"third{g.name}"] = pltpu.VMEM((g.count, 3, g.rows, g.cols), HALF)
        scratch[f"sem{g.name}"] = pltpu.SemaphoreType.DMA((g.count, 13))
    names = list(operands) + list(small) + list(outs) + list(scratch)
    results = pl.pallas_call(
        functools.partial(layer_kernel, names, groups, reduce, rows, length, width, hidden),
        out_shape=[jax.ShapeDtypeStruct(*out) for out in outs.values()],
        in_specs=[pl.BlockSpec(memory_space=pl.ANY)] * len(operands)
        + [pl.BlockSpec(memory_space=pltpu.VMEM)] * len(small),
        out_specs=[pl.BlockSpec(memory_space=pl.ANY)] * len(outs),
        scratch_shapes=list(scratch.values()),
        compiler_params=pltpu.CompilerParams(
            collective_id=1, has_side_effects=True, vmem_limit_bytes=VMEM_LIMIT
        ),
    )(*operands.values(), *small.values())
    return dict(zip(outs, results)), reduce


LAYER, INPUT, MISC = "layer_out", "grad_inputs", "out_misc"
VMEM_LIMIT = 64 * 2**20 - 64 * 2**10


def shards(*args):
    inputs, rel_bias = args[0], args[4]
    ways = lax.axis_size("dp")
    _, rows, length, width = inputs.shape
    hidden = args[10].shape[1]
    out, reduce = run_layers(args, ways)

    def wide(name):
        value = out[f"out{name}"]
        if reduce:
            return value.astype(FULL)
        total = lax.psum_scatter(value, "dp", scatter_dimension=1, tiled=True)
        if name == CROSS:
            total = lax.psum(jnp.where(lax.axis_index("section") == 1, total, 0), "section")
        return total.astype(FULL)

    def side_by_side(value):
        return jnp.swapaxes(value, 0, 1).reshape(value.shape[1], -1)

    gate_up = wide(GATE_UP)
    chunks, block, _ = gate_up.shape
    gate_up = gate_up.reshape(chunks, block, 2, CHUNK).transpose(1, 2, 0, 3).reshape(block, 2 * hidden)
    down, cross, late = wide(DOWN), wide(CROSS), wide(SELF)
    misc = out[MISC]
    section = lax.axis_index("section")
    if not reduce:
        mine = lax.psum(misc[0], "dp")
        misc = lax.all_gather(mine, "section", axis=0)
    own = lax.dynamic_index_in_dim(misc, section, 0, keepdims=False)
    start = lax.axis_index("dp") * block

    def piece(vector):
        return lax.dynamic_slice_in_dim(vector, start, block, 0)

    rel = (misc[0] + misc[1])[:H, width : width + NBUCKET].T
    return (
        out[LAYER].reshape(inputs.shape),
        out[INPUT].reshape(inputs.shape),
        side_by_side(late[1:])[None],
        late[0][None],
        gate_up[None],
        side_by_side(down)[None],
        piece(own[0, :width])[None],
        piece(own[1, :width])[None],
        cross[1],
        side_by_side(cross[2:]),
        cross[0],
        piece(misc[1, 2, :width]),
        piece(misc[0, 2, :width]),
        rel,
    )


def solution(mesh):
    layer = P("section", "dp", None, None)
    matrix = P("section", None, None)
    return jax.shard_map(
        shards,
        mesh=mesh,
        in_specs=(layer, layer, P("dp", None), P("dp", None), P())
        + (P("section", None),) * 2
        + (matrix,) * 4
        + (P(),) * 5,
        out_specs=(layer, layer)
        + (P("section", "dp", None),) * 4
        + (P("section", "dp"),) * 2
        + (P("dp", None),) * 3
        + (P("dp"),) * 2
        + (P(),),
        check_vma=False,
    )
```

```python
import functools
import math
import types

import jax
import jax.numpy as jnp
import numpy as np
from jax import lax
from jax.experimental import pallas as pl
from jax.experimental.pallas import tpu as pltpu
from jax.sharding import PartitionSpec as P

H = 12
HD = 64
NBUCKET = 32
MAXDIST = 128
EPSILON = 1e-06
MASKED = -1000000000.0
MESH = pl.DeviceIdType.MESH
PRECISE = lax.Precision.HIGHEST
HALF = jnp.bfloat16
FULL = jnp.float32
PAIRS = H // 2
CHUNK = 256
BLOCK = 64
UNROLL = 2
RING = 4
GATE_UP, DOWN, CROSS, SELF, SMALL = range(5)
GELU_SCALE = math.sqrt(2.0 / math.pi)
GELU_CUBE = 0.044715


def bucket_of(offsets, causal, buckets, reach_max):
    if causal:
        half_count = buckets
        side_offset = offsets * 0
        distance = np.maximum(-offsets, 0)
    else:
        half_count = buckets // 2
        side_offset = (offsets > 0).astype(np.int32) * half_count
        distance = np.abs(offsets)
    exact_count = half_count // 2
    clipped = np.maximum(distance, exact_count)
    spread = exact_count + np.floor(
        np.log(clipped / exact_count) / np.log(reach_max / exact_count) * (half_count - exact_count)
        + 1e-09
    ).astype(np.int32)
    spread = np.minimum(spread, half_count - 1)
    return (side_offset + np.where(distance < exact_count, distance, spread)).astype(np.int32)


def bucket_tables(length):
    lane = np.arange(length)
    spread = np.concatenate([-lane, length - lane])
    summed = np.concatenate([-(lane + 1), length - 1 - lane])
    tables = []
    for offsets in (spread, summed):
        clipped = np.clip(offsets, -(length - 1), length - 1)
        tables.append(
            np.stack(
                [
                    (bucket_of(clipped, causal, NBUCKET, MAXDIST)[None] == np.arange(NBUCKET)[:, None])
                    for causal in (False, True)
                ]
            ).astype(np.float32)
        )
    return tables


def dot(left, right):
    return jnp.dot(left, right, preferred_element_type=FULL)


def dot_outer(left, right):
    return lax.dot_general(left, right, (((1,), (1,)), ((), ())), preferred_element_type=FULL)


def repeat(count, step):
    def body(index, carry):
        step(index)
        return carry

    lax.fori_loop(0, count, body, 0)


def at128(index, scale):
    return pl.multiple_of(index * scale, 128)


class Group:
    def __init__(self, name, count, rows, cols):
        self.name, self.count, self.rows, self.cols = name, count, rows, cols


def layer_kernel(names, groups, reduce, rows, length, width, hidden, *refs):
    v = types.SimpleNamespace(**dict(zip(names, refs)))
    tokens = rows * length
    chunks = hidden // CHUNK
    ways_rows = width // 16
    me, section = lax.axis_index("dp"), lax.axis_index("section")
    encoder, decoder = section == 0, section == 1
    z, y, c = me // 4, (me // 2) % 2, me % 2
    other = (1 - section, me)

    x_send, x_recv = v.x_send, v.x_recv
    low, low_t, grad_mix = v.low, v.low_t, v.grad_mix
    joint, units = grad_mix.at[:, : 2 * CHUNK], grad_mix.at[:, 2 * CHUNK : 3 * CHUNK]
    unit_ffn, unit_mid, cot = v.unit_ffn, v.unit_mid, v.cot
    res, grad = v.res, v.grad
    w_att, w_out = v.w_att, v.w_out
    qkv_self, qkv_cross = v.qkv_self, v.qkv_cross
    mix_self, mix_cross = v.mix_self, v.mix_cross
    probs, big = v.probs, v.big
    inverse, table, sums, mask = v.inverse, v.table, v.sums, v.mask
    misc = v.misc
    load, sem_x, sem_out = v.load, v.sem_x, v.sem_out

    def device(zz, yy, cc):
        return (section, zz * 4 + yy * 2 + cc)

    z_low, z_high = z % 2, z // 2
    near_y, near_z = device(z, 1 - y, c), device(z + 1 - 2 * z_low, y, c)
    sibling, far_z = device(z, y, 1 - c), device(z + 2 - 4 * z_high, y, c)
    partners = [other] + ([sibling, near_y, near_z, far_z] if reduce else [])
    barrier = pltpu.get_barrier_semaphore()
    for target in partners:
        pl.semaphore_signal(barrier, inc=1, device_id=target, device_id_type=MESH)

    def copy_in(source, target, slot):
        return pltpu.make_async_copy(source, target, load.at[slot])

    def load_x():
        return copy_in(v.inputs, x_send, 0)

    def load_cot():
        return copy_in(v.cotangent, cot, 1)

    def load_att():
        return copy_in(v.w_qkv.at[0], w_att, 2)

    def load_out():
        return copy_in(v.w_attn_out.at[0], w_out, 3)

    def load_cross():
        return [
            copy_in(v.cross_query, w_att.at[:, pl.ds(0, width)], 2),
            copy_in(v.cross_kv, w_att.at[:, pl.ds(width, 2 * width)], 4),
        ]

    def load_cross_out():
        return copy_in(v.cross_out, w_out, 3)

    ring = v.own2

    def load_chunk(index):
        slot = index % RING
        at = at128(index, CHUNK)
        pieces = [
            copy_in(
                v.w_down.at[0, pl.ds(at, CHUNK), pl.ds(j * 256, 256)],
                ring.at[slot, pl.ds(j * 256, 256), pl.ds(2 * CHUNK, 256)],
                7 + j + 5 * slot,
            )
            for j in range(width // 256)
        ]
        return pieces + [
            copy_in(
                v.w_gate_up.at[0, :, pl.ds(at, CHUNK)], ring.at[slot, :, pl.ds(0, CHUNK)], 5 + 5 * slot
            ),
            copy_in(
                v.w_gate_up.at[0, :, pl.ds(pl.multiple_of(hidden + at, 128), CHUNK)],
                ring.at[slot, :, pl.ds(CHUNK, CHUNK)],
                6 + 5 * slot,
            ),
        ]

    load_x().start()
    load_att().start()
    load_out().start()
    load_cot().start()
    misc[...] = jnp.zeros_like(misc)
    sums[...] = jnp.zeros_like(sums)
    for k in range(RING - 1):
        for copy in load_chunk(k):
            copy.start()

    by_name = {group.name: group for group in groups}
    stacks = {
        group.name: (big if group.name == SELF else getattr(v, f"own{group.name}")) for group in groups
    }

    def block_place(zz, yy, cc):
        return cc * 8 + yy * 4 + (zz % 2) * 2 + zz // 2

    def put(name, item, columns, tile):
        own, r = stacks[name], by_name[name].rows
        low_tile = tile.astype(HALF)
        for shard in range(16):
            place = shard
            if reduce:
                place = block_place(shard // 4, (shard // 2) % 2, shard % 2)
            own[item, place * r : (place + 1) * r, columns] = low_tile[
                shard * r : (shard + 1) * r
            ]

    def stages(name):
        result, base, count = [], 0, 16 * by_name[name].rows
        for bit, target in ((c, sibling), (y, near_y), (z_low, near_z), (z_high, far_z)):
            count = count // 2
            sent, base = base + (1 - bit) * count, base + bit * count
            result.append((target, pl.multiple_of(sent, 16), pl.multiple_of(base, 16), count))
        return result

    def exchange(name, i, stage):
        target, sent, _, count = stages(name)[stage]
        sems = getattr(v, f"sem{name}")
        return pltpu.make_async_remote_copy(
            stacks[name].at[i, pl.ds(sent, count)],
            getattr(v, f"came{stage}x{name}").at[i],
            sems.at[i, 2 * stage],
            sems.at[i, 2 * stage + 1],
            device_id=target,
            device_id_type=MESH,
        )

    def kept_rows(name):
        _, _, kept, count = stages(name)[3]
        return pl.ds(kept, count)

    def write_out(name, i):
        source = stacks[name].at[i, kept_rows(name)] if reduce else stacks[name].at[i]
        place = section if name == SMALL else i
        return pltpu.make_async_copy(
            source, getattr(v, f"out{name}").at[place], getattr(v, f"sem{name}").at[i, 8]
        )

    def cross_over(name, i, place):
        sems = getattr(v, f"sem{name}")
        return pltpu.make_async_remote_copy(
            stacks[name].at[i, kept_rows(name)],
            getattr(v, f"out{name}").at[place],
            sems.at[i, 9],
            sems.at[i, 10],
            device_id=other,
            device_id_type=MESH,
        )

    def begin(name, i):
        if reduce:
            exchange(name, i, 0).start()
        else:
            write_out(name, i).start()

    def add(name, i, stage):
        if not reduce:
            return
        own, came = stacks[name], getattr(v, f"came{stage}x{name}")
        exchange(name, i, stage).wait_recv()
        _, _, kept, count = stages(name)[stage]
        size = min(count, 2 * by_name[name].rows)

        def step(m):
            at = pl.ds(pl.multiple_of(kept + m * size, 16), size)
            own[i, at] = own[i, at] + came[i, pl.ds(pl.multiple_of(m * size, 16), size)]

        repeat(count // size, step)
        if stage < 3:
            exchange(name, i, stage + 1).start()
        else:
            write_out(name, i).start()
            if name == CROSS:
                cross_over(name, i, i).start()
            if name == SMALL:
                cross_over(name, i, section).start()

    def add_first(name, i):
        add(name, i, 0)

    def finish(name, i):
        write_out(name, i).wait()
        if reduce:
            for stage in range(4):
                exchange(name, i, stage).wait_send()
            if name in (CROSS, SMALL):
                cross_over(name, i, i).wait_send()

    def block_of(ref, b):
        return ref.at[b // 9, pl.ds(at128((b % 9) // 3, 256), 256), pl.ds(at128(b % 3, 256), 256)]

    def decoder_unit(k):
        return block_of(big, H + 2 * chunks + k)

    def encoder_unit(k):
        lanes = pl.ds(pl.multiple_of(width + k // 2 * CHUNK, 128), CHUNK)
        return qkv_cross.at[pl.ds(at128(k % 2, length), length), lanes]

    def self_probs(head, row):
        return probs.at[head * rows + row]

    def cross_probs(head, row):
        return block_of(big, head)

    def row_slice(row):
        return pl.ds(pl.multiple_of(row * length, length), length)

    def part_slice(row, b, size):
        return pl.ds(pl.multiple_of(row * length + b * size, size), size)

    lanes = lax.broadcasted_iota(jnp.int32, (1, 128), 1)
    half_lanes = [(lanes < HD).astype(HALF), (lanes >= HD).astype(HALF)]

    def make_mask(key_segments, query_segments, row, causal):
        keys = key_segments[pl.ds(row, 1), :].astype(FULL)
        keys = jnp.broadcast_to(keys, (8, length)).T[:, :1]
        queries = query_segments[pl.ds(row, 1), :].astype(FULL)
        same = keys == queries
        if causal is not None:
            key_at = lax.broadcasted_iota(jnp.int32, (length, length), 0)
            query_at = lax.broadcasted_iota(jnp.int32, (length, length), 1)
            same = same & ((key_at <= query_at) | causal)
        mask[...] = jnp.where(same, 0.0, MASKED).astype(HALF)

    def lanes_of(offset, hp):
        return pl.ds(pl.multiple_of(offset + hp * 128, 128), 128)

    def attend(qkv, probs_of, mix, row, with_bias):
        at = row_slice(row)

        def pair(hp):
            queries = qkv[at, lanes_of(0, hp)]
            keys = qkv[at, lanes_of(width, hp)]
            values_t = qkv[at, lanes_of(2 * width, hp)].T
            both = jnp.concatenate([keys * half_lanes[0], keys * half_lanes[1]], 0)
            scores = dot_outer(both, queries)
            for e in range(2):
                if with_bias:
                    line = table[pl.ds(hp * 2 + e, 1), :]
                    skewed = line[:, length:] + v.near[...].astype(FULL) * (line[:, :length] - line[:, length:])
                    bias = pltpu.roll(skewed, 0, 1, stride=1, stride_axis=0)
                soft_parts = []
                for part in range(length // 128):
                    n = slice(part * 128, (part + 1) * 128)
                    shifted = scores[e * length : (e + 1) * length, n] + mask[:, n].astype(FULL)
                    if with_bias:
                        shifted = shifted + bias[:, n]
                    raised = jnp.exp(shifted - jnp.max(shifted, 0, keepdims=True))
                    total = jnp.sum(raised, 0, keepdims=True)
                    soft_parts.append((raised * (1.0 / total)).astype(HALF))
                softmaxed = jnp.concatenate(soft_parts, 1)
                probs_of(hp * 2 + e, row)[...] = softmaxed
                mixed = dot(values_t[e * HD : (e + 1) * HD], softmaxed)
                mix[pl.ds(pl.multiple_of(hp * 128 + e * HD, 16), HD), at] = mixed.astype(HALF)

        repeat_pairs(pair)

    def repeat_pairs(pair):
        def step(g):
            for u in range(UNROLL):
                pair(g * UNROLL + u)

        repeat(PAIRS // UNROLL, step)

    def attend_back(qkv, probs_of, row, with_bias, tick):
        at = row_slice(row)
        left = lax.broadcasted_iota(jnp.int32, (length, 128), 1) < HD
        def pair(hp):
            q_lanes, k_lanes, v_lanes = lanes_of(0, hp), lanes_of(width, hp), lanes_of(2 * width, hp)
            queries, keys, values = qkv[at, q_lanes], qkv[at, k_lanes], qkv[at, v_lanes]
            outer = grad_mix[:, q_lanes]
            keys_t = keys.T
            both = jnp.concatenate([values * half_lanes[0], values * half_lanes[1]], 0)
            grad_soft = dot_outer(both, outer)
            softs, scores = [], []
            for e in range(2):
                soft_low = probs_of(hp * 2 + e, row)[...]
                score_parts = []
                for part in range(length // 128):
                    n = slice(part * 128, (part + 1) * 128)
                    soft = soft_low[:, n].astype(FULL)
                    weighted = soft * grad_soft[e * length : (e + 1) * length, n]
                    shared = jnp.sum(weighted, 0, keepdims=True)
                    score_parts.append((weighted - soft * shared).astype(HALF))
                scores.append(jnp.concatenate(score_parts, 1))
                softs.append(soft_low)
            grad_keys = dot(jnp.concatenate(scores, 0), queries)
            grad_values = dot(jnp.concatenate(softs, 0), outer)
            left_side = jnp.concatenate([keys_t, v.flip[...]], 0) if with_bias else keys_t
            parts = []
            for e in range(2):
                product = dot(left_side, scores[e])
                parts.append(product[e * HD : (e + 1) * HD])
                if with_bias:
                    aligned = pltpu.roll(product[128:], 0, 1, stride=1, stride_axis=0)
                    before = jnp.sum(aligned * v.past[...].astype(FULL), 0, keepdims=True)
                    after = jnp.sum(aligned, 0, keepdims=True) - before
                    line = pl.ds(hp * 2 + e, 1)
                    sums[line, :] = sums[line, :] + jnp.concatenate([before, after], 1)
            qkv[at, q_lanes] = jnp.concatenate(parts, 0).T.astype(HALF)
            qkv[at, k_lanes] = jnp.where(left, grad_keys[:length], grad_keys[length:]).astype(HALF)
            qkv[at, v_lanes] = jnp.where(left, grad_values[:length], grad_values[length:]).astype(HALF)
            if tick is not None:
                tick(hp)

        repeat_pairs(pair)

    def normalise(load_rows, row, column, gain, unit_ref, target):
        for b in range(length // BLOCK):
            at = part_slice(row, b, BLOCK)
            value = load_rows(at)
            scale = lax.rsqrt(jnp.mean(value * value, -1, keepdims=True) + EPSILON)
            inverse[at, column : column + 1] = scale
            unit = value * scale
            if unit_ref is not None:
                unit_ref[at, :] = unit.astype(HALF)
            target[at, :] = (unit * gain).astype(HALF)

    def norm_back(load_grad, load_unit, row, column, gain, misc_row, load_base, low_ref):
        def step(b, gain_sum):
            at = part_slice(row, b, BLOCK)
            normed, unit = load_grad(at), load_unit(at)
            weighted = normed * unit
            grad_unit = normed * gain
            scale = inverse[at, column : column + 1]
            inner = jnp.mean(weighted * gain, -1, keepdims=True)
            result = scale * (grad_unit - unit * inner)
            if load_base is not None:
                result = result + load_base(at)
            grad[at, :] = result
            if low_ref is not None:
                low_ref[at, :] = result.astype(HALF)
            return gain_sum + jnp.sum(weighted.reshape(BLOCK // 8, 8, width), 0)

        gain_sum = lax.fori_loop(0, length // BLOCK, step, jnp.zeros((8, width), FULL))
        line = slice(misc_row, misc_row + 1)
        misc[line, :width] = misc[line, :width] + jnp.sum(gain_sum, 0, keepdims=True)

    def transpose_rows(target, source, row):
        for b in range(length // 128):
            at = part_slice(row, b, 128)
            target[:, at] = source[at, :].T

    def transpose_back(target, source, row):
        for b in range(length // 128):
            at = part_slice(row, b, 128)
            target[at, :] = source[:, at].T

    def add_projection(weights, base, row):
        at = row_slice(row)
        for j in range(width // 256):
            n = slice(j * 256, (j + 1) * 256)
            res[at, n] = base[at, n].astype(FULL) + dot(low[at, :], weights[:, n])

    def feed_forward(row, forward, backward, total, base, unit_block, more):
        at = row_slice(row)
        if backward:
            total[at, :] = jnp.zeros((length, width), FULL)

        def step(k):
            slot = k % RING
            pair_weights = ring.at[slot, :, : 2 * CHUNK]
            lower = [ring.at[slot, j * 256 : (j + 1) * 256, 2 * CHUNK :] for j in range(width // 256)]

            @pl.when((k + RING - 1 < chunks) | more)
            def _():
                for copy in load_chunk((k + RING - 1) % chunks):
                    copy.start()

            for copy in load_chunk(k):
                copy.wait()
            kept = [block_of(big, row * 2 * chunks + k * 2 + side) for side in range(2)]
            if forward:
                joined = dot(low[at, :], pair_weights[...])
                gate, up = joined[:, :CHUNK], joined[:, CHUNK:]
                if not backward:
                    kept[0][...] = gate.astype(HALF)
                    kept[1][...] = up.astype(HALF)
            else:
                gate, up = kept[0][...].astype(FULL), kept[1][...].astype(FULL)
            squared = gate * gate
            curve = jnp.tanh(gate * (GELU_SCALE + GELU_SCALE * GELU_CUBE * squared))
            rising = 0.5 + 0.5 * curve
            bent = gate * rising
            unit = (bent * up).astype(HALF)
            if forward:
                for j in range(width // 256):
                    n = slice(j * 256, (j + 1) * 256)
                    res[at, n] = res[at, n] + dot(unit, lower[j][...])
            if not backward:
                return
            grad_hidden = sum(
                dot_outer(cot[at, j * 256 : (j + 1) * 256], lower[j][...]) for j in range(width // 256)
            )
            slope = rising + 0.5 * gate * (1.0 - curve * curve) * (
                GELU_SCALE + 3.0 * GELU_SCALE * GELU_CUBE * squared
            )
            pair = jnp.concatenate(
                [(grad_hidden * up * slope).astype(HALF), (grad_hidden * bent).astype(HALF)], 1
            )
            total[at, :] = total[at, :] + dot_outer(pair, pair_weights[...])
            joint[...] = pair
            units[...] = unit.T
            first = [block_of(big, base + k * 2 + side) for side in range(2)]

            @pl.when(row == 0)
            def _():
                first[0][...] = joint[:, :CHUNK]
                first[1][...] = joint[:, CHUNK:]
                unit_block(k)[...] = units[...]

            @pl.when(row == rows - 1)
            def _():
                for part in range(2):
                    columns = slice(part * CHUNK, (part + 1) * CHUNK)
                    right = jnp.concatenate([first[part][...], joint[:, columns]], 0)
                    put(GATE_UP, k, columns, dot(low_t[...], right))
                begin(GATE_UP, k)
                r = by_name[DOWN].rows
                both = jnp.concatenate([unit_block(k)[...], units[...]], 1)
                for part in range(3):
                    tile = dot(both, cot[:, part * 256 : (part + 1) * 256]).astype(HALF)
                    if reduce:
                        for shard in range(CHUNK // r):
                            place = block_place(k // 2, k % 2, shard)
                            v.own1[part, pl.ds(pl.multiple_of(place * r, 16), r)] = tile[
                                shard * r : (shard + 1) * r
                            ]
                    else:
                        v.own1[part, pl.ds(at128(k, CHUNK), CHUNK)] = tile

                @pl.when(k > 0)
                def _():
                    add_first(GATE_UP, k - 1)

        repeat(chunks, step)
        if backward:

            @pl.when(row == rows - 1)
            def _():
                for part in range(3):
                    begin(DOWN, part)
                add_first(GATE_UP, chunks - 1)
                for part in range(3):
                    add_first(DOWN, part)

    def weight_gradient(name, item, left_t, right, at):
        def step(j):
            tile = dot(left_t[...], right[:, pl.ds(pl.multiple_of(at + j * 256, 128), 256)])
            put(name, item, pl.ds(at128(j, 256), 256), tile)

        repeat(width // 256, step)
        begin(name, item)

    def back_through_out(row):
        for j in range(width // 256):
            n = slice(j * 256, (j + 1) * 256)
            grad_mix[:, n] = dot_outer(low[row_slice(row), :], w_out[n, :]).astype(HALF)

    def as_full(ref):
        return lambda at: ref[at, :].astype(FULL)

    def memory_copy(row):
        return pltpu.make_async_remote_copy(
            x_send.at[row_slice(row)],
            x_recv.at[row_slice(row)],
            sem_x.at[0, row],
            sem_x.at[1, row],
            device_id=other,
            device_id_type=MESH,
        )

    def memory_back(row):
        return pltpu.make_async_remote_copy(
            x_send.at[row_slice(row)],
            x_recv.at[row_slice(row)],
            sem_x.at[2, row],
            sem_x.at[3, row],
            device_id=other,
            device_id_type=MESH,
        )

    def write_layer(row):
        return pltpu.make_async_copy(
            x_send.at[row_slice(row)], v.layer_out.at[row_slice(row)], sem_out.at[4 + row]
        )

    ffn_gain = v.ffn_norm[...].astype(FULL)
    attn_gain = v.attn_norm[...].astype(FULL)
    cross_gain = v.mid_norms[...].astype(FULL)[0:1]
    final_gain = v.mid_norms[...].astype(FULL)[1:2]

    def enter_feed_forward(row):
        normalise(as_full(res), row, 1, ffn_gain, unit_ffn, low)
        transpose_rows(low_t, low, row)

    row_at = lax.broadcasted_iota(jnp.int32, (length, length), 0)
    lane_at = lax.broadcasted_iota(jnp.int32, (length, length), 1)
    v.near[...] = (lane_at + row_at < length).astype(FULL).astype(HALF)
    v.past[...] = (lane_at < row_at).astype(FULL).astype(HALF)
    v.flip[...] = (row_at + lane_at == length - 1).astype(FULL).astype(HALF)

    table[0:H, :] = lax.dot_general(
        v.rel_bias[...],
        v.spread[section].astype(FULL),
        (((0,), (0,)), ((), ())),
        precision=PRECISE,
        preferred_element_type=FULL,
    )
    segments = jnp.where(encoder, v.enc_segments[...], v.dec_segments[...])
    v.segments[0:rows, :] = segments
    load_x().wait()
    load_att().wait()
    load_out().wait()
    load_cot().wait()
    pl.semaphore_wait(barrier, len(partners))

    def forward_row(row):
        at = row_slice(row)
        normalise(as_full(x_send), row, 0, attn_gain, None, low)

        def project(j):
            columns = pl.ds(at128(j, 256), 256)
            qkv_self[at, columns] = dot(low[at, :], w_att[:, columns]).astype(HALF)

        repeat(3 * width // 256, project)
        make_mask(v.segments, v.segments, row, encoder)
        attend(qkv_self, self_probs, mix_self, row, True)
        transpose_back(low, mix_self, row)
        add_projection(w_out, x_send, row)

        @pl.when(encoder)
        def _():
            enter_feed_forward(row)
            feed_forward(row, True, False, None, 0, None, True)
            normalise(as_full(res), row, 2, final_gain, unit_mid, x_send)
            memory_copy(row).start()
            write_layer(row).start()

    repeat(rows, forward_row)

    def decoder_row(row):
        at = row_slice(row)
        normalise(as_full(res), row, 2, cross_gain, unit_mid, low)
        for j in range(width // 256):
            n = slice(j * 256, (j + 1) * 256)
            qkv_cross[at, n] = dot(low[at, :], w_att[:, n]).astype(HALF)
        make_mask(v.enc_segments, v.dec_segments, row, None)
        memory_copy(row).wait_recv()

        def project_memory(j):
            columns = pl.ds(pl.multiple_of(width + j * 256, 128), 256)
            qkv_cross[at, columns] = dot(x_recv[at, :], w_att[:, columns]).astype(HALF)

        repeat(2 * width // 256, project_memory)
        attend(qkv_cross, cross_probs, mix_cross, row, False)
        transpose_back(low, mix_cross, row)
        add_projection(w_out, res, row)
        enter_feed_forward(row)
        feed_forward(row, True, True, grad, H, decoder_unit, row + 1 < rows)
        x_send[at, :] = res[at, :].astype(HALF)
        write_layer(row).start()
        norm_back(as_full(grad), as_full(unit_ffn), row, 1, ffn_gain, 1, as_full(cot), low)
        back_through_out(row)
        attend_back(qkv_cross, cross_probs, row, False, None)
        write_layer(row).wait()
        for j in range(width // 256):
            n = slice(j * 256, (j + 1) * 256)
            x_send[at, n] = dot_outer(
                qkv_cross[at, width : 3 * width], w_att[n, width : 3 * width]
            ).astype(HALF)
        memory_back(row).start()
        for j in range(width // 256):
            n = slice(j * 256, (j + 1) * 256)
            res[at, n] = dot_outer(qkv_cross[at, :width], w_att[n, :width])

    def load_x_again():
        return copy_in(v.inputs, qkv_cross.at[:, pl.ds(0, width)], 0)

    @pl.when(encoder)
    def _():
        load_x_again().start()

    @pl.when(decoder)
    def _():
        for copy in load_cross():
            copy.start()
        load_cross_out().start()
        for copy in load_cross():
            copy.wait()
        load_cross_out().wait()
        repeat(rows, decoder_row)
        load_att().start()
        load_out().start()
        weight_gradient(CROSS, 0, mix_cross, low, 0)

        def gained(b):
            at = pl.ds(at128(b, 128), 128)
            low_t[:, at] = (unit_mid[at, :].astype(FULL) * cross_gain).astype(HALF).T

        repeat(tokens // 128, gained)
        weight_gradient(CROSS, 1, low_t, qkv_cross, 0)
        for row in range(rows):
            transpose_rows(low_t, x_recv, row)
        weight_gradient(CROSS, 2, low_t, qkv_cross, width)
        weight_gradient(CROSS, 3, low_t, qkv_cross, 2 * width)
        load_x_again().start()
        for row in range(rows):
            norm_back(as_full(res), as_full(unit_mid), row, 2, cross_gain, 2, as_full(grad), low)
        for item in range(4):
            add_first(CROSS, item)
        load_att().wait()
        load_out().wait()

    load_x_again().wait()

    def unit_self(at):
        return qkv_cross[at, :width].astype(FULL) * inverse[at, 0:1]

    def advance(i):
        add(GATE_UP, i, 1)

        @pl.when(i >= 1)
        def _():
            add(GATE_UP, i - 1, 2)

        @pl.when(i >= 2)
        def _():
            add(GATE_UP, i - 2, 3)

    def backward_row(row):
        at = row_slice(row)

        @pl.when(encoder)
        def _():
            memory_back(row).wait_recv()

            def memory_grads(at):
                return cot[at, :].astype(FULL) + x_recv[at, :].astype(FULL)

            norm_back(memory_grads, as_full(unit_mid), row, 2, final_gain, 2, None, cot)
            feed_forward(row, False, True, res, 0, encoder_unit, row + 1 < rows)
            norm_back(as_full(res), as_full(unit_ffn), row, 1, ffn_gain, 1, as_full(grad), low)

        def tick(hp):
            @pl.when(jnp.where(encoder, row == rows - 1, row == 0))
            def _():
                advance(hp)

            @pl.when(decoder & (row == rows - 1) & (hp < chunks - PAIRS))
            def _():
                advance(PAIRS + hp)

        back_through_out(row)
        attend_back(qkv_self, self_probs, row, True, tick)
        for j in range(width // 256):
            n = slice(j * 256, (j + 1) * 256)
            res[at, n] = dot_outer(qkv_self[at, :], w_att[n, :])
        norm_back(as_full(res), unit_self, row, 0, attn_gain, 0, as_full(grad), None)

    repeat(rows, backward_row)
    write_grad = pltpu.make_async_copy(grad, v.grad_inputs, sem_out.at[1])
    write_grad.start()
    weight_gradient(SELF, 0, mix_self, low, 0)

    def gained_self(b):
        at = pl.ds(at128(b, 128), 128)
        low_t[:, at] = (unit_self(at) * attn_gain).astype(HALF).T

    repeat(tokens // 128, gained_self)
    for item in range(1, 4):
        weight_gradient(SELF, item, low_t, qkv_self, (item - 1) * width)
    for item in range(4):
        add_first(SELF, item)
    by_bucket = lax.dot_general(
        sums[...],
        v.summed[section].astype(FULL),
        (((1,), (1,)), ((), ())),
        precision=PRECISE,
        preferred_element_type=FULL,
    )
    if reduce:
        misc[:, width:] = misc[:, :128]
        by_bucket = jnp.concatenate([by_bucket, jnp.zeros((16, 128 - NBUCKET), FULL)], 1)
        for shard in range(16):
            place = block_place(shard // 4, (shard // 2) % 2, shard % 2)
            turned = pltpu.roll(misc[...], (width + 128 - shard * ways_rows) % (width + 128), 1)
            block = jnp.concatenate([turned[:, :128], by_bucket, jnp.zeros((8, 128), FULL)], 0)
            v.own4[0, place * 32 : (place + 1) * 32, :] = block.astype(HALF)
        begin(SMALL, 0)
        add_first(SMALL, 0)

    def drain(names, done):
        line = [(name, i) for name in names for i in range(by_name[name].count)]
        for n in range(done, len(line) + 2):
            for stage in (1, 2, 3):
                if 0 <= n + 1 - stage < len(line):
                    add(*line[n + 1 - stage], stage)

    @pl.when(encoder)
    def _():
        drain([GATE_UP, DOWN, SELF] + ([SMALL] if reduce else []), PAIRS)

    @pl.when(decoder)
    def _():
        drain([GATE_UP, DOWN, CROSS, SELF] + ([SMALL] if reduce else []), chunks)

    if not reduce:
        misc[8:24, :NBUCKET] = by_bucket
        outs = pltpu.make_async_copy(misc, v.out_misc, sem_out.at[2])
        outs.start()
    for name in [GATE_UP, DOWN, SELF] + ([SMALL] if reduce else []):
        repeat(by_name[name].count, functools.partial(finish, name))

    @pl.when(decoder)
    def _():
        repeat(by_name[CROSS].count, functools.partial(finish, CROSS))

    if reduce:

        @pl.when(encoder)
        def _():
            repeat(by_name[CROSS].count, lambda i: cross_over(CROSS, i, i).wait_recv())

        cross_over(SMALL, 0, 1 - section).wait_recv()
    else:
        outs.wait()
    write_grad.wait()

    @pl.when(encoder)
    def _():
        for row in range(rows):
            memory_copy(row).wait_send()
            write_layer(row).wait()

    @pl.when(decoder)
    def _():
        for row in range(rows):
            memory_back(row).wait_send()


def run_layers(args, ways):
    (
        inputs,
        cotangent,
        enc_segments,
        dec_segments,
        rel_bias,
        attn_norm,
        ffn_norm,
        w_qkv,
        w_attn_out,
        w_gate_up,
        w_down,
        cross_norm,
        cross_query,
        cross_kv,
        cross_out,
        final_norm,
    ) = args
    _, rows, length, width = inputs.shape
    hidden = w_down.shape[1]
    tokens = rows * length
    reduce = ways == 16
    spread, summed = bucket_tables(length)
    operands = dict(
        inputs=inputs.reshape(tokens, width),
        cotangent=cotangent.reshape(tokens, width),
        w_qkv=w_qkv,
        w_attn_out=w_attn_out,
        w_gate_up=w_gate_up,
        w_down=w_down,
        cross_query=cross_query,
        cross_kv=cross_kv,
        cross_out=cross_out,
    )
    small = dict(
        enc_segments=enc_segments,
        dec_segments=dec_segments,
        rel_bias=rel_bias,
        attn_norm=attn_norm,
        ffn_norm=ffn_norm,
        mid_norms=jnp.stack([cross_norm, final_norm]),
        spread=jnp.asarray(spread, HALF),
        summed=jnp.asarray(summed, HALF),
    )
    block = width // 16
    groups = [
        Group(GATE_UP, hidden // CHUNK, block, 2 * CHUNK),
        Group(DOWN, 3, hidden // 16, 256),
        Group(CROSS, 4, block, width),
        Group(SELF, 4, block, width),
    ]
    outs = dict(
        layer_out=((tokens, width), HALF),
        grad_inputs=((tokens, width), FULL),
    )
    if reduce:
        groups.append(Group(SMALL, 1, 32, 128))
    for g in groups:
        outs[f"out{g.name}"] = ((g.count, g.rows if reduce else 16 * g.rows, g.cols), HALF)
    if reduce:
        outs[f"out{SMALL}"] = ((2, 32, 128), HALF)
    else:
        outs[MISC] = ((24, width + 128), FULL)
    scratch = dict(
        x_send=pltpu.VMEM((tokens, width), HALF),
        x_recv=pltpu.VMEM((tokens, width), HALF),
        low=pltpu.VMEM((tokens, width), HALF),
        low_t=pltpu.VMEM((width, tokens), HALF),
        unit_ffn=pltpu.VMEM((tokens, width), HALF),
        unit_mid=pltpu.VMEM((tokens, width), HALF),
        cot=pltpu.VMEM((tokens, width), HALF),
        res=pltpu.VMEM((tokens, width), FULL),
        grad=pltpu.VMEM((tokens, width), FULL),
        w_att=pltpu.VMEM((width, 3 * width), HALF),
        w_out=pltpu.VMEM((width, width), HALF),
        qkv_self=pltpu.VMEM((tokens, 3 * width), HALF),
        qkv_cross=pltpu.VMEM((tokens, 3 * width), HALF),
        mix_self=pltpu.VMEM((width, tokens), HALF),
        mix_cross=pltpu.VMEM((width, tokens), HALF),
        probs=pltpu.VMEM((H * rows, length, length), HALF),
        big=pltpu.VMEM((4, width, width), HALF),
        inverse=pltpu.VMEM((tokens, 8), FULL),
        mask=pltpu.VMEM((length, length), HALF),
        near=pltpu.VMEM((length, length), HALF),
        past=pltpu.VMEM((length, length), HALF),
        flip=pltpu.VMEM((length, length), HALF),
        grad_mix=pltpu.VMEM((length, width), HALF),
        segments=pltpu.VMEM((8, length), jnp.int32),
        table=pltpu.VMEM((16, 2 * length), FULL),
        sums=pltpu.VMEM((16, 2 * length), FULL),
        misc=pltpu.VMEM((8 if reduce else 24, width + 128), FULL),
        load=pltpu.SemaphoreType.DMA((5 + 5 * RING,)),
        sem_x=pltpu.SemaphoreType.DMA((4, rows)),
        sem_out=pltpu.SemaphoreType.DMA((4 + rows,)),
    )
    for g in groups:
        if g.name != SELF:
            scratch[f"own{g.name}"] = pltpu.VMEM((g.count, 16 * g.rows, g.cols), HALF)
        if reduce:
            for stage in range(4):
                scratch[f"came{stage}x{g.name}"] = pltpu.VMEM((g.count, (8 >> stage) * g.rows, g.cols), HALF)
        scratch[f"sem{g.name}"] = pltpu.SemaphoreType.DMA((g.count, 11))
    names = list(operands) + list(small) + list(outs) + list(scratch)
    results = pl.pallas_call(
        functools.partial(layer_kernel, names, groups, reduce, rows, length, width, hidden),
        out_shape=[jax.ShapeDtypeStruct(*out) for out in outs.values()],
        in_specs=[pl.BlockSpec(memory_space=pl.ANY)] * len(operands)
        + [pl.BlockSpec(memory_space=pltpu.VMEM)] * len(small),
        out_specs=[pl.BlockSpec(memory_space=pl.ANY)] * len(outs),
        scratch_shapes=list(scratch.values()),
        compiler_params=pltpu.CompilerParams(
            collective_id=1, has_side_effects=True, vmem_limit_bytes=VMEM_LIMIT
        ),
    )(*operands.values(), *small.values())
    return dict(zip(outs, results)), reduce


LAYER, INPUT, MISC = "layer_out", "grad_inputs", "out_misc"
VMEM_LIMIT = 64 * 2**20 - 64 * 2**10


def finish_kernel(width, pair, lower, cross, own, small, layer, grad, *refs):
    layer_out, grad_out, qkv, attn_out, gate_up, down, attn, ffn, query, kv, outer, mid, final, rel = refs[:14]
    layer_held, grad_held, sem = refs[14:]
    through = [(layer, layer_held, layer_out), (grad, grad_held, grad_out)]
    arriving = [pltpu.make_async_copy(a, b, sem.at[n]) for n, (a, b, _) in enumerate(through)]
    leaving = [pltpu.make_async_copy(b, c, sem.at[2 + n]) for n, (_, b, c) in enumerate(through)]
    for copy in arriving:
        copy.start()
    for came, copy in zip(arriving, leaving):
        came.wait()
        copy.start()
    chunks = pair.shape[0]
    for k in range(chunks):
        gate_up[:, k * CHUNK : (k + 1) * CHUNK] = pair[k, :, :CHUNK].astype(FULL)
        up = (chunks + k) * CHUNK
        gate_up[:, up : up + CHUNK] = pair[k, :, CHUNK:].astype(FULL)
    for j in range(3):
        down[:, j * 256 : (j + 1) * 256] = lower[j].astype(FULL)
        qkv[:, j * width : (j + 1) * width] = own[1 + j].astype(FULL)
    attn_out[...] = own[0].astype(FULL)
    outer[...] = cross[0].astype(FULL)
    query[...] = cross[1].astype(FULL)
    for j in range(2):
        kv[:, j * width : (j + 1) * width] = cross[2 + j].astype(FULL)
    block = attn.shape[1]
    mine = small[lax.axis_index("section")].astype(FULL)
    attn[...] = mine[0:1, :block]
    ffn[...] = mine[1:2, :block]
    encoder, decoder = small[0].astype(FULL), small[1].astype(FULL)
    mid[...] = decoder[2:3, :block]
    final[...] = encoder[2:3, :block]
    rel[...] = (encoder[8:24] + decoder[8:24]).T[:NBUCKET, :H]
    for copy in leaving:
        copy.wait()


def finished(out, inputs, hidden):
    tokens, width = out[LAYER].shape
    block = width // 16
    shapes = [(out[LAYER].shape, HALF), (out[INPUT].shape, FULL)] + [
        (shape, FULL)
        for shape in [
            (block, 3 * width),
            (block, width),
            (block, 2 * hidden),
            (hidden // 16, width),
            (1, block),
            (1, block),
            (block, width),
            (block, 2 * width),
            (block, width),
            (1, block),
            (1, block),
            (NBUCKET, H),
        ]
    ]
    layer, grad, qkv, attn_out, gate_up, down, attn, ffn, query, kv, outer, mid, final, rel = pl.pallas_call(
        functools.partial(finish_kernel, width),
        out_shape=[jax.ShapeDtypeStruct(*shape) for shape in shapes],
        in_specs=[pl.BlockSpec(memory_space=pltpu.VMEM)] * 5 + [pl.BlockSpec(memory_space=pl.ANY)] * 2,
        out_specs=[pl.BlockSpec(memory_space=pl.ANY)] * 2 + [pl.BlockSpec(memory_space=pltpu.VMEM)] * 12,
        scratch_shapes=[
            pltpu.VMEM(out[LAYER].shape, HALF),
            pltpu.VMEM(out[INPUT].shape, FULL),
            pltpu.SemaphoreType.DMA((4,)),
        ],
        compiler_params=pltpu.CompilerParams(vmem_limit_bytes=VMEM_LIMIT),
    )(*[out[f"out{name}"] for name in range(5)], out[LAYER], out[INPUT])
    return (
        layer.reshape(inputs.shape),
        grad.reshape(inputs.shape),
        qkv[None],
        attn_out[None],
        gate_up[None],
        down[None],
        attn,
        ffn,
        query,
        kv,
        outer,
        mid.reshape(block),
        final.reshape(block),
        rel,
    )


def shards(*args):
    inputs = args[0]
    ways = lax.axis_size("dp")
    width = inputs.shape[3]
    hidden = args[10].shape[1]
    out, reduce = run_layers(args, ways)
    if reduce:
        return finished(out, inputs, hidden)

    def wide(name):
        value = out[f"out{name}"]
        total = lax.psum_scatter(value, "dp", scatter_dimension=1, tiled=True)
        if name == CROSS:
            total = lax.psum(jnp.where(lax.axis_index("section") == 1, total, 0), "section")
        return total.astype(FULL)

    def side_by_side(value):
        return jnp.swapaxes(value, 0, 1).reshape(value.shape[1], -1)

    gate_up = wide(GATE_UP)
    chunks, block, _ = gate_up.shape
    gate_up = gate_up.reshape(chunks, block, 2, CHUNK).transpose(1, 2, 0, 3).reshape(block, 2 * hidden)
    down, cross, late = wide(DOWN), wide(CROSS), wide(SELF)
    own = lax.psum(out[MISC], "dp")
    misc = lax.all_gather(own, "section", axis=0)
    start = lax.axis_index("dp") * block

    def piece(vector):
        return lax.dynamic_slice_in_dim(vector, start, block, 0)

    return (
        out[LAYER].reshape(inputs.shape),
        out[INPUT].reshape(inputs.shape),
        side_by_side(late[1:])[None],
        late[0][None],
        gate_up[None],
        side_by_side(down)[None],
        piece(own[0, :width])[None],
        piece(own[1, :width])[None],
        cross[1],
        side_by_side(cross[2:]),
        cross[0],
        piece(misc[1, 2, :width]),
        piece(misc[0, 2, :width]),
        (misc[0] + misc[1])[8 : 8 + H, :NBUCKET].T,
    )


def solution(mesh):
    layer = P("section", "dp", None, None)
    matrix = P("section", None, None)
    return jax.shard_map(
        shards,
        mesh=mesh,
        in_specs=(layer, layer, P("dp", None), P("dp", None), P())
        + (P("section", None),) * 2
        + (matrix,) * 4
        + (P(),) * 5,
        out_specs=(layer, layer)
        + (P("section", "dp", None),) * 4
        + (P("section", "dp"),) * 2
        + (P("dp", None),) * 3
        + (P("dp"),) * 2
        + (P(),),
        check_vma=False,
    )
```

```python
import functools
import math
import types

import jax
import jax.numpy as jnp
import numpy as np
from jax import lax
from jax.experimental import pallas as pl
from jax.experimental.pallas import tpu as pltpu
from jax.sharding import PartitionSpec as P

H = 12
HD = 64
NBUCKET = 32
MAXDIST = 128
EPSILON = 1e-06
MASKED = -1000000000.0
MESH = pl.DeviceIdType.MESH
PRECISE = lax.Precision.HIGHEST
HALF = jnp.bfloat16
FULL = jnp.float32
PAIRS = H // 2
CHUNK = 256
BLOCK = 64
RING = 4
DECODER_TICKS = 4
GATE_UP, DOWN, CROSS, SELF, SMALL = range(5)
GELU_SCALE = math.sqrt(2.0 / math.pi)
GELU_CUBE = 0.044715


def bucket_of(offsets, causal, buckets, reach_max):
    if causal:
        half_count = buckets
        side_offset = offsets * 0
        distance = np.maximum(-offsets, 0)
    else:
        half_count = buckets // 2
        side_offset = (offsets > 0).astype(np.int32) * half_count
        distance = np.abs(offsets)
    exact_count = half_count // 2
    clipped = np.maximum(distance, exact_count)
    spread = exact_count + np.floor(
        np.log(clipped / exact_count) / np.log(reach_max / exact_count) * (half_count - exact_count)
        + 1e-09
    ).astype(np.int32)
    spread = np.minimum(spread, half_count - 1)
    return (side_offset + np.where(distance < exact_count, distance, spread)).astype(np.int32)


def bucket_tables(length):
    lane = np.arange(length)
    spread = np.concatenate([-lane, length - lane])
    summed = np.concatenate([-(lane + 1), length - 1 - lane])
    tables = []
    for offsets in (spread, summed):
        clipped = np.clip(offsets, -(length - 1), length - 1)
        tables.append(
            np.stack(
                [
                    (bucket_of(clipped, causal, NBUCKET, MAXDIST)[None] == np.arange(NBUCKET)[:, None])
                    for causal in (False, True)
                ]
            ).astype(np.float32)
        )
    return tables


def dot(left, right):
    return jnp.dot(left, right, preferred_element_type=FULL)


def dot_outer(left, right):
    return lax.dot_general(left, right, (((1,), (1,)), ((), ())), preferred_element_type=FULL)


def repeat(count, step):
    def body(index, carry):
        step(index)
        return carry

    lax.fori_loop(0, count, body, 0)


def at128(index, scale):
    return pl.multiple_of(index * scale, 128)


class Group:
    def __init__(self, name, count, rows, cols):
        self.name, self.count, self.rows, self.cols = name, count, rows, cols


def layer_kernel(names, groups, reduce, rows, length, width, hidden, *refs):
    v = types.SimpleNamespace(**dict(zip(names, refs)))
    tokens = rows * length
    chunks = hidden // CHUNK
    ways_rows = width // 16
    me, section = lax.axis_index("dp"), lax.axis_index("section")
    encoder, decoder = section == 0, section == 1
    z, y, c = me // 4, (me // 2) % 2, me % 2
    other = (1 - section, me)

    x_send, x_recv = v.x_send, v.x_recv
    low, low_t, grad_mix = v.low, v.low_t, v.grad_mix
    joint, units = grad_mix.at[:, : 2 * CHUNK], grad_mix.at[:, 2 * CHUNK : 3 * CHUNK]
    unit_ffn, unit_mid, cot = v.unit_ffn, v.unit_mid, v.cot
    res, grad = v.res, v.grad
    w_att, w_out = v.w_att, v.w_out
    qkv_self, qkv_cross = v.qkv_self, v.qkv_cross
    mix_self, mix_cross = v.mix_self, v.mix_cross
    probs, big = v.probs, v.big
    inverse, table, sums, mask = v.inverse, v.table, v.sums, v.mask
    misc = v.misc
    load, sem_x, sem_out = v.load, v.sem_x, v.sem_out

    def device(zz, yy, cc):
        return (section, zz * 4 + yy * 2 + cc)

    z_low, z_high = z % 2, z // 2
    near_y, near_z = device(z, 1 - y, c), device(z + 1 - 2 * z_low, y, c)
    sibling, far_z = device(z, y, 1 - c), device(z + 2 - 4 * z_high, y, c)
    partners = [other] + ([sibling, near_y, near_z, far_z] if reduce else [])
    barrier = pltpu.get_barrier_semaphore()
    for target in partners:
        pl.semaphore_signal(barrier, inc=1, device_id=target, device_id_type=MESH)

    def copy_in(source, target, slot):
        return pltpu.make_async_copy(source, target, load.at[slot])

    def load_x():
        return copy_in(v.inputs, x_send, 0)

    def load_cot():
        return copy_in(v.cotangent, cot, 1)

    def load_att():
        return copy_in(v.w_qkv.at[0], w_att, 2)

    def load_out():
        return copy_in(v.w_attn_out.at[0], w_out, 3)

    def load_cross():
        return [
            copy_in(v.cross_query, w_att.at[:, pl.ds(0, width)], 2),
            copy_in(v.cross_kv, w_att.at[:, pl.ds(width, 2 * width)], 4),
        ]

    def load_cross_out():
        return copy_in(v.cross_out, w_out, 3)

    ring = v.own2

    def load_chunk(index):
        slot = index % RING
        at = at128(index, CHUNK)
        pieces = [
            copy_in(
                v.w_down.at[0, pl.ds(at, CHUNK), pl.ds(j * 256, 256)],
                ring.at[slot, pl.ds(j * 256, 256), pl.ds(2 * CHUNK, 256)],
                7 + j + 5 * slot,
            )
            for j in range(width // 256)
        ]
        return pieces + [
            copy_in(
                v.w_gate_up.at[0, :, pl.ds(at, CHUNK)], ring.at[slot, :, pl.ds(0, CHUNK)], 5 + 5 * slot
            ),
            copy_in(
                v.w_gate_up.at[0, :, pl.ds(pl.multiple_of(hidden + at, 128), CHUNK)],
                ring.at[slot, :, pl.ds(CHUNK, CHUNK)],
                6 + 5 * slot,
            ),
        ]

    load_x().start()
    load_att().start()
    load_out().start()
    load_cot().start()
    misc[...] = jnp.zeros_like(misc)
    sums[...] = jnp.zeros_like(sums)
    for k in range(RING - 1):
        for copy in load_chunk(k):
            copy.start()

    by_name = {group.name: group for group in groups}
    stacks = {
        group.name: (big if group.name == SELF else getattr(v, f"own{group.name}")) for group in groups
    }

    def block_place(zz, yy, cc):
        return cc * 8 + yy * 4 + (zz % 2) * 2 + zz // 2

    def put(name, item, columns, tile):
        own, r = stacks[name], by_name[name].rows
        low_tile = tile.astype(HALF)
        for shard in range(16):
            place = shard
            if reduce:
                place = block_place(shard // 4, (shard // 2) % 2, shard % 2)
            own[item, place * r : (place + 1) * r, columns] = low_tile[
                shard * r : (shard + 1) * r
            ]

    def stages(name):
        result, base, count = [], 0, 16 * by_name[name].rows
        for bit, target in ((c, sibling), (y, near_y), (z_low, near_z), (z_high, far_z)):
            count = count // 2
            sent, base = base + (1 - bit) * count, base + bit * count
            result.append((target, pl.multiple_of(sent, 16), pl.multiple_of(base, 16), count))
        return result

    def exchange(name, i, stage):
        target, sent, _, count = stages(name)[stage]
        sems = getattr(v, f"sem{name}")
        return pltpu.make_async_remote_copy(
            stacks[name].at[i, pl.ds(sent, count)],
            getattr(v, f"came{stage}x{name}").at[i],
            sems.at[i, 2 * stage],
            sems.at[i, 2 * stage + 1],
            device_id=target,
            device_id_type=MESH,
        )

    def kept_rows(name):
        _, _, kept, count = stages(name)[3]
        return pl.ds(kept, count)

    def write_out(name, i):
        source = stacks[name].at[i, kept_rows(name)] if reduce else stacks[name].at[i]
        place = section if name == SMALL else i
        return pltpu.make_async_copy(
            source, getattr(v, f"out{name}").at[place], getattr(v, f"sem{name}").at[i, 8]
        )

    def cross_over(name, i, place):
        sems = getattr(v, f"sem{name}")
        return pltpu.make_async_remote_copy(
            stacks[name].at[i, kept_rows(name)],
            getattr(v, f"out{name}").at[place],
            sems.at[i, 9],
            sems.at[i, 10],
            device_id=other,
            device_id_type=MESH,
        )

    def begin(name, i):
        if reduce:
            exchange(name, i, 0).start()
        else:
            write_out(name, i).start()

    def add(name, i, stage):
        if not reduce:
            return
        own, came = stacks[name], getattr(v, f"came{stage}x{name}")
        exchange(name, i, stage).wait_recv()
        _, _, kept, count = stages(name)[stage]
        size = min(count, 2 * by_name[name].rows)

        def step(m):
            at = pl.ds(pl.multiple_of(kept + m * size, 16), size)
            own[i, at] = own[i, at] + came[i, pl.ds(pl.multiple_of(m * size, 16), size)]

        repeat(count // size, step)
        if stage < 3:
            exchange(name, i, stage + 1).start()
        else:
            write_out(name, i).start()
            if name == CROSS:
                cross_over(name, i, i).start()
            if name == SMALL:
                cross_over(name, i, section).start()

    def add_first(name, i):
        add(name, i, 0)

    def finish(name, i):
        write_out(name, i).wait()
        if reduce:
            for stage in range(4):
                exchange(name, i, stage).wait_send()
            if name in (CROSS, SMALL):
                cross_over(name, i, i).wait_send()

    def items_of(*names):
        return [(name, i) for name in names for i in range(by_name[name].count)]

    last = items_of(SELF, SMALL) if reduce else items_of(SELF)
    encoder_line = items_of(GATE_UP, DOWN) + last
    decoder_line = items_of(GATE_UP, DOWN, CROSS) + last

    def advance(line, n):
        for stage in (1, 2, 3):
            if 0 <= n + 1 - stage < len(line):
                add(*line[n + 1 - stage], stage)

    def block_of(ref, b):
        return ref.at[b // 9, pl.ds(at128((b % 9) // 3, 256), 256), pl.ds(at128(b % 3, 256), 256)]

    def decoder_unit(k):
        return block_of(big, H + 2 * chunks + k)

    def encoder_unit(k):
        lanes = pl.ds(pl.multiple_of(width + k // 2 * CHUNK, 128), CHUNK)
        return qkv_cross.at[pl.ds(at128(k % 2, length), length), lanes]

    def self_probs(head, row):
        return probs.at[head * rows + row]

    def cross_probs(head, row):
        return block_of(big, head)

    def row_slice(row):
        return pl.ds(pl.multiple_of(row * length, length), length)

    def part_slice(row, b, size):
        return pl.ds(pl.multiple_of(row * length + b * size, size), size)

    lanes = lax.broadcasted_iota(jnp.int32, (1, 128), 1)
    half_lanes = [(lanes < HD).astype(HALF), (lanes >= HD).astype(HALF)]

    def make_mask(key_segments, query_segments, row, causal):
        keys = key_segments[pl.ds(row, 1), :].astype(FULL)
        keys = jnp.broadcast_to(keys, (8, length)).T[:, :1]
        queries = query_segments[pl.ds(row, 1), :].astype(FULL)
        same = keys == queries
        if causal is not None:
            key_at = lax.broadcasted_iota(jnp.int32, (length, length), 0)
            query_at = lax.broadcasted_iota(jnp.int32, (length, length), 1)
            same = same & ((key_at <= query_at) | causal)
        mask[...] = jnp.where(same, 0.0, MASKED).astype(HALF)

    def lanes_of(offset, hp):
        return pl.ds(pl.multiple_of(offset + hp * 128, 128), 128)

    def attend(qkv, probs_of, mix, row, with_bias):
        at = row_slice(row)

        def pair(hp):
            queries = qkv[at, lanes_of(0, hp)]
            keys = qkv[at, lanes_of(width, hp)]
            values_t = qkv[at, lanes_of(2 * width, hp)].T
            both = jnp.concatenate([keys * half_lanes[0], keys * half_lanes[1]], 0)
            scores = dot_outer(both, queries)
            for e in range(2):
                if with_bias:
                    line = table[pl.ds(hp * 2 + e, 1), :]
                    skewed = line[:, length:] + v.near[...].astype(FULL) * (line[:, :length] - line[:, length:])
                    bias = pltpu.roll(skewed, 0, 1, stride=1, stride_axis=0)
                soft_parts = []
                for part in range(length // 128):
                    n = slice(part * 128, (part + 1) * 128)
                    shifted = scores[e * length : (e + 1) * length, n] + mask[:, n].astype(FULL)
                    if with_bias:
                        shifted = shifted + bias[:, n]
                    raised = jnp.exp(shifted - jnp.max(shifted, 0, keepdims=True))
                    total = jnp.sum(raised, 0, keepdims=True)
                    soft_parts.append((raised * (1.0 / total)).astype(HALF))
                softmaxed = jnp.concatenate(soft_parts, 1)
                probs_of(hp * 2 + e, row)[...] = softmaxed
                mixed = dot(values_t[e * HD : (e + 1) * HD], softmaxed)
                mix[pl.ds(pl.multiple_of(hp * 128 + e * HD, 16), HD), at] = mixed.astype(HALF)

        for hp in range(PAIRS):
            pair(hp)

    def attend_back(qkv, probs_of, row, with_bias):
        at = row_slice(row)
        left = lax.broadcasted_iota(jnp.int32, (length, 128), 1) < HD
        def pair(hp):
            q_lanes, k_lanes, v_lanes = lanes_of(0, hp), lanes_of(width, hp), lanes_of(2 * width, hp)
            queries, keys, values = qkv[at, q_lanes], qkv[at, k_lanes], qkv[at, v_lanes]
            outer = grad_mix[:, q_lanes]
            keys_t = keys.T
            both = jnp.concatenate([values * half_lanes[0], values * half_lanes[1]], 0)
            grad_soft = dot_outer(both, outer)
            softs, scores = [], []
            for e in range(2):
                soft_low = probs_of(hp * 2 + e, row)[...]
                score_parts = []
                for part in range(length // 128):
                    n = slice(part * 128, (part + 1) * 128)
                    soft = soft_low[:, n].astype(FULL)
                    weighted = soft * grad_soft[e * length : (e + 1) * length, n]
                    shared = jnp.sum(weighted, 0, keepdims=True)
                    score_parts.append((weighted - soft * shared).astype(HALF))
                scores.append(jnp.concatenate(score_parts, 1))
                softs.append(soft_low)
            grad_keys = dot(jnp.concatenate(scores, 0), queries)
            grad_values = dot(jnp.concatenate(softs, 0), outer)
            left_side = jnp.concatenate([keys_t, v.flip[...]], 0) if with_bias else keys_t
            parts = []
            for e in range(2):
                product = dot(left_side, scores[e])
                parts.append(product[e * HD : (e + 1) * HD])
                if with_bias:
                    aligned = pltpu.roll(product[128:], 0, 1, stride=1, stride_axis=0)
                    before = jnp.sum(aligned * v.past[...].astype(FULL), 0, keepdims=True)
                    after = jnp.sum(aligned, 0, keepdims=True) - before
                    line = pl.ds(hp * 2 + e, 1)
                    sums[line, :] = sums[line, :] + jnp.concatenate([before, after], 1)
            qkv[at, q_lanes] = jnp.concatenate(parts, 0).T.astype(HALF)
            qkv[at, k_lanes] = jnp.where(left, grad_keys[:length], grad_keys[length:]).astype(HALF)
            qkv[at, v_lanes] = jnp.where(left, grad_values[:length], grad_values[length:]).astype(HALF)

        for hp in range(PAIRS):
            pair(hp)

    def normalise(load_rows, row, column, gain, unit_ref, target):
        for b in range(length // BLOCK):
            at = part_slice(row, b, BLOCK)
            value = load_rows(at)
            scale = lax.rsqrt(jnp.mean(value * value, -1, keepdims=True) + EPSILON)
            inverse[at, column : column + 1] = scale
            unit = value * scale
            if unit_ref is not None:
                unit_ref[at, :] = unit.astype(HALF)
            target[at, :] = (unit * gain).astype(HALF)

    def norm_back(load_grad, load_unit, row, column, gain, misc_row, load_base, low_ref):
        def step(b, gain_sum):
            at = part_slice(row, b, BLOCK)
            normed, unit = load_grad(at), load_unit(at)
            weighted = normed * unit
            grad_unit = normed * gain
            scale = inverse[at, column : column + 1]
            inner = jnp.mean(weighted * gain, -1, keepdims=True)
            result = scale * (grad_unit - unit * inner)
            if load_base is not None:
                result = result + load_base(at)
            grad[at, :] = result
            if low_ref is not None:
                low_ref[at, :] = result.astype(HALF)
            return gain_sum + jnp.sum(weighted.reshape(BLOCK // 8, 8, width), 0)

        gain_sum = lax.fori_loop(0, length // BLOCK, step, jnp.zeros((8, width), FULL))
        line = slice(misc_row, misc_row + 1)
        misc[line, :width] = misc[line, :width] + jnp.sum(gain_sum, 0, keepdims=True)

    def transpose_rows(target, source, row):
        for b in range(length // 128):
            at = part_slice(row, b, 128)
            target[:, at] = source[at, :].T

    def transpose_back(target, source, row):
        for b in range(length // 128):
            at = part_slice(row, b, 128)
            target[at, :] = source[:, at].T

    def add_projection(weights, base, row):
        at = row_slice(row)
        for j in range(width // 256):
            n = slice(j * 256, (j + 1) * 256)
            res[at, n] = base[at, n].astype(FULL) + dot(low[at, :], weights[:, n])

    def feed_forward(row, forward, backward, total, base, unit_block, more):
        at = row_slice(row)
        if backward:
            total[at, :] = jnp.zeros((length, width), FULL)

        def step(k):
            slot = k % RING
            pair_weights = ring.at[slot, :, : 2 * CHUNK]
            lower = [ring.at[slot, j * 256 : (j + 1) * 256, 2 * CHUNK :] for j in range(width // 256)]

            @pl.when((k + RING - 1 < chunks) | more)
            def _():
                for copy in load_chunk((k + RING - 1) % chunks):
                    copy.start()

            for copy in load_chunk(k):
                copy.wait()
            kept = [block_of(big, row * 2 * chunks + k * 2 + side) for side in range(2)]
            if forward:
                joined = dot(low[at, :], pair_weights[...])
                gate, up = joined[:, :CHUNK], joined[:, CHUNK:]
                if not backward:
                    kept[0][...] = gate.astype(HALF)
                    kept[1][...] = up.astype(HALF)
            else:
                gate, up = kept[0][...].astype(FULL), kept[1][...].astype(FULL)
            squared = gate * gate
            curve = jnp.tanh(gate * (GELU_SCALE + GELU_SCALE * GELU_CUBE * squared))
            rising = 0.5 + 0.5 * curve
            bent = gate * rising
            unit = (bent * up).astype(HALF)
            if forward:
                for j in range(width // 256):
                    n = slice(j * 256, (j + 1) * 256)
                    res[at, n] = res[at, n] + dot(unit, lower[j][...])
            if not backward:
                return
            grad_hidden = sum(
                dot_outer(cot[at, j * 256 : (j + 1) * 256], lower[j][...]) for j in range(width // 256)
            )
            slope = rising + 0.5 * gate * (1.0 - curve * curve) * (
                GELU_SCALE + 3.0 * GELU_SCALE * GELU_CUBE * squared
            )
            pair = jnp.concatenate(
                [(grad_hidden * up * slope).astype(HALF), (grad_hidden * bent).astype(HALF)], 1
            )
            total[at, :] = total[at, :] + dot_outer(pair, pair_weights[...])
            joint[...] = pair
            units[...] = unit.T
            first = [block_of(big, base + k * 2 + side) for side in range(2)]

            @pl.when(row == 0)
            def _():
                first[0][...] = joint[:, :CHUNK]
                first[1][...] = joint[:, CHUNK:]
                unit_block(k)[...] = units[...]

            @pl.when(row == rows - 1)
            def _():
                for part in range(2):
                    columns = slice(part * CHUNK, (part + 1) * CHUNK)
                    right = jnp.concatenate([first[part][...], joint[:, columns]], 0)
                    put(GATE_UP, k, columns, dot(low_t[...], right))
                begin(GATE_UP, k)
                r = by_name[DOWN].rows
                both = jnp.concatenate([unit_block(k)[...], units[...]], 1)
                for part in range(3):
                    tile = dot(both, cot[:, part * 256 : (part + 1) * 256]).astype(HALF)
                    if reduce:
                        for shard in range(CHUNK // r):
                            place = block_place(k // 2, k % 2, shard)
                            v.own1[part, pl.ds(pl.multiple_of(place * r, 16), r)] = tile[
                                shard * r : (shard + 1) * r
                            ]
                    else:
                        v.own1[part, pl.ds(at128(k, CHUNK), CHUNK)] = tile

                @pl.when(k > 0)
                def _():
                    add_first(GATE_UP, k - 1)

        repeat(chunks, step)
        if backward:

            @pl.when(row == rows - 1)
            def _():
                for part in range(3):
                    begin(DOWN, part)
                add_first(GATE_UP, chunks - 1)
                for part in range(3):
                    add_first(DOWN, part)

    def weight_gradient(name, item, left_t, right, at):
        for j in range(width // 256):
            n = slice(j * 256, (j + 1) * 256)
            put(name, item, n, dot(left_t[...], right[:, at + j * 256 : at + (j + 1) * 256]))
        begin(name, item)

    def back_through_out(row):
        for j in range(width // 256):
            n = slice(j * 256, (j + 1) * 256)
            grad_mix[:, n] = dot_outer(low[row_slice(row), :], w_out[n, :]).astype(HALF)

    def as_full(ref):
        return lambda at: ref[at, :].astype(FULL)

    def memory_copy(row):
        return pltpu.make_async_remote_copy(
            x_send.at[row_slice(row)],
            x_recv.at[row_slice(row)],
            sem_x.at[0, row],
            sem_x.at[1, row],
            device_id=other,
            device_id_type=MESH,
        )

    def memory_back(row):
        return pltpu.make_async_remote_copy(
            x_send.at[row_slice(row)],
            x_recv.at[row_slice(row)],
            sem_x.at[2, row],
            sem_x.at[3, row],
            device_id=other,
            device_id_type=MESH,
        )

    def write_layer(row):
        return pltpu.make_async_copy(
            x_send.at[row_slice(row)], v.layer_out.at[row_slice(row)], sem_out.at[4 + row]
        )

    ffn_gain = v.ffn_norm[...].astype(FULL)
    attn_gain = v.attn_norm[...].astype(FULL)
    cross_gain = v.mid_norms[...].astype(FULL)[0:1]
    final_gain = v.mid_norms[...].astype(FULL)[1:2]

    def enter_feed_forward(row):
        normalise(as_full(res), row, 1, ffn_gain, unit_ffn, low)
        transpose_rows(low_t, low, row)

    row_at = lax.broadcasted_iota(jnp.int32, (length, length), 0)
    lane_at = lax.broadcasted_iota(jnp.int32, (length, length), 1)
    v.near[...] = (lane_at + row_at < length).astype(FULL).astype(HALF)
    v.past[...] = (lane_at < row_at).astype(FULL).astype(HALF)
    v.flip[...] = (row_at + lane_at == length - 1).astype(FULL).astype(HALF)

    table[0:H, :] = lax.dot_general(
        v.rel_bias[...],
        v.spread[section].astype(FULL),
        (((0,), (0,)), ((), ())),
        precision=PRECISE,
        preferred_element_type=FULL,
    )
    segments = jnp.where(encoder, v.enc_segments[...], v.dec_segments[...])
    v.segments[0:rows, :] = segments
    load_x().wait()
    load_att().wait()
    load_out().wait()
    load_cot().wait()
    pl.semaphore_wait(barrier, len(partners))

    def forward_row(row):
        at = row_slice(row)
        normalise(as_full(x_send), row, 0, attn_gain, None, low)

        for j in range(3 * width // 256):
            n = slice(j * 256, (j + 1) * 256)
            qkv_self[at, n] = dot(low[at, :], w_att[:, n]).astype(HALF)
        make_mask(v.segments, v.segments, row, encoder)
        attend(qkv_self, self_probs, mix_self, row, True)
        transpose_back(low, mix_self, row)
        add_projection(w_out, x_send, row)

        @pl.when(encoder)
        def _():
            enter_feed_forward(row)
            feed_forward(row, True, False, None, 0, None, True)
            normalise(as_full(res), row, 2, final_gain, unit_mid, x_send)
            memory_copy(row).start()
            write_layer(row).start()

    repeat(rows, forward_row)

    def decoder_row(row):
        at = row_slice(row)
        normalise(as_full(res), row, 2, cross_gain, unit_mid, low)
        for j in range(width // 256):
            n = slice(j * 256, (j + 1) * 256)
            qkv_cross[at, n] = dot(low[at, :], w_att[:, n]).astype(HALF)
        make_mask(v.enc_segments, v.dec_segments, row, None)
        memory_copy(row).wait_recv()

        for j in range(width // 256, 3 * width // 256):
            n = slice(j * 256, (j + 1) * 256)
            qkv_cross[at, n] = dot(x_recv[at, :], w_att[:, n]).astype(HALF)
        attend(qkv_cross, cross_probs, mix_cross, row, False)
        transpose_back(low, mix_cross, row)
        add_projection(w_out, res, row)
        enter_feed_forward(row)
        feed_forward(row, True, True, grad, H, decoder_unit, row + 1 < rows)
        x_send[at, :] = res[at, :].astype(HALF)
        write_layer(row).start()
        norm_back(as_full(grad), as_full(unit_ffn), row, 1, ffn_gain, 1, as_full(cot), low)
        back_through_out(row)
        attend_back(qkv_cross, cross_probs, row, False)
        write_layer(row).wait()
        for j in range(width // 256):
            n = slice(j * 256, (j + 1) * 256)
            x_send[at, n] = dot_outer(
                qkv_cross[at, width : 3 * width], w_att[n, width : 3 * width]
            ).astype(HALF)
        memory_back(row).start()
        for j in range(width // 256):
            n = slice(j * 256, (j + 1) * 256)
            res[at, n] = dot_outer(qkv_cross[at, :width], w_att[n, :width])

    def load_x_again():
        return copy_in(v.inputs, qkv_cross.at[:, pl.ds(0, width)], 0)

    @pl.when(encoder)
    def _():
        load_x_again().start()

    @pl.when(decoder)
    def _():
        for copy in load_cross():
            copy.start()
        load_cross_out().start()
        for copy in load_cross():
            copy.wait()
        load_cross_out().wait()
        repeat(rows, decoder_row)
        load_att().start()
        load_out().start()
        weight_gradient(CROSS, 0, mix_cross, low, 0)

        def gained(b):
            at = pl.ds(at128(b, 128), 128)
            low_t[:, at] = (unit_mid[at, :].astype(FULL) * cross_gain).astype(HALF).T

        repeat(tokens // 128, gained)
        add_first(CROSS, 0)
        advance(decoder_line, 0)
        weight_gradient(CROSS, 1, low_t, qkv_cross, 0)
        advance(decoder_line, 1)
        for row in range(rows):
            transpose_rows(low_t, x_recv, row)
        add_first(CROSS, 1)
        weight_gradient(CROSS, 2, low_t, qkv_cross, width)
        advance(decoder_line, 2)
        add_first(CROSS, 2)
        weight_gradient(CROSS, 3, low_t, qkv_cross, 2 * width)
        advance(decoder_line, 3)
        load_x_again().start()
        for row in range(rows):
            norm_back(as_full(res), as_full(unit_mid), row, 2, cross_gain, 2, as_full(grad), low)
        add_first(CROSS, 3)
        load_att().wait()
        load_out().wait()

    load_x_again().wait()

    def unit_self(at):
        return qkv_cross[at, :width].astype(FULL) * inverse[at, 0:1]

    def backward_row(row):
        at = row_slice(row)

        @pl.when(encoder)
        def _():
            memory_back(row).wait_recv()

            def memory_grads(at):
                return cot[at, :].astype(FULL) + x_recv[at, :].astype(FULL)

            norm_back(memory_grads, as_full(unit_mid), row, 2, final_gain, 2, None, cot)
            feed_forward(row, False, True, res, 0, encoder_unit, row + 1 < rows)
            norm_back(as_full(res), as_full(unit_ffn), row, 1, ffn_gain, 1, as_full(grad), low)

        def ticks(first, count):
            @pl.when(encoder & (row == rows - 1))
            def _():
                for j in range(first, first + count):
                    advance(encoder_line, j)

            @pl.when(decoder & (row == 0))
            def _():
                for j in range(first, first + count):
                    advance(decoder_line, DECODER_TICKS + j)

        back_through_out(row)
        ticks(0, 1)
        attend_back(qkv_self, self_probs, row, True)
        ticks(1, PAIRS - 1)

        @pl.when(decoder & (row == rows - 1))
        def _():
            advance(decoder_line, DECODER_TICKS + PAIRS)

        for j in range(width // 256):
            n = slice(j * 256, (j + 1) * 256)
            res[at, n] = dot_outer(qkv_self[at, :], w_att[n, :])
        norm_back(as_full(res), unit_self, row, 0, attn_gain, 0, as_full(grad), None)

    repeat(rows, backward_row)
    write_grad = pltpu.make_async_copy(grad, v.grad_inputs, sem_out.at[1])
    write_grad.start()
    weight_gradient(SELF, 0, mix_self, low, 0)

    def gained_self(b):
        at = pl.ds(at128(b, 128), 128)
        low_t[:, at] = (unit_self(at) * attn_gain).astype(HALF).T

    repeat(tokens // 128, gained_self)
    for item in range(1, 4):
        weight_gradient(SELF, item, low_t, qkv_self, (item - 1) * width)
    for item in range(4):
        add_first(SELF, item)
    by_bucket = lax.dot_general(
        sums[...],
        v.summed[section].astype(FULL),
        (((1,), (1,)), ((), ())),
        precision=PRECISE,
        preferred_element_type=FULL,
    )
    if reduce:
        misc[:, width:] = misc[:, :128]
        by_bucket = jnp.concatenate([by_bucket, jnp.zeros((16, 128 - NBUCKET), FULL)], 1)
        for shard in range(16):
            place = block_place(shard // 4, (shard // 2) % 2, shard % 2)
            turned = pltpu.roll(misc[...], (width + 128 - shard * ways_rows) % (width + 128), 1)
            block = jnp.concatenate([turned[:, :128], by_bucket, jnp.zeros((8, 128), FULL)], 0)
            v.own4[0, place * 32 : (place + 1) * 32, :] = block.astype(HALF)
        begin(SMALL, 0)
        add_first(SMALL, 0)

    def drain(line, done):
        for n in range(done, len(line) + 2):
            advance(line, n)

    @pl.when(encoder)
    def _():
        drain(encoder_line, PAIRS)

    @pl.when(decoder)
    def _():
        drain(decoder_line, DECODER_TICKS + PAIRS + 1)

    if not reduce:
        misc[8:24, :NBUCKET] = by_bucket
        outs = pltpu.make_async_copy(misc, v.out_misc, sem_out.at[2])
        outs.start()
    for name in [GATE_UP, DOWN, SELF] + ([SMALL] if reduce else []):
        repeat(by_name[name].count, functools.partial(finish, name))

    @pl.when(decoder)
    def _():
        repeat(by_name[CROSS].count, functools.partial(finish, CROSS))

    if reduce:

        @pl.when(encoder)
        def _():
            repeat(by_name[CROSS].count, lambda i: cross_over(CROSS, i, i).wait_recv())

        cross_over(SMALL, 0, 1 - section).wait_recv()
    else:
        outs.wait()
    write_grad.wait()

    @pl.when(encoder)
    def _():
        for row in range(rows):
            memory_copy(row).wait_send()
            write_layer(row).wait()

    @pl.when(decoder)
    def _():
        for row in range(rows):
            memory_back(row).wait_send()


def run_layers(args, ways):
    (
        inputs,
        cotangent,
        enc_segments,
        dec_segments,
        rel_bias,
        attn_norm,
        ffn_norm,
        w_qkv,
        w_attn_out,
        w_gate_up,
        w_down,
        cross_norm,
        cross_query,
        cross_kv,
        cross_out,
        final_norm,
    ) = args
    _, rows, length, width = inputs.shape
    hidden = w_down.shape[1]
    tokens = rows * length
    reduce = ways == 16
    spread, summed = bucket_tables(length)
    operands = dict(
        inputs=inputs.reshape(tokens, width),
        cotangent=cotangent.reshape(tokens, width),
        w_qkv=w_qkv,
        w_attn_out=w_attn_out,
        w_gate_up=w_gate_up,
        w_down=w_down,
        cross_query=cross_query,
        cross_kv=cross_kv,
        cross_out=cross_out,
    )
    small = dict(
        enc_segments=enc_segments,
        dec_segments=dec_segments,
        rel_bias=rel_bias,
        attn_norm=attn_norm,
        ffn_norm=ffn_norm,
        mid_norms=jnp.stack([cross_norm, final_norm]),
        spread=jnp.asarray(spread, HALF),
        summed=jnp.asarray(summed, HALF),
    )
    block = width // 16
    groups = [
        Group(GATE_UP, hidden // CHUNK, block, 2 * CHUNK),
        Group(DOWN, 3, hidden // 16, 256),
        Group(CROSS, 4, block, width),
        Group(SELF, 4, block, width),
    ]
    outs = dict(
        layer_out=((tokens, width), HALF),
        grad_inputs=((tokens, width), FULL),
    )
    if reduce:
        groups.append(Group(SMALL, 1, 32, 128))
    for g in groups:
        outs[f"out{g.name}"] = ((g.count, g.rows if reduce else 16 * g.rows, g.cols), HALF)
    if reduce:
        outs[f"out{SMALL}"] = ((2, 32, 128), HALF)
    else:
        outs[MISC] = ((24, width + 128), FULL)
    scratch = dict(
        x_send=pltpu.VMEM((tokens, width), HALF),
        x_recv=pltpu.VMEM((tokens, width), HALF),
        low=pltpu.VMEM((tokens, width), HALF),
        low_t=pltpu.VMEM((width, tokens), HALF),
        unit_ffn=pltpu.VMEM((tokens, width), HALF),
        unit_mid=pltpu.VMEM((tokens, width), HALF),
        cot=pltpu.VMEM((tokens, width), HALF),
        res=pltpu.VMEM((tokens, width), FULL),
        grad=pltpu.VMEM((tokens, width), FULL),
        w_att=pltpu.VMEM((width, 3 * width), HALF),
        w_out=pltpu.VMEM((width, width), HALF),
        qkv_self=pltpu.VMEM((tokens, 3 * width), HALF),
        qkv_cross=pltpu.VMEM((tokens, 3 * width), HALF),
        mix_self=pltpu.VMEM((width, tokens), HALF),
        mix_cross=pltpu.VMEM((width, tokens), HALF),
        probs=pltpu.VMEM((H * rows, length, length), HALF),
        big=pltpu.VMEM((4, width, width), HALF),
        inverse=pltpu.VMEM((tokens, 8), FULL),
        mask=pltpu.VMEM((length, length), HALF),
        near=pltpu.VMEM((length, length), HALF),
        past=pltpu.VMEM((length, length), HALF),
        flip=pltpu.VMEM((length, length), HALF),
        grad_mix=pltpu.VMEM((length, width), HALF),
        segments=pltpu.VMEM((8, length), jnp.int32),
        table=pltpu.VMEM((16, 2 * length), FULL),
        sums=pltpu.VMEM((16, 2 * length), FULL),
        misc=pltpu.VMEM((8 if reduce else 24, width + 128), FULL),
        load=pltpu.SemaphoreType.DMA((5 + 5 * RING,)),
        sem_x=pltpu.SemaphoreType.DMA((4, rows)),
        sem_out=pltpu.SemaphoreType.DMA((4 + rows,)),
    )
    for g in groups:
        if g.name != SELF:
            scratch[f"own{g.name}"] = pltpu.VMEM((g.count, 16 * g.rows, g.cols), HALF)
        if reduce:
            for stage in range(4):
                scratch[f"came{stage}x{g.name}"] = pltpu.VMEM((g.count, (8 >> stage) * g.rows, g.cols), HALF)
        scratch[f"sem{g.name}"] = pltpu.SemaphoreType.DMA((g.count, 11))
    names = list(operands) + list(small) + list(outs) + list(scratch)
    results = pl.pallas_call(
        functools.partial(layer_kernel, names, groups, reduce, rows, length, width, hidden),
        out_shape=[jax.ShapeDtypeStruct(*out) for out in outs.values()],
        in_specs=[pl.BlockSpec(memory_space=pl.ANY)] * len(operands)
        + [pl.BlockSpec(memory_space=pltpu.VMEM)] * len(small),
        out_specs=[pl.BlockSpec(memory_space=pl.ANY)] * len(outs),
        scratch_shapes=list(scratch.values()),
        compiler_params=pltpu.CompilerParams(
            collective_id=1, has_side_effects=True, vmem_limit_bytes=VMEM_LIMIT
        ),
    )(*operands.values(), *small.values())
    return dict(zip(outs, results)), reduce


LAYER, INPUT, MISC = "layer_out", "grad_inputs", "out_misc"
VMEM_LIMIT = 64 * 2**20 - 64 * 2**10


def finish_kernel(width, pair, lower, cross, own, small, layer, grad, *refs):
    layer_out, grad_out, qkv, attn_out, gate_up, down, attn, ffn, query, kv, outer, mid, final, rel = refs[:14]
    layer_held, grad_held, sem = refs[14:]
    through = [(layer, layer_held, layer_out), (grad, grad_held, grad_out)]
    arriving = [pltpu.make_async_copy(a, b, sem.at[n]) for n, (a, b, _) in enumerate(through)]
    leaving = [pltpu.make_async_copy(b, c, sem.at[2 + n]) for n, (_, b, c) in enumerate(through)]
    for copy in arriving:
        copy.start()
    for came, copy in zip(arriving, leaving):
        came.wait()
        copy.start()
    chunks = pair.shape[0]
    for k in range(chunks):
        gate_up[:, k * CHUNK : (k + 1) * CHUNK] = pair[k, :, :CHUNK].astype(FULL)
        up = (chunks + k) * CHUNK
        gate_up[:, up : up + CHUNK] = pair[k, :, CHUNK:].astype(FULL)
    for j in range(3):
        down[:, j * 256 : (j + 1) * 256] = lower[j].astype(FULL)
        qkv[:, j * width : (j + 1) * width] = own[1 + j].astype(FULL)
    attn_out[...] = own[0].astype(FULL)
    outer[...] = cross[0].astype(FULL)
    query[...] = cross[1].astype(FULL)
    for j in range(2):
        kv[:, j * width : (j + 1) * width] = cross[2 + j].astype(FULL)
    block = attn.shape[1]
    mine = small[lax.axis_index("section")].astype(FULL)
    attn[...] = mine[0:1, :block]
    ffn[...] = mine[1:2, :block]
    encoder, decoder = small[0].astype(FULL), small[1].astype(FULL)
    mid[...] = decoder[2:3, :block]
    final[...] = encoder[2:3, :block]
    rel[...] = (encoder[8:24] + decoder[8:24]).T[:NBUCKET, :H]
    for copy in leaving:
        copy.wait()


def finished(out, inputs, hidden):
    tokens, width = out[LAYER].shape
    block = width // 16
    shapes = [(out[LAYER].shape, HALF), (out[INPUT].shape, FULL)] + [
        (shape, FULL)
        for shape in [
            (block, 3 * width),
            (block, width),
            (block, 2 * hidden),
            (hidden // 16, width),
            (1, block),
            (1, block),
            (block, width),
            (block, 2 * width),
            (block, width),
            (1, block),
            (1, block),
            (NBUCKET, H),
        ]
    ]
    layer, grad, qkv, attn_out, gate_up, down, attn, ffn, query, kv, outer, mid, final, rel = pl.pallas_call(
        functools.partial(finish_kernel, width),
        out_shape=[jax.ShapeDtypeStruct(*shape) for shape in shapes],
        in_specs=[pl.BlockSpec(memory_space=pltpu.VMEM)] * 5 + [pl.BlockSpec(memory_space=pl.ANY)] * 2,
        out_specs=[pl.BlockSpec(memory_space=pl.ANY)] * 2 + [pl.BlockSpec(memory_space=pltpu.VMEM)] * 12,
        scratch_shapes=[
            pltpu.VMEM(out[LAYER].shape, HALF),
            pltpu.VMEM(out[INPUT].shape, FULL),
            pltpu.SemaphoreType.DMA((4,)),
        ],
        compiler_params=pltpu.CompilerParams(vmem_limit_bytes=VMEM_LIMIT),
    )(*[out[f"out{name}"] for name in range(5)], out[LAYER], out[INPUT])
    return (
        layer.reshape(inputs.shape),
        grad.reshape(inputs.shape),
        qkv[None],
        attn_out[None],
        gate_up[None],
        down[None],
        attn,
        ffn,
        query,
        kv,
        outer,
        mid.reshape(block),
        final.reshape(block),
        rel,
    )


def shards(*args):
    inputs = args[0]
    ways = lax.axis_size("dp")
    width = inputs.shape[3]
    hidden = args[10].shape[1]
    out, reduce = run_layers(args, ways)
    if reduce:
        return finished(out, inputs, hidden)

    def wide(name):
        value = out[f"out{name}"]
        total = lax.psum_scatter(value, "dp", scatter_dimension=1, tiled=True)
        if name == CROSS:
            total = lax.psum(jnp.where(lax.axis_index("section") == 1, total, 0), "section")
        return total.astype(FULL)

    def side_by_side(value):
        return jnp.swapaxes(value, 0, 1).reshape(value.shape[1], -1)

    gate_up = wide(GATE_UP)
    chunks, block, _ = gate_up.shape
    gate_up = gate_up.reshape(chunks, block, 2, CHUNK).transpose(1, 2, 0, 3).reshape(block, 2 * hidden)
    down, cross, late = wide(DOWN), wide(CROSS), wide(SELF)
    own = lax.psum(out[MISC], "dp")
    misc = lax.all_gather(own, "section", axis=0)
    start = lax.axis_index("dp") * block

    def piece(vector):
        return lax.dynamic_slice_in_dim(vector, start, block, 0)

    return (
        out[LAYER].reshape(inputs.shape),
        out[INPUT].reshape(inputs.shape),
        side_by_side(late[1:])[None],
        late[0][None],
        gate_up[None],
        side_by_side(down)[None],
        piece(own[0, :width])[None],
        piece(own[1, :width])[None],
        cross[1],
        side_by_side(cross[2:]),
        cross[0],
        piece(misc[1, 2, :width]),
        piece(misc[0, 2, :width]),
        (misc[0] + misc[1])[8 : 8 + H, :NBUCKET].T,
    )


def solution(mesh):
    layer = P("section", "dp", None, None)
    matrix = P("section", None, None)
    return jax.shard_map(
        shards,
        mesh=mesh,
        in_specs=(layer, layer, P("dp", None), P("dp", None), P())
        + (P("section", None),) * 2
        + (matrix,) * 4
        + (P(),) * 5,
        out_specs=(layer, layer)
        + (P("section", "dp", None),) * 4
        + (P("section", "dp"),) * 2
        + (P("dp", None),) * 3
        + (P("dp"),) * 2
        + (P(),),
        check_vma=False,
    )
```

```python
import functools
import math
import types

import jax
import jax.numpy as jnp
import numpy as np
from jax import lax
from jax.experimental import pallas as pl
from jax.experimental.pallas import tpu as pltpu
from jax.sharding import PartitionSpec as P

H = 12
HD = 64
NBUCKET = 32
MAXDIST = 128
EPSILON = 1e-06
MASKED = -1000000000.0
MESH = pl.DeviceIdType.MESH
PRECISE = lax.Precision.HIGHEST
HALF = jnp.bfloat16
FULL = jnp.float32
PAIRS = H // 2
CHUNK = 256
BLOCK = 64
RING = 4
DECODER_TICKS = 4
GATE_UP, DOWN, CROSS, SELF, SMALL = range(5)
GELU_SCALE = math.sqrt(2.0 / math.pi)
GELU_CUBE = 0.044715


def bucket_of(offsets, causal, buckets, reach_max):
    if causal:
        half_count = buckets
        side_offset = offsets * 0
        distance = np.maximum(-offsets, 0)
    else:
        half_count = buckets // 2
        side_offset = (offsets > 0).astype(np.int32) * half_count
        distance = np.abs(offsets)
    exact_count = half_count // 2
    clipped = np.maximum(distance, exact_count)
    spread = exact_count + np.floor(
        np.log(clipped / exact_count) / np.log(reach_max / exact_count) * (half_count - exact_count)
        + 1e-09
    ).astype(np.int32)
    spread = np.minimum(spread, half_count - 1)
    return (side_offset + np.where(distance < exact_count, distance, spread)).astype(np.int32)


def bucket_tables(length):
    lane = np.arange(length)
    spread = np.concatenate([-lane, length - lane])
    summed = np.concatenate([-(lane + 1), length - 1 - lane])
    tables = []
    for offsets in (spread, summed):
        clipped = np.clip(offsets, -(length - 1), length - 1)
        tables.append(
            np.stack(
                [
                    (bucket_of(clipped, causal, NBUCKET, MAXDIST)[None] == np.arange(NBUCKET)[:, None])
                    for causal in (False, True)
                ]
            ).astype(np.float32)
        )
    return tables


def dot(left, right):
    return jnp.dot(left, right, preferred_element_type=FULL)


def dot_outer(left, right):
    return lax.dot_general(left, right, (((1,), (1,)), ((), ())), preferred_element_type=FULL)


def repeat(count, step):
    def body(index, carry):
        step(index)
        return carry

    lax.fori_loop(0, count, body, 0)


def at128(index, scale):
    return pl.multiple_of(index * scale, 128)


class Group:
    def __init__(self, name, count, rows, cols):
        self.name, self.count, self.rows, self.cols = name, count, rows, cols


def layer_kernel(names, groups, reduce, rows, length, width, hidden, *refs):
    v = types.SimpleNamespace(**dict(zip(names, refs)))
    tokens = rows * length
    chunks = hidden // CHUNK
    ways_rows = width // 16
    me, section = lax.axis_index("dp"), lax.axis_index("section")
    encoder, decoder = section == 0, section == 1
    z, y, c = me // 4, (me // 2) % 2, me % 2
    other = (1 - section, me)

    x_send, x_recv = v.x_send, v.x_recv
    low, low_t, grad_mix = v.low, v.low_t, v.grad_mix
    joint, units = grad_mix.at[:, : 2 * CHUNK], grad_mix.at[:, 2 * CHUNK : 3 * CHUNK]
    unit_ffn, unit_mid, cot = v.unit_ffn, v.unit_mid, v.cot
    res, grad = v.res, v.grad
    w_att, w_out = v.w_att, v.w_out
    qkv_self, qkv_cross = v.qkv_self, v.qkv_cross
    mix_self, mix_cross = v.mix_self, v.mix_cross
    probs, big = v.probs, v.big
    inverse, table, sums, mask = v.inverse, v.table, v.sums, v.mask
    misc = v.misc
    load, sem_x, sem_out = v.load, v.sem_x, v.sem_out

    def device(zz, yy, cc):
        return (section, zz * 4 + yy * 2 + cc)

    z_low, z_high = z % 2, z // 2
    near_y, near_z = device(z, 1 - y, c), device(z + 1 - 2 * z_low, y, c)
    sibling, far_z = device(z, y, 1 - c), device(z + 2 - 4 * z_high, y, c)
    partners = [other] + ([sibling, near_y, near_z, far_z] if reduce else [])
    barrier = pltpu.get_barrier_semaphore()
    for target in partners:
        pl.semaphore_signal(barrier, inc=1, device_id=target, device_id_type=MESH)

    def copy_in(source, target, slot):
        return pltpu.make_async_copy(source, target, load.at[slot])

    def load_x():
        return copy_in(v.inputs, x_send, 0)

    def load_cot():
        return copy_in(v.cotangent, cot, 1)

    def load_att():
        return copy_in(v.w_qkv.at[0], w_att, 2)

    def load_out():
        return copy_in(v.w_attn_out.at[0], w_out, 3)

    def load_cross():
        return [
            copy_in(v.cross_query, w_att.at[:, pl.ds(0, width)], 2),
            copy_in(v.cross_kv, w_att.at[:, pl.ds(width, 2 * width)], 4),
        ]

    def load_cross_out():
        return copy_in(v.cross_out, w_out, 3)

    ring = v.own2

    def load_chunk(index):
        slot = index % RING
        at = at128(index, CHUNK)
        pieces = [
            copy_in(
                v.w_down.at[0, pl.ds(at, CHUNK), pl.ds(j * 256, 256)],
                ring.at[slot, pl.ds(j * 256, 256), pl.ds(2 * CHUNK, 256)],
                7 + j + 5 * slot,
            )
            for j in range(width // 256)
        ]
        return pieces + [
            copy_in(
                v.w_gate_up.at[0, :, pl.ds(at, CHUNK)], ring.at[slot, :, pl.ds(0, CHUNK)], 5 + 5 * slot
            ),
            copy_in(
                v.w_gate_up.at[0, :, pl.ds(pl.multiple_of(hidden + at, 128), CHUNK)],
                ring.at[slot, :, pl.ds(CHUNK, CHUNK)],
                6 + 5 * slot,
            ),
        ]

    load_x().start()
    load_att().start()
    load_out().start()
    load_cot().start()
    misc[...] = jnp.zeros_like(misc)
    sums[...] = jnp.zeros_like(sums)
    for k in range(RING - 1):
        for copy in load_chunk(k):
            copy.start()

    by_name = {group.name: group for group in groups}
    stacks = {
        group.name: (big if group.name == SELF else getattr(v, f"own{group.name}")) for group in groups
    }

    def block_place(zz, yy, cc):
        return cc * 8 + yy * 4 + (zz % 2) * 2 + zz // 2

    def put(name, item, columns, tile):
        own, r = stacks[name], by_name[name].rows
        low_tile = tile.astype(HALF)
        for shard in range(16):
            place = shard
            if reduce:
                place = block_place(shard // 4, (shard // 2) % 2, shard % 2)
            own[item, place * r : (place + 1) * r, columns] = low_tile[
                shard * r : (shard + 1) * r
            ]

    def stages(name):
        result, base, count = [], 0, 16 * by_name[name].rows
        for bit, target in ((c, sibling), (y, near_y), (z_low, near_z), (z_high, far_z)):
            count = count // 2
            sent, base = base + (1 - bit) * count, base + bit * count
            result.append((target, pl.multiple_of(sent, 16), pl.multiple_of(base, 16), count))
        return result

    def exchange(name, i, stage):
        target, sent, _, count = stages(name)[stage]
        sems = getattr(v, f"sem{name}")
        return pltpu.make_async_remote_copy(
            stacks[name].at[i, pl.ds(sent, count)],
            getattr(v, f"came{stage}x{name}").at[i],
            sems.at[i, 2 * stage],
            sems.at[i, 2 * stage + 1],
            device_id=target,
            device_id_type=MESH,
        )

    def kept_rows(name):
        _, _, kept, count = stages(name)[3]
        return pl.ds(kept, count)

    def write_out(name, i):
        source = stacks[name].at[i, kept_rows(name)] if reduce else stacks[name].at[i]
        place = section if name == SMALL else i
        return pltpu.make_async_copy(
            source, getattr(v, f"out{name}").at[place], getattr(v, f"sem{name}").at[i, 8]
        )

    def cross_over(name, i, place):
        sems = getattr(v, f"sem{name}")
        return pltpu.make_async_remote_copy(
            stacks[name].at[i, kept_rows(name)],
            getattr(v, f"out{name}").at[place],
            sems.at[i, 9],
            sems.at[i, 10],
            device_id=other,
            device_id_type=MESH,
        )

    def begin(name, i):
        if reduce:
            exchange(name, i, 0).start()
        else:
            write_out(name, i).start()

    def add(name, i, stage):
        if not reduce:
            return
        own, came = stacks[name], getattr(v, f"came{stage}x{name}")
        exchange(name, i, stage).wait_recv()
        _, _, kept, count = stages(name)[stage]
        size = min(count, 2 * by_name[name].rows)

        def step(m):
            at = pl.ds(pl.multiple_of(kept + m * size, 16), size)
            own[i, at] = own[i, at] + came[i, pl.ds(pl.multiple_of(m * size, 16), size)]

        repeat(count // size, step)
        if stage < 3:
            exchange(name, i, stage + 1).start()
        else:
            write_out(name, i).start()
            if name == CROSS:
                cross_over(name, i, i).start()
            if name == SMALL:
                cross_over(name, i, section).start()

    def add_first(name, i):
        add(name, i, 0)

    def finish(name, i):
        write_out(name, i).wait()
        if reduce:
            for stage in range(4):
                exchange(name, i, stage).wait_send()
            if name in (CROSS, SMALL):
                cross_over(name, i, i).wait_send()

    def items_of(*names):
        return [(name, i) for name in names for i in range(by_name[name].count)]

    last = items_of(SELF, SMALL) if reduce else items_of(SELF)
    encoder_line = items_of(GATE_UP, DOWN) + last
    decoder_line = items_of(GATE_UP, DOWN, CROSS) + last

    def advance(line, n):
        for stage in (1, 2, 3):
            if 0 <= n + 1 - stage < len(line):
                add(*line[n + 1 - stage], stage)

    def block_of(ref, b):
        return ref.at[b // 9, pl.ds(at128((b % 9) // 3, 256), 256), pl.ds(at128(b % 3, 256), 256)]

    def decoder_unit(k):
        return block_of(big, H + 2 * chunks + k)

    def encoder_unit(k):
        lanes = pl.ds(pl.multiple_of(width + k // 2 * CHUNK, 128), CHUNK)
        return qkv_cross.at[pl.ds(at128(k % 2, length), length), lanes]

    def self_probs(head, row):
        return probs.at[head * rows + row]

    def cross_probs(head, row):
        return block_of(big, head)

    def row_slice(row):
        return pl.ds(pl.multiple_of(row * length, length), length)

    def part_slice(row, b, size):
        return pl.ds(pl.multiple_of(row * length + b * size, size), size)

    lanes = lax.broadcasted_iota(jnp.int32, (1, 128), 1)
    half_lanes = [(lanes < HD).astype(HALF), (lanes >= HD).astype(HALF)]

    def make_mask(key_segments, query_segments, row, causal):
        keys = key_segments[pl.ds(row, 1), :].astype(FULL)
        keys = jnp.broadcast_to(keys, (8, length)).T[:, :1]
        queries = query_segments[pl.ds(row, 1), :].astype(FULL)
        same = keys == queries
        if causal is not None:
            key_at = lax.broadcasted_iota(jnp.int32, (length, length), 0)
            query_at = lax.broadcasted_iota(jnp.int32, (length, length), 1)
            same = same & ((key_at <= query_at) | causal)
        mask[...] = jnp.where(same, 0.0, MASKED).astype(HALF)

    def lanes_of(offset, hp):
        return pl.ds(pl.multiple_of(offset + hp * 128, 128), 128)

    def attend(qkv, probs_of, mix, row, with_bias):
        at = row_slice(row)

        def pair(hp):
            queries = qkv[at, lanes_of(0, hp)]
            keys = qkv[at, lanes_of(width, hp)]
            values_t = qkv[at, lanes_of(2 * width, hp)].T
            both = jnp.concatenate([keys * half_lanes[0], keys * half_lanes[1]], 0)
            scores = dot_outer(both, queries)
            for e in range(2):
                if with_bias:
                    line = table[pl.ds(hp * 2 + e, 1), :]
                    skewed = line[:, length:] + v.near[...].astype(FULL) * (line[:, :length] - line[:, length:])
                    bias = pltpu.roll(skewed, 0, 1, stride=1, stride_axis=0)
                soft_parts = []
                for part in range(length // 128):
                    n = slice(part * 128, (part + 1) * 128)
                    shifted = scores[e * length : (e + 1) * length, n] + mask[:, n].astype(FULL)
                    if with_bias:
                        shifted = shifted + bias[:, n]
                    raised = jnp.exp(shifted - jnp.max(shifted, 0, keepdims=True))
                    total = jnp.sum(raised, 0, keepdims=True)
                    soft_parts.append((raised * (1.0 / total)).astype(HALF))
                softmaxed = jnp.concatenate(soft_parts, 1)
                probs_of(hp * 2 + e, row)[...] = softmaxed
                mixed = dot(values_t[e * HD : (e + 1) * HD], softmaxed)
                mix[pl.ds(pl.multiple_of(hp * 128 + e * HD, 16), HD), at] = mixed.astype(HALF)

        for hp in range(PAIRS):
            pair(hp)

    def attend_back(qkv, probs_of, row, with_bias):
        at = row_slice(row)
        left = lax.broadcasted_iota(jnp.int32, (length, 128), 1) < HD
        def pair(hp):
            q_lanes, k_lanes, v_lanes = lanes_of(0, hp), lanes_of(width, hp), lanes_of(2 * width, hp)
            queries, keys, values = qkv[at, q_lanes], qkv[at, k_lanes], qkv[at, v_lanes]
            outer = grad_mix[:, q_lanes]
            keys_t = keys.T
            both = jnp.concatenate([values * half_lanes[0], values * half_lanes[1]], 0)
            grad_soft = dot_outer(both, outer)
            softs, scores = [], []
            for e in range(2):
                soft_low = probs_of(hp * 2 + e, row)[...]
                score_parts = []
                for part in range(length // 128):
                    n = slice(part * 128, (part + 1) * 128)
                    soft = soft_low[:, n].astype(FULL)
                    weighted = soft * grad_soft[e * length : (e + 1) * length, n]
                    shared = jnp.sum(weighted, 0, keepdims=True)
                    score_parts.append((weighted - soft * shared).astype(HALF))
                scores.append(jnp.concatenate(score_parts, 1))
                softs.append(soft_low)
            grad_keys = dot(jnp.concatenate(scores, 0), queries)
            grad_values = dot(jnp.concatenate(softs, 0), outer)
            left_side = jnp.concatenate([keys_t, v.flip[...]], 0) if with_bias else keys_t
            parts = []
            for e in range(2):
                product = dot(left_side, scores[e])
                parts.append(product[e * HD : (e + 1) * HD])
                if with_bias:
                    aligned = pltpu.roll(product[128:], 0, 1, stride=1, stride_axis=0)
                    before = jnp.sum(aligned * v.past[...].astype(FULL), 0, keepdims=True)
                    after = jnp.sum(aligned, 0, keepdims=True) - before
                    line = pl.ds(hp * 2 + e, 1)
                    sums[line, :] = sums[line, :] + jnp.concatenate([before, after], 1)
            qkv[at, q_lanes] = jnp.concatenate(parts, 0).T.astype(HALF)
            qkv[at, k_lanes] = jnp.where(left, grad_keys[:length], grad_keys[length:]).astype(HALF)
            qkv[at, v_lanes] = jnp.where(left, grad_values[:length], grad_values[length:]).astype(HALF)

        for hp in range(PAIRS):
            pair(hp)

    def normalise(load_rows, row, column, gain, unit_ref, target):
        for b in range(length // BLOCK):
            at = part_slice(row, b, BLOCK)
            value = load_rows(at)
            scale = lax.rsqrt(jnp.mean(value * value, -1, keepdims=True) + EPSILON)
            inverse[at, column : column + 1] = scale
            unit = value * scale
            if unit_ref is not None:
                unit_ref[at, :] = unit.astype(HALF)
            target[at, :] = (unit * gain).astype(HALF)

    def norm_back(load_grad, load_unit, row, column, gain, misc_row, load_base, low_ref):
        def step(b, gain_sum):
            at = part_slice(row, b, BLOCK)
            normed, unit = load_grad(at), load_unit(at)
            weighted = normed * unit
            grad_unit = normed * gain
            scale = inverse[at, column : column + 1]
            inner = jnp.mean(weighted * gain, -1, keepdims=True)
            result = scale * (grad_unit - unit * inner)
            if load_base is not None:
                result = result + load_base(at)
            grad[at, :] = result
            if low_ref is not None:
                low_ref[at, :] = result.astype(HALF)
            return gain_sum + jnp.sum(weighted.reshape(BLOCK // 8, 8, width), 0)

        gain_sum = lax.fori_loop(0, length // BLOCK, step, jnp.zeros((8, width), FULL))
        line = slice(misc_row, misc_row + 1)
        misc[line, :width] = misc[line, :width] + jnp.sum(gain_sum, 0, keepdims=True)

    def transpose_rows(target, source, row):
        for b in range(length // 128):
            at = part_slice(row, b, 128)
            target[:, at] = source[at, :].T

    def transpose_back(target, source, row):
        for b in range(length // 128):
            at = part_slice(row, b, 128)
            target[at, :] = source[:, at].T

    def add_projection(weights, base, row):
        at = row_slice(row)
        for j in range(width // 256):
            n = slice(j * 256, (j + 1) * 256)
            res[at, n] = base[at, n].astype(FULL) + dot(low[at, :], weights[:, n])

    def feed_forward(row, forward, backward, total, base, unit_block, more):
        at = row_slice(row)
        if backward:
            total[at, :] = jnp.zeros((length, width), FULL)

        def step(k):
            slot = k % RING
            pair_weights = ring.at[slot, :, : 2 * CHUNK]
            lower = [ring.at[slot, j * 256 : (j + 1) * 256, 2 * CHUNK :] for j in range(width // 256)]

            @pl.when((k + RING - 1 < chunks) | more)
            def _():
                for copy in load_chunk((k + RING - 1) % chunks):
                    copy.start()

            for copy in load_chunk(k):
                copy.wait()
            kept = [block_of(big, row * 2 * chunks + k * 2 + side) for side in range(2)]
            if forward:
                joined = dot(low[at, :], pair_weights[...])
                gate, up = joined[:, :CHUNK], joined[:, CHUNK:]
                if not backward:
                    kept[0][...] = gate.astype(HALF)
                    kept[1][...] = up.astype(HALF)
            else:
                gate, up = kept[0][...].astype(FULL), kept[1][...].astype(FULL)
            squared = gate * gate
            curve = jnp.tanh(gate * (GELU_SCALE + GELU_SCALE * GELU_CUBE * squared))
            rising = 0.5 + 0.5 * curve
            bent = gate * rising
            unit = (bent * up).astype(HALF)
            if forward:
                for j in range(width // 256):
                    n = slice(j * 256, (j + 1) * 256)
                    res[at, n] = res[at, n] + dot(unit, lower[j][...])
            if not backward:
                return
            grad_hidden = sum(
                dot_outer(cot[at, j * 256 : (j + 1) * 256], lower[j][...]) for j in range(width // 256)
            )
            slope = rising + 0.5 * gate * (1.0 - curve * curve) * (
                GELU_SCALE + 3.0 * GELU_SCALE * GELU_CUBE * squared
            )
            pair = jnp.concatenate(
                [(grad_hidden * up * slope).astype(HALF), (grad_hidden * bent).astype(HALF)], 1
            )
            total[at, :] = total[at, :] + dot_outer(pair, pair_weights[...])
            joint[...] = pair
            units[...] = unit.T
            first = [block_of(big, base + k * 2 + side) for side in range(2)]

            @pl.when(row == 0)
            def _():
                first[0][...] = joint[:, :CHUNK]
                first[1][...] = joint[:, CHUNK:]
                unit_block(k)[...] = units[...]

            @pl.when(row == rows - 1)
            def _():
                @pl.when(k > 0)
                def _():
                    add_first(GATE_UP, k - 1)

                for part in range(2):
                    columns = slice(part * CHUNK, (part + 1) * CHUNK)
                    right = jnp.concatenate([first[part][...], joint[:, columns]], 0)
                    put(GATE_UP, k, columns, dot(low_t[...], right))
                begin(GATE_UP, k)
                r = by_name[DOWN].rows
                both = jnp.concatenate([unit_block(k)[...], units[...]], 1)
                for part in range(3):
                    tile = dot(both, cot[:, part * 256 : (part + 1) * 256]).astype(HALF)
                    if reduce:
                        for shard in range(CHUNK // r):
                            place = block_place(k // 2, k % 2, shard)
                            v.own1[part, pl.ds(pl.multiple_of(place * r, 16), r)] = tile[
                                shard * r : (shard + 1) * r
                            ]
                    else:
                        v.own1[part, pl.ds(at128(k, CHUNK), CHUNK)] = tile

        repeat(chunks, step)
        if backward:

            @pl.when(row == rows - 1)
            def _():
                for part in range(3):
                    begin(DOWN, part)
                add_first(GATE_UP, chunks - 1)
                for part in range(3):
                    add_first(DOWN, part)

    def weight_gradient(name, item, left_t, right, at):
        for j in range(width // 256):
            n = slice(j * 256, (j + 1) * 256)
            put(name, item, n, dot(left_t[...], right[:, at + j * 256 : at + (j + 1) * 256]))
        begin(name, item)

    def back_through_out(row):
        for j in range(width // 256):
            n = slice(j * 256, (j + 1) * 256)
            grad_mix[:, n] = dot_outer(low[row_slice(row), :], w_out[n, :]).astype(HALF)

    def as_full(ref):
        return lambda at: ref[at, :].astype(FULL)

    def memory_copy(row):
        return pltpu.make_async_remote_copy(
            x_send.at[row_slice(row)],
            x_recv.at[row_slice(row)],
            sem_x.at[0, row],
            sem_x.at[1, row],
            device_id=other,
            device_id_type=MESH,
        )

    def memory_back(row):
        return pltpu.make_async_remote_copy(
            x_send.at[row_slice(row)],
            x_recv.at[row_slice(row)],
            sem_x.at[2, row],
            sem_x.at[3, row],
            device_id=other,
            device_id_type=MESH,
        )

    def write_layer(row):
        return pltpu.make_async_copy(
            x_send.at[row_slice(row)], v.layer_out.at[row_slice(row)], sem_out.at[4 + row]
        )

    ffn_gain = v.ffn_norm[...].astype(FULL)
    attn_gain = v.attn_norm[...].astype(FULL)
    cross_gain = v.mid_norms[...].astype(FULL)[0:1]
    final_gain = v.mid_norms[...].astype(FULL)[1:2]

    def enter_feed_forward(row):
        normalise(as_full(res), row, 1, ffn_gain, unit_ffn, low)
        transpose_rows(low_t, low, row)

    row_at = lax.broadcasted_iota(jnp.int32, (length, length), 0)
    lane_at = lax.broadcasted_iota(jnp.int32, (length, length), 1)
    v.near[...] = (lane_at + row_at < length).astype(FULL).astype(HALF)
    v.past[...] = (lane_at < row_at).astype(FULL).astype(HALF)
    v.flip[...] = (row_at + lane_at == length - 1).astype(FULL).astype(HALF)

    table[0:H, :] = lax.dot_general(
        v.rel_bias[...],
        v.spread[section].astype(FULL),
        (((0,), (0,)), ((), ())),
        precision=PRECISE,
        preferred_element_type=FULL,
    )
    segments = jnp.where(encoder, v.enc_segments[...], v.dec_segments[...])
    v.segments[0:rows, :] = segments
    load_x().wait()
    load_att().wait()
    load_out().wait()
    load_cot().wait()
    pl.semaphore_wait(barrier, len(partners))

    def forward_row(row):
        at = row_slice(row)
        normalise(as_full(x_send), row, 0, attn_gain, None, low)

        for j in range(3 * width // 256):
            n = slice(j * 256, (j + 1) * 256)
            qkv_self[at, n] = dot(low[at, :], w_att[:, n]).astype(HALF)
        make_mask(v.segments, v.segments, row, encoder)
        attend(qkv_self, self_probs, mix_self, row, True)
        transpose_back(low, mix_self, row)
        add_projection(w_out, x_send, row)

        @pl.when(encoder)
        def _():
            enter_feed_forward(row)
            feed_forward(row, True, False, None, 0, None, True)
            normalise(as_full(res), row, 2, final_gain, unit_mid, x_send)
            memory_copy(row).start()
            write_layer(row).start()

    repeat(rows, forward_row)

    def decoder_row(row):
        at = row_slice(row)
        normalise(as_full(res), row, 2, cross_gain, unit_mid, low)
        for j in range(width // 256):
            n = slice(j * 256, (j + 1) * 256)
            qkv_cross[at, n] = dot(low[at, :], w_att[:, n]).astype(HALF)
        make_mask(v.enc_segments, v.dec_segments, row, None)
        memory_copy(row).wait_recv()

        for j in range(width // 256, 3 * width // 256):
            n = slice(j * 256, (j + 1) * 256)
            qkv_cross[at, n] = dot(x_recv[at, :], w_att[:, n]).astype(HALF)
        attend(qkv_cross, cross_probs, mix_cross, row, False)
        transpose_back(low, mix_cross, row)
        add_projection(w_out, res, row)
        enter_feed_forward(row)
        feed_forward(row, True, True, grad, H, decoder_unit, row + 1 < rows)
        x_send[at, :] = res[at, :].astype(HALF)
        write_layer(row).start()
        norm_back(as_full(grad), as_full(unit_ffn), row, 1, ffn_gain, 1, as_full(cot), low)
        back_through_out(row)
        attend_back(qkv_cross, cross_probs, row, False)
        write_layer(row).wait()
        for j in range(width // 256):
            n = slice(j * 256, (j + 1) * 256)
            x_send[at, n] = dot_outer(
                qkv_cross[at, width : 3 * width], w_att[n, width : 3 * width]
            ).astype(HALF)
        memory_back(row).start()
        for j in range(width // 256):
            n = slice(j * 256, (j + 1) * 256)
            res[at, n] = dot_outer(qkv_cross[at, :width], w_att[n, :width])

    def load_x_again():
        return copy_in(v.inputs, qkv_cross.at[:, pl.ds(0, width)], 0)

    @pl.when(encoder)
    def _():
        load_x_again().start()

    @pl.when(decoder)
    def _():
        for copy in load_cross():
            copy.start()
        load_cross_out().start()
        for copy in load_cross():
            copy.wait()
        load_cross_out().wait()
        repeat(rows, decoder_row)
        load_att().start()
        load_out().start()
        weight_gradient(CROSS, 0, mix_cross, low, 0)

        def gained(b):
            at = pl.ds(at128(b, 128), 128)
            low_t[:, at] = (unit_mid[at, :].astype(FULL) * cross_gain).astype(HALF).T

        repeat(tokens // 128, gained)
        add_first(CROSS, 0)
        advance(decoder_line, 0)
        weight_gradient(CROSS, 1, low_t, qkv_cross, 0)
        advance(decoder_line, 1)
        for row in range(rows):
            transpose_rows(low_t, x_recv, row)
        add_first(CROSS, 1)
        weight_gradient(CROSS, 2, low_t, qkv_cross, width)
        advance(decoder_line, 2)
        add_first(CROSS, 2)
        weight_gradient(CROSS, 3, low_t, qkv_cross, 2 * width)
        advance(decoder_line, 3)
        load_x_again().start()
        for row in range(rows):
            norm_back(as_full(res), as_full(unit_mid), row, 2, cross_gain, 2, as_full(grad), low)
        add_first(CROSS, 3)
        load_att().wait()
        load_out().wait()

    load_x_again().wait()

    def unit_self(at):
        return qkv_cross[at, :width].astype(FULL) * inverse[at, 0:1]

    def backward_row(row):
        at = row_slice(row)

        @pl.when(encoder)
        def _():
            memory_back(row).wait_recv()

            def memory_grads(at):
                return cot[at, :].astype(FULL) + x_recv[at, :].astype(FULL)

            norm_back(memory_grads, as_full(unit_mid), row, 2, final_gain, 2, None, cot)
            feed_forward(row, False, True, res, 0, encoder_unit, row + 1 < rows)
            norm_back(as_full(res), as_full(unit_ffn), row, 1, ffn_gain, 1, as_full(grad), low)

        def ticks(first, count):
            @pl.when(encoder & (row == rows - 1))
            def _():
                for j in range(first, first + count):
                    advance(encoder_line, j)

            @pl.when(decoder & (row == 0))
            def _():
                for j in range(first, first + count):
                    advance(decoder_line, DECODER_TICKS + j)

        back_through_out(row)
        ticks(0, 1)
        attend_back(qkv_self, self_probs, row, True)
        ticks(1, PAIRS - 1)

        @pl.when(decoder & (row == rows - 1))
        def _():
            advance(decoder_line, DECODER_TICKS + PAIRS)

        for j in range(width // 256):
            n = slice(j * 256, (j + 1) * 256)
            res[at, n] = dot_outer(qkv_self[at, :], w_att[n, :])
        norm_back(as_full(res), unit_self, row, 0, attn_gain, 0, as_full(grad), None)

    repeat(rows, backward_row)
    write_grad = pltpu.make_async_copy(grad, v.grad_inputs, sem_out.at[1])
    write_grad.start()
    weight_gradient(SELF, 0, mix_self, low, 0)

    def gained_self(b):
        at = pl.ds(at128(b, 128), 128)
        low_t[:, at] = (unit_self(at) * attn_gain).astype(HALF).T

    repeat(tokens // 128, gained_self)
    for item in range(1, 4):
        weight_gradient(SELF, item, low_t, qkv_self, (item - 1) * width)
    for item in range(4):
        add_first(SELF, item)
    by_bucket = lax.dot_general(
        sums[...],
        v.summed[section].astype(FULL),
        (((1,), (1,)), ((), ())),
        precision=PRECISE,
        preferred_element_type=FULL,
    )
    if reduce:
        misc[:, width:] = misc[:, :128]
        by_bucket = jnp.concatenate([by_bucket, jnp.zeros((16, 128 - NBUCKET), FULL)], 1)
        for shard in range(16):
            place = block_place(shard // 4, (shard // 2) % 2, shard % 2)
            turned = pltpu.roll(misc[...], (width + 128 - shard * ways_rows) % (width + 128), 1)
            block = jnp.concatenate([turned[:, :128], by_bucket, jnp.zeros((8, 128), FULL)], 0)
            v.own4[0, place * 32 : (place + 1) * 32, :] = block.astype(HALF)
        begin(SMALL, 0)
        add_first(SMALL, 0)

    def drain(line, done):
        for n in range(done, len(line) + 2):
            advance(line, n)

    @pl.when(encoder)
    def _():
        drain(encoder_line, PAIRS)

    @pl.when(decoder)
    def _():
        drain(decoder_line, DECODER_TICKS + PAIRS + 1)

    if not reduce:
        misc[8:24, :NBUCKET] = by_bucket
        outs = pltpu.make_async_copy(misc, v.out_misc, sem_out.at[2])
        outs.start()
    for name in [GATE_UP, DOWN, SELF] + ([SMALL] if reduce else []):
        repeat(by_name[name].count, functools.partial(finish, name))

    @pl.when(decoder)
    def _():
        repeat(by_name[CROSS].count, functools.partial(finish, CROSS))

    if reduce:

        @pl.when(encoder)
        def _():
            repeat(by_name[CROSS].count, lambda i: cross_over(CROSS, i, i).wait_recv())

        cross_over(SMALL, 0, 1 - section).wait_recv()
    else:
        outs.wait()
    write_grad.wait()

    @pl.when(encoder)
    def _():
        for row in range(rows):
            memory_copy(row).wait_send()
            write_layer(row).wait()

    @pl.when(decoder)
    def _():
        for row in range(rows):
            memory_back(row).wait_send()


def run_layers(args, ways):
    (
        inputs,
        cotangent,
        enc_segments,
        dec_segments,
        rel_bias,
        attn_norm,
        ffn_norm,
        w_qkv,
        w_attn_out,
        w_gate_up,
        w_down,
        cross_norm,
        cross_query,
        cross_kv,
        cross_out,
        final_norm,
    ) = args
    _, rows, length, width = inputs.shape
    hidden = w_down.shape[1]
    tokens = rows * length
    reduce = ways == 16
    spread, summed = bucket_tables(length)
    operands = dict(
        inputs=inputs.reshape(tokens, width),
        cotangent=cotangent.reshape(tokens, width),
        w_qkv=w_qkv,
        w_attn_out=w_attn_out,
        w_gate_up=w_gate_up,
        w_down=w_down,
        cross_query=cross_query,
        cross_kv=cross_kv,
        cross_out=cross_out,
    )
    small = dict(
        enc_segments=enc_segments,
        dec_segments=dec_segments,
        rel_bias=rel_bias,
        attn_norm=attn_norm,
        ffn_norm=ffn_norm,
        mid_norms=jnp.stack([cross_norm, final_norm]),
        spread=jnp.asarray(spread, HALF),
        summed=jnp.asarray(summed, HALF),
    )
    block = width // 16
    groups = [
        Group(GATE_UP, hidden // CHUNK, block, 2 * CHUNK),
        Group(DOWN, 3, hidden // 16, 256),
        Group(CROSS, 4, block, width),
        Group(SELF, 4, block, width),
    ]
    outs = dict(
        layer_out=((tokens, width), HALF),
        grad_inputs=((tokens, width), FULL),
    )
    if reduce:
        groups.append(Group(SMALL, 1, 32, 128))
    for g in groups:
        outs[f"out{g.name}"] = ((g.count, g.rows if reduce else 16 * g.rows, g.cols), HALF)
    if reduce:
        outs[f"out{SMALL}"] = ((2, 32, 128), HALF)
    else:
        outs[MISC] = ((24, width + 128), FULL)
    scratch = dict(
        x_send=pltpu.VMEM((tokens, width), HALF),
        x_recv=pltpu.VMEM((tokens, width), HALF),
        low=pltpu.VMEM((tokens, width), HALF),
        low_t=pltpu.VMEM((width, tokens), HALF),
        unit_ffn=pltpu.VMEM((tokens, width), HALF),
        unit_mid=pltpu.VMEM((tokens, width), HALF),
        cot=pltpu.VMEM((tokens, width), HALF),
        res=pltpu.VMEM((tokens, width), FULL),
        grad=pltpu.VMEM((tokens, width), FULL),
        w_att=pltpu.VMEM((width, 3 * width), HALF),
        w_out=pltpu.VMEM((width, width), HALF),
        qkv_self=pltpu.VMEM((tokens, 3 * width), HALF),
        qkv_cross=pltpu.VMEM((tokens, 3 * width), HALF),
        mix_self=pltpu.VMEM((width, tokens), HALF),
        mix_cross=pltpu.VMEM((width, tokens), HALF),
        probs=pltpu.VMEM((H * rows, length, length), HALF),
        big=pltpu.VMEM((4, width, width), HALF),
        inverse=pltpu.VMEM((tokens, 8), FULL),
        mask=pltpu.VMEM((length, length), HALF),
        near=pltpu.VMEM((length, length), HALF),
        past=pltpu.VMEM((length, length), HALF),
        flip=pltpu.VMEM((length, length), HALF),
        grad_mix=pltpu.VMEM((length, width), HALF),
        segments=pltpu.VMEM((8, length), jnp.int32),
        table=pltpu.VMEM((16, 2 * length), FULL),
        sums=pltpu.VMEM((16, 2 * length), FULL),
        misc=pltpu.VMEM((8 if reduce else 24, width + 128), FULL),
        load=pltpu.SemaphoreType.DMA((5 + 5 * RING,)),
        sem_x=pltpu.SemaphoreType.DMA((4, rows)),
        sem_out=pltpu.SemaphoreType.DMA((4 + rows,)),
    )
    for g in groups:
        if g.name != SELF:
            scratch[f"own{g.name}"] = pltpu.VMEM((g.count, 16 * g.rows, g.cols), HALF)
        if reduce:
            for stage in range(4):
                scratch[f"came{stage}x{g.name}"] = pltpu.VMEM((g.count, (8 >> stage) * g.rows, g.cols), HALF)
        scratch[f"sem{g.name}"] = pltpu.SemaphoreType.DMA((g.count, 11))
    names = list(operands) + list(small) + list(outs) + list(scratch)
    results = pl.pallas_call(
        functools.partial(layer_kernel, names, groups, reduce, rows, length, width, hidden),
        out_shape=[jax.ShapeDtypeStruct(*out) for out in outs.values()],
        in_specs=[pl.BlockSpec(memory_space=pl.ANY)] * len(operands)
        + [pl.BlockSpec(memory_space=pltpu.VMEM)] * len(small),
        out_specs=[pl.BlockSpec(memory_space=pl.ANY)] * len(outs),
        scratch_shapes=list(scratch.values()),
        compiler_params=pltpu.CompilerParams(
            collective_id=1, has_side_effects=True, vmem_limit_bytes=VMEM_LIMIT
        ),
    )(*operands.values(), *small.values())
    return dict(zip(outs, results)), reduce


LAYER, INPUT, MISC = "layer_out", "grad_inputs", "out_misc"
VMEM_LIMIT = 64 * 2**20 - 64 * 2**10


def finish_kernel(width, pair, lower, cross, own, small, layer, grad, *refs):
    layer_out, grad_out, qkv, attn_out, gate_up, down, attn, ffn, query, kv, outer, mid, final, rel = refs[:14]
    layer_held, grad_held, sem = refs[14:]
    through = [(layer, layer_held, layer_out), (grad, grad_held, grad_out)]
    arriving = [pltpu.make_async_copy(a, b, sem.at[n]) for n, (a, b, _) in enumerate(through)]
    leaving = [pltpu.make_async_copy(b, c, sem.at[2 + n]) for n, (_, b, c) in enumerate(through)]
    for copy in arriving:
        copy.start()
    for came, copy in zip(arriving, leaving):
        came.wait()
        copy.start()
    chunks = pair.shape[0]
    for k in range(chunks):
        gate_up[:, k * CHUNK : (k + 1) * CHUNK] = pair[k, :, :CHUNK].astype(FULL)
        up = (chunks + k) * CHUNK
        gate_up[:, up : up + CHUNK] = pair[k, :, CHUNK:].astype(FULL)
    for j in range(3):
        down[:, j * 256 : (j + 1) * 256] = lower[j].astype(FULL)
        qkv[:, j * width : (j + 1) * width] = own[1 + j].astype(FULL)
    attn_out[...] = own[0].astype(FULL)
    outer[...] = cross[0].astype(FULL)
    query[...] = cross[1].astype(FULL)
    for j in range(2):
        kv[:, j * width : (j + 1) * width] = cross[2 + j].astype(FULL)
    block = attn.shape[1]
    mine = small[lax.axis_index("section")].astype(FULL)
    attn[...] = mine[0:1, :block]
    ffn[...] = mine[1:2, :block]
    encoder, decoder = small[0].astype(FULL), small[1].astype(FULL)
    mid[...] = decoder[2:3, :block]
    final[...] = encoder[2:3, :block]
    rel[...] = (encoder[8:24] + decoder[8:24]).T[:NBUCKET, :H]
    for copy in leaving:
        copy.wait()


def finished(out, inputs, hidden):
    tokens, width = out[LAYER].shape
    block = width // 16
    shapes = [(out[LAYER].shape, HALF), (out[INPUT].shape, FULL)] + [
        (shape, FULL)
        for shape in [
            (block, 3 * width),
            (block, width),
            (block, 2 * hidden),
            (hidden // 16, width),
            (1, block),
            (1, block),
            (block, width),
            (block, 2 * width),
            (block, width),
            (1, block),
            (1, block),
            (NBUCKET, H),
        ]
    ]
    layer, grad, qkv, attn_out, gate_up, down, attn, ffn, query, kv, outer, mid, final, rel = pl.pallas_call(
        functools.partial(finish_kernel, width),
        out_shape=[jax.ShapeDtypeStruct(*shape) for shape in shapes],
        in_specs=[pl.BlockSpec(memory_space=pltpu.VMEM)] * 5 + [pl.BlockSpec(memory_space=pl.ANY)] * 2,
        out_specs=[pl.BlockSpec(memory_space=pl.ANY)] * 2 + [pl.BlockSpec(memory_space=pltpu.VMEM)] * 12,
        scratch_shapes=[
            pltpu.VMEM(out[LAYER].shape, HALF),
            pltpu.VMEM(out[INPUT].shape, FULL),
            pltpu.SemaphoreType.DMA((4,)),
        ],
        compiler_params=pltpu.CompilerParams(vmem_limit_bytes=VMEM_LIMIT),
    )(*[out[f"out{name}"] for name in range(5)], out[LAYER], out[INPUT])
    return (
        layer.reshape(inputs.shape),
        grad.reshape(inputs.shape),
        qkv[None],
        attn_out[None],
        gate_up[None],
        down[None],
        attn,
        ffn,
        query,
        kv,
        outer,
        mid.reshape(block),
        final.reshape(block),
        rel,
    )


def shards(*args):
    inputs = args[0]
    ways = lax.axis_size("dp")
    width = inputs.shape[3]
    hidden = args[10].shape[1]
    out, reduce = run_layers(args, ways)
    if reduce:
        return finished(out, inputs, hidden)

    def wide(name):
        value = out[f"out{name}"]
        total = lax.psum_scatter(value, "dp", scatter_dimension=1, tiled=True)
        if name == CROSS:
            total = lax.psum(jnp.where(lax.axis_index("section") == 1, total, 0), "section")
        return total.astype(FULL)

    def side_by_side(value):
        return jnp.swapaxes(value, 0, 1).reshape(value.shape[1], -1)

    gate_up = wide(GATE_UP)
    chunks, block, _ = gate_up.shape
    gate_up = gate_up.reshape(chunks, block, 2, CHUNK).transpose(1, 2, 0, 3).reshape(block, 2 * hidden)
    down, cross, late = wide(DOWN), wide(CROSS), wide(SELF)
    own = lax.psum(out[MISC], "dp")
    misc = lax.all_gather(own, "section", axis=0)
    start = lax.axis_index("dp") * block

    def piece(vector):
        return lax.dynamic_slice_in_dim(vector, start, block, 0)

    return (
        out[LAYER].reshape(inputs.shape),
        out[INPUT].reshape(inputs.shape),
        side_by_side(late[1:])[None],
        late[0][None],
        gate_up[None],
        side_by_side(down)[None],
        piece(own[0, :width])[None],
        piece(own[1, :width])[None],
        cross[1],
        side_by_side(cross[2:]),
        cross[0],
        piece(misc[1, 2, :width]),
        piece(misc[0, 2, :width]),
        (misc[0] + misc[1])[8 : 8 + H, :NBUCKET].T,
    )


def solution(mesh):
    layer = P("section", "dp", None, None)
    matrix = P("section", None, None)
    return jax.shard_map(
        shards,
        mesh=mesh,
        in_specs=(layer, layer, P("dp", None), P("dp", None), P())
        + (P("section", None),) * 2
        + (matrix,) * 4
        + (P(),) * 5,
        out_specs=(layer, layer)
        + (P("section", "dp", None),) * 4
        + (P("section", "dp"),) * 2
        + (P("dp", None),) * 3
        + (P("dp"),) * 2
        + (P(),),
        check_vma=False,
    )
```
